32 devices in a mesh: dp: 4 (over x, core), fsdp: 8 (over z, y).
Axes of the slice: x: 2, y: 2, z: 4, core: 2. Of those that a mesh axis runs over, the one named last changes fastest.
Arguments:
- inputs: bfloat16 [16384, 768], P(('dp', 'fsdp')), may hold values from -6 to 6
- cotangent: bfloat16 [16384, 768], P(('dp', 'fsdp')), may hold values from -6 to 6
- lengths: int32 [128], P(('dp', 'fsdp')), may hold values from 96 to 128, as said below
- tags: int32 [128, 1], P(('dp', 'fsdp')), may hold values from 0 to 1; in each aligned block of 4 rows (0 to 3, 4 to 7, ...) at most 3 rows name the same one
- query_weight: bfloat16 [2, 768, 768], P(None, ('dp', 'fsdp')), may hold values from -0.21875 to 0.21875
- query_bias: bfloat16 [2, 768], P(None, ('dp', 'fsdp')), may hold values from -3 to 3
- key_weight: bfloat16 [2, 768, 768], P(None, ('dp', 'fsdp')), may hold values from -0.21875 to 0.21875
- value_weight: bfloat16 [2, 768, 768], P(None, ('dp', 'fsdp')), may hold values from -0.21875 to 0.21875
- value_bias: bfloat16 [2, 768], P(None, ('dp', 'fsdp')), may hold values from -1.75 to 1.75
- output_projection_weight: bfloat16 [2, 768, 768], P(None, ('dp', 'fsdp')), may hold values from -0.875 to 0.875
- out_bias: bfloat16 [2, 768], P(None, ('dp', 'fsdp')), may hold values from -1.75 to 1.75
- first_gain: bfloat16 [2, 768], P(None, ('dp', 'fsdp')), may hold values from 0.099609375 to 1.8984375
- first_shift: bfloat16 [2, 768], P(None, ('dp', 'fsdp')), may hold values from -1.75 to 1.75
- up_weight: bfloat16 [2, 768, 3072], P(None, ('dp', 'fsdp')), may hold values from -0.21875 to 0.21875
- up_bias: bfloat16 [2, 3072], P(None, ('dp', 'fsdp')), may hold values from -1.75 to 1.75
- down_weight: bfloat16 [2, 3072, 768], P(None, ('dp', 'fsdp')), may hold values from -0.109375 to 0.109375
- down_bias: bfloat16 [2, 768], P(None, ('dp', 'fsdp')), may hold values from -1.75 to 1.75
- second_gain: bfloat16 [2, 768], P(None, ('dp', 'fsdp')), may hold values from 0.099609375 to 1.8984375
- second_shift: bfloat16 [2, 768], P(None, ('dp', 'fsdp')), may hold values from -1.75 to 1.75
Outputs:
- output: bfloat16 [16384, 768], P(('dp', 'fsdp'))
- input_grad: bfloat16 [16384, 768], P(('dp', 'fsdp'))
- grad_query_weight: float32 [2, 768, 768], P(None, ('dp', 'fsdp'))
- grad_query_bias: float32 [2, 768], P(None, ('dp', 'fsdp'))
- grad_key_weight: float32 [2, 768, 768], P(None, ('dp', 'fsdp'))
- grad_value_weight: float32 [2, 768, 768], P(None, ('dp', 'fsdp'))
- grad_value_bias: float32 [2, 768], P(None, ('dp', 'fsdp'))
- grad_out_weight: float32 [2, 768, 768], P(None, ('dp', 'fsdp'))
- grad_out_bias: float32 [2, 768], P(None, ('dp', 'fsdp'))
- grad_first_gain: float32 [2, 768], P(None, ('dp', 'fsdp'))
- grad_first_shift: float32 [2, 768], P(None, ('dp', 'fsdp'))
- grad_up_weight: float32 [2, 768, 3072], P(None, ('dp', 'fsdp'))
- grad_up_bias: float32 [2, 3072], P(None, ('dp', 'fsdp'))
- grad_down_weight: float32 [2, 3072, 768], P(None, ('dp', 'fsdp'))
- grad_down_bias: float32 [2, 768], P(None, ('dp', 'fsdp'))
- grad_second_gain: float32 [2, 768], P(None, ('dp', 'fsdp'))
- grad_second_shift: float32 [2, 768], P(None, ('dp', 'fsdp'))
The draws below stay inside these ranges and needn't reach their ends.
Inputs may be any that keep to these rules, and one draw needn't show every extreme that they name: `lengths`: some chain has exactly 128 live slots and some exactly 96. `tags`: among the 4 chains of one device at most 3 carry either tag, and some device holds exactly 3 of one tag.
All inputs are finite; a program needn't handle non-finite values.
Results may differ from the reference program's by a relative error of at most 0.02.
Values may be sent and summed in bfloat16 or wider, within the bound.
No kernel may reach another device: no remote copies, remote signals or barrier semaphores. Data moves between devices by JAX's collectives and lax.ppermute only.
A program may use at most 192 MiB of HBM per device.

```python
import math
import jax
import jax.numpy as jnp
import numpy as np
from jax import lax

D = 768
HEADS = 12
HEAD_DIM = 64
FF = 3072
LEN = 128
MIN_LEN = 96
CHAINS_PER_UNIT = 4
CAP = 3
CHAINS = 128
TOKENS = 16384


def draw_lengths(key, part):
    key = jax.random.fold_in(key, 7)
    drawn = jax.random.randint(key, (CHAINS,), MIN_LEN, LEN + 1, dtype=jnp.int32)
    return drawn.at[0].set(LEN).at[1].set(MIN_LEN)


def raised(values, own_key, source, target, blocks, factor):
    def block_of(axis_at):
        return (jnp.arange(values.shape[axis_at]) // (values.shape[axis_at] // blocks)).reshape((-1,) + (1,) * (values.ndim - 1 - axis_at))

    one_side = jax.random.permutation(own_key, blocks)[block_of(target)]
    far = (block_of(target) + blocks // 2) % blocks
    return jnp.where((block_of(source) == one_side) | (block_of(source) == far), factor * values, values)


def steps_of(own_key, dims, pieces, smallest, largest):
    loudness, own = 1.0, jax.random.fold_in(own_key, 6)
    for dim, shards_of in pieces:
        heights = jnp.exp(jax.random.uniform(jax.random.fold_in(own, dim), (shards_of,), jnp.float32, smallest / len(pieces), largest / len(pieces)))
        loudness = loudness * jnp.repeat(heights, dims[dim] // shards_of).reshape([-1 if axis == dim else 1 for axis in range(len(dims))])
    return loudness


def assign_block(stream_key, own, number, rows, count, top, most, slope):
    ranking = jax.random.permutation(stream_key, count)
    packed, ordinary = portions_of(count, rows * top, most, slope, True), portions_of(count, rows * top, most, slope, False)
    places = jnp.arange(count)

    def named(sizes, offset_by):
        used = int((sizes > 0).sum())
        fixed = max(1, used // 4)
        passed = fixed + (places - fixed + offset_by * (used - fixed)) % max(1, count - fixed)
        return jnp.zeros((count,), jnp.int32).at[ranking[jnp.where(places < fixed, places, passed)]].set(jnp.asarray(sizes, jnp.int32))

    sizes = jnp.where(number % 4 == 0, named(packed, number // 4), named(ordinary, number - number // 4 - 1))
    mixed = jax.random.permutation(jax.random.fold_in(own, 3), count)
    giver, sink = mixed[0:count // 2 * 2:2], mixed[1:count // 2 * 2:2]
    room = jnp.minimum(sizes[giver] - 1, most - sizes[sink]) // 2
    room = jnp.where((giver == ranking[0]) | (sink == ranking[0]) | (sizes[sink] == 0), 0, jnp.maximum(room, 0))
    passed = jax.random.randint(jax.random.fold_in(own, 4), (count // 2,), 0, 1 << 20) % (room + 1)
    sizes = sizes.at[giver].add(-passed).at[sink].add(passed)
    items = jnp.searchsorted(jnp.cumsum(sizes), jnp.arange(rows * top), side="right").astype(jnp.int32)
    grid = items.reshape(top, rows).T
    grid = grid[jax.random.permutation(jax.random.fold_in(own, 1), rows)]
    offset_by = jax.random.randint(jax.random.fold_in(own, 2), (rows, 1), 0, top)
    return jnp.take_along_axis(grid, (jnp.arange(top)[None, :] + offset_by) % top, axis=1)


def portions_of(amount, total, reach, skew, full):
    portions = [(1 << 20) // math.isqrt(standing ** skew) + 1 for standing in range(1, amount + 1)]
    largest = reach if full else min(reach, max(-(-total // amount), total * portions[0] // sum(portions)))
    least = 1 if total - largest >= amount - 1 else 0
    holding, rest = [largest] + [least] * (amount - 1), total - largest - least * (amount - 1)
    while rest > 0:
        movable = [i for i in range(1, amount) if holding[i] < largest] or [i for i in range(1, amount) if holding[i] < reach]
        whole, remaining = sum([portions[i] for i in movable]), rest
        for i in movable:
            addition = min(reach - holding[i], max(1, remaining * portions[i] // whole), rest)
            holding[i] = holding[i] + addition
            rest = rest - addition
    return np.array(holding)


def centred(stream_key, shape, deviation, reach, shards=(), kind=jnp.bfloat16):
    values = deviation * jax.random.normal(stream_key, shape, jnp.float32)
    if shards:
        values = values * steps_of(stream_key, shape, shards, -0.22, 0.18)
    return jnp.clip(values, -reach, reach).astype(kind)


def bell_draw_with(rng, extent, spread, bound, cuts, heavy, held_as=jnp.bfloat16):
    values = spread * jax.random.normal(rng, extent, jnp.float32)
    if cuts:
        values = values * steps_of(rng, extent, cuts, -0.22, 0.18)
    return jnp.clip(raised(values, jax.random.fold_in(rng, 3), *heavy), -bound, bound).astype(held_as)


def setup_inputs(seed: int = 0) -> dict:
    key_list = jax.random.split(jax.random.key(seed), 20)
    inputs = bell_draw_with(key_list[0], (TOKENS, D), 1.0, 6.0, ((0, 32),), (0, 1, 32, 2.75))
    cotangent = centred(key_list[1], (TOKENS, D), 1.0, 6.0, ((0, 32),))
    lengths = draw_lengths(jax.random.fold_in(key_list[19], 71), 0)
    tags_keys = jax.random.split(jax.random.fold_in(key_list[3], 1), CHAINS // CHAINS_PER_UNIT)
    tags_turns = jax.random.permutation(jax.random.fold_in(key_list[3], 3), CHAINS // CHAINS_PER_UNIT)
    tags = jax.vmap(lambda own, number: assign_block(jax.random.fold_in(key_list[3], 2), own, number, CHAINS_PER_UNIT, 2, 1, CAP, 0))(tags_keys, tags_turns).reshape((CHAINS, 1))
    query_weight = centred(key_list[4], (2, D, D), D ** -0.5, 0.21875, ((1, 32),))
    query_bias = centred(key_list[5], (2, D), 0.5, 3.0, ((1, 32),))
    key_weight = centred(key_list[6], (2, D, D), D ** -0.5, 0.21875, ((1, 32),))
    value_weight = centred(key_list[7], (2, D, D), D ** -0.5, 0.21875, ((1, 32),))
    value_bias = centred(key_list[8], (2, D), 0.3, 1.75, ((1, 32),))
    output_projection_weight = centred(key_list[9], (2, D, D), (D // 16) ** -0.5, 0.875, ((1, 32),))
    out_bias = centred(key_list[10], (2, D), 0.3, 1.75, ((1, 32),))
    first_gain = jnp.clip(1.0 + 0.18 * jax.random.normal(key_list[11], (2, D), jnp.float32), 0.099609375, 1.8984375).astype(jnp.bfloat16)
    first_shift = centred(key_list[12], (2, D), 0.3, 1.75, ((1, 32),))
    up_weight = centred(key_list[13], (2, D, FF), D ** -0.5, 0.21875, ((1, 32),))
    up_bias = centred(key_list[14], (2, FF), 0.3, 1.75, ((1, 32),))
    down_weight = centred(key_list[15], (2, FF, D), FF ** -0.5, 0.109375, ((1, 32),))
    down_bias = centred(key_list[16], (2, D), 0.3, 1.75, ((1, 32),))
    second_gain = jnp.clip(1.0 + 0.18 * jax.random.normal(key_list[17], (2, D), jnp.float32), 0.099609375, 1.8984375).astype(jnp.bfloat16)
    second_shift = centred(key_list[18], (2, D), 0.3, 1.75, ((1, 32),))
    return {"inputs": inputs, "cotangent": cotangent, "lengths": lengths, "tags": tags, "query_weight": query_weight, "query_bias": query_bias, "key_weight": key_weight, "value_weight": value_weight, "value_bias": value_bias, "output_projection_weight": output_projection_weight, "out_bias": out_bias, "first_gain": first_gain, "first_shift": first_shift, "up_weight": up_weight, "up_bias": up_bias, "down_weight": down_weight, "down_bias": down_bias, "second_gain": second_gain, "second_shift": second_shift}


@jax.custom_vjp
def low(v):
    return lax.optimization_barrier(v.astype(jnp.bfloat16)).astype(jnp.float32)

@jax.custom_vjp
def low_back(v):
    return v

def low_keep(v):
    return (low(v), None)

def low_pass(kept, grad):
    return (grad,)

def back_keep(v):
    return (v, None)

def back_low(kept, grad):
    return (low(grad),)
low.defvjp(low_keep, low_pass)
low_back.defvjp(back_keep, back_low)

def layer_norm(values, norm_gain, norm_shift):
    centre = values - lax.optimization_barrier(jnp.mean(values, axis=-1, keepdims=True))
    return centre * lax.rsqrt(lax.optimization_barrier(jnp.mean(centre * centre, axis=-1, keepdims=True)) + 1e-05) * norm_gain + norm_shift

def product(left_side, right_side):
    return jnp.einsum('gld,de->gle', left_side, right_side, precision=lax.Precision.HIGHEST)

def one_model(chain_token_rows, chain_len, params):
    query_weight, query_bias, key_weight, value_weight, value_bias, output_projection_weight, out_bias, first_gain, first_shift, up_weight, up_bias, down_weight, down_bias, second_gain, second_shift = params
    group, slot_length, model_width = chain_token_rows.shape
    head_shape = (group, slot_length, HEADS, HEAD_DIM)
    queries = low(low_back(product(chain_token_rows, query_weight) + query_bias)).reshape(head_shape)
    key_rows = low(low_back(product(chain_token_rows, key_weight))).reshape(head_shape)
    value_rows = low(low_back(product(chain_token_rows, value_weight) + value_bias)).reshape(head_shape)
    raw_scores = jnp.einsum('gqhe,gkhe->ghqk', queries, key_rows, precision=lax.Precision.HIGHEST)
    scores = low_back(raw_scores * HEAD_DIM ** (-0.5))
    positions = jnp.arange(slot_length, dtype=jnp.int32)
    scores = jnp.where(positions[None, None, None, :] < chain_len[:, None, None, None], scores, -1000000000.0)
    row_top = lax.optimization_barrier(jnp.max(scores, axis=-1, keepdims=True))
    exponent = jnp.exp(scores - row_top)
    probabilities = low(exponent / lax.optimization_barrier(jnp.sum(exponent, axis=-1, keepdims=True)))
    context = jnp.einsum('ghqk,gkhe->gqhe', probabilities, value_rows, precision=lax.Precision.HIGHEST)
    context = low(low_back(context.reshape(group, slot_length, model_width)))
    branch = low_back(product(context, output_projection_weight) + out_bias)
    normed_first = layer_norm(chain_token_rows + branch, first_gain, first_shift)
    hidden = low_back(product(low(normed_first), up_weight) + up_bias)
    active = low(jax.nn.gelu(hidden, approximate=False))
    second_branch = low_back(product(active, down_weight) + down_bias)
    return layer_norm(normed_first + second_branch, second_gain, second_shift)

def group_forward(chain_token_rows, chain_len, chain_tag, heavy_params, light_params):
    heavy_out = one_model(chain_token_rows, chain_len, heavy_params)
    light_out = one_model(chain_token_rows, chain_len, light_params)
    return jnp.where(chain_tag[:, None, None] == 0, heavy_out, light_out)

def reference(inputs, cotangent, lengths, tags, query_weight, query_bias, key_weight, value_weight, value_bias, output_projection_weight, out_bias, first_gain, first_shift, up_weight, up_bias, down_weight, down_bias, second_gain, second_shift):
    params = tuple((tensor.astype(jnp.float32) for tensor in (query_weight, query_bias, key_weight, value_weight, value_bias, output_projection_weight, out_bias, first_gain, first_shift, up_weight, up_bias, down_weight, down_bias, second_gain, second_shift)))
    heavy_params = tuple((tensor[0] for tensor in params))
    light_params = tuple((tensor[1] for tensor in params))
    group = math.gcd(CHAINS, max(1, 4096 // LEN))
    count = CHAINS // group
    blocks = inputs.astype(jnp.float32).reshape(count, group, LEN, D)
    grad_blocks = cotangent.astype(jnp.float32).reshape(count, group, LEN, D)
    chain_lens = lengths.reshape(count, group)
    chain_tags = tags[:, 0].reshape(count, group)

    def step(summed, scan_item):
        chain_token_rows, grad_rows, chain_len, chain_tag = scan_item

        def local_forward(rows_in, heavy_in, light_in):
            return group_forward(rows_in, chain_len, chain_tag, heavy_in, light_in)
        result, pull_back = jax.vjp(local_forward, chain_token_rows, heavy_params, light_params)
        grad_rows_in, grad_heavy, grad_light = pull_back(grad_rows)
        summed = jax.tree.map(lambda total, heavy_part, light_part: total + jnp.stack([heavy_part, light_part]), summed, grad_heavy, grad_light)
        return (summed, (result.astype(jnp.bfloat16), grad_rows_in.astype(jnp.bfloat16)))
    zeros = tuple((jnp.zeros_like(tensor) for tensor in params))
    summed, (results, grad_inputs) = lax.scan(step, zeros, (blocks, grad_blocks, chain_lens, chain_tags))
    return (results.reshape(TOKENS, D), grad_inputs.reshape(TOKENS, D), summed[0], summed[1], summed[2], summed[3], summed[4], summed[5], summed[6], summed[7], summed[8], summed[9], summed[10], summed[11], summed[12], summed[13], summed[14])
```

```python
import functools

import jax
import jax.numpy as jnp
import numpy as np
from jax import lax
from jax.experimental import pallas as pl
from jax.experimental.pallas import tpu as pltpu
from jax.sharding import Mesh
from jax.sharding import PartitionSpec as P

HEADS = 12
HEAD_DIM = 64
CAP = 3
LANES = 128
BF16 = jnp.bfloat16
F32 = jnp.float32
NN = (((1,), (0,)), ((), ()))
NT = (((1,), (1,)), ((), ()))
TN = (((0,), (0,)), ((), ()))
SWAP = [(0, 1), (1, 0)]


def dot(a, b, dims=NN):
    return lax.dot_general(a, b, dims, preferred_element_type=F32)


def head_masks():
    lane = lax.broadcasted_iota(jnp.int32, (1, LANES), 1)
    first = (lane < HEAD_DIM).astype(F32).astype(BF16)
    second = (lane >= HEAD_DIM).astype(F32).astype(BF16)
    return first, second


def stacked(two_heads, masks):
    return jnp.concatenate([two_heads * masks[0], two_heads * masks[1]], axis=0)


def side_by_side(rows):
    half = rows.shape[0] // 2
    return jnp.concatenate([rows[:half], rows[half:]], axis=1)


def pair_probs(k_stack, q_pair, length):
    scores = dot(k_stack, q_pair, NT) * HEAD_DIM**-0.5
    keys = k_stack.shape[0] // 2
    scores = scores.reshape(2, keys, scores.shape[1])
    slot = lax.broadcasted_iota(jnp.int32, scores.shape, 1)
    scores = jnp.where(slot < length, scores, -1000000000.0)
    exponent = jnp.exp(scores - jnp.max(scores, axis=1, keepdims=True))
    probs = exponent / jnp.sum(exponent, axis=1, keepdims=True)
    return probs


def attention_kernel(lens_ref, qkv_ref, ctx_ref):
    width = ctx_ref.shape[1]
    length = lens_ref[pl.program_id(0)]
    masks = head_masks()
    for start in range(0, width, LANES):
        q_pair = qkv_ref[:, start : start + LANES]
        k_stack = stacked(qkv_ref[:, width + start : width + start + LANES], masks)
        v_stack = stacked(qkv_ref[:, 2 * width + start : 2 * width + start + LANES], masks)
        probs = pair_probs(k_stack, q_pair, length)
        low = probs.astype(BF16).reshape(k_stack.shape[0], q_pair.shape[0])
        ctx_ref[:, start : start + LANES] = dot(low, v_stack, TN).astype(BF16)


def attention_back_kernel(lens_ref, qkv_ref, dctx_ref, dqkv_ref):
    width = dctx_ref.shape[1]
    length = lens_ref[pl.program_id(0)]
    masks = head_masks()
    scale = HEAD_DIM**-0.5
    for start in range(0, width, LANES):
        q_pair = qkv_ref[:, start : start + LANES]
        k_stack = stacked(qkv_ref[:, width + start : width + start + LANES], masks)
        v_stack = stacked(qkv_ref[:, 2 * width + start : 2 * width + start + LANES], masks)
        d_pair = dctx_ref[:, start : start + LANES]
        probs = pair_probs(k_stack, q_pair, length)
        low = probs.astype(BF16).reshape(k_stack.shape[0], q_pair.shape[0])
        dv = dot(side_by_side(low), stacked(d_pair, masks))
        dprobs = dot(v_stack, d_pair, NT).reshape(probs.shape)
        inner = jnp.sum(dprobs * probs, axis=1, keepdims=True)
        dscores = (probs * (dprobs - inner)).astype(BF16).reshape(low.shape)
        dq = scale * dot(dscores, k_stack, TN)
        dk = scale * dot(side_by_side(dscores), stacked(q_pair, masks))
        dqkv_ref[:, start : start + LANES] = dq.astype(BF16)
        dqkv_ref[:, width + start : width + start + LANES] = dk.astype(BF16)
        dqkv_ref[:, 2 * width + start : 2 * width + start + LANES] = dv.astype(BF16)


def attention(qkv, lens, width):
    chains = lens.shape[0]
    rows = qkv.shape[0] // chains
    return pl.pallas_call(
        attention_kernel,
        out_shape=jax.ShapeDtypeStruct((qkv.shape[0], width), BF16),
        grid_spec=pltpu.PrefetchScalarGridSpec(
            num_scalar_prefetch=1,
            grid=(chains,),
            in_specs=[pl.BlockSpec((rows, 3 * width), lambda i, _: (i, 0))],
            out_specs=pl.BlockSpec((rows, width), lambda i, _: (i, 0)),
        ),
        cost_estimate=pl.CostEstimate(
            flops=8 * qkv.shape[0] * rows * width,
            bytes_accessed=8 * qkv.shape[0] * width,
            transcendentals=qkv.shape[0] * rows * HEADS,
        ),
        name="attention_forward",
    )(lens, qkv)


def attention_back(qkv, dctx, lens):
    chains = lens.shape[0]
    width = dctx.shape[1]
    rows = qkv.shape[0] // chains
    return pl.pallas_call(
        attention_back_kernel,
        out_shape=jax.ShapeDtypeStruct(qkv.shape, BF16),
        grid_spec=pltpu.PrefetchScalarGridSpec(
            num_scalar_prefetch=1,
            grid=(chains,),
            in_specs=[
                pl.BlockSpec((rows, 3 * width), lambda i, _: (i, 0)),
                pl.BlockSpec((rows, width), lambda i, _: (i, 0)),
            ],
            out_specs=pl.BlockSpec((rows, 3 * width), lambda i, _: (i, 0)),
        ),
        cost_estimate=pl.CostEstimate(
            flops=20 * qkv.shape[0] * rows * width,
            bytes_accessed=14 * qkv.shape[0] * width,
            transcendentals=qkv.shape[0] * rows * HEADS,
        ),
        name="attention_backward",
    )(lens, qkv, dctx)


def up_kernel(low_ref, up_ref, bias_ref, active_ref, slope_ref):
    hidden = dot(low_ref[...], up_ref[...]) + bias_ref[...]
    cdf = 0.5 * (1.0 + lax.erf(hidden * (2.0**-0.5)))
    active_ref[...] = (hidden * cdf).astype(BF16)
    density = jnp.exp(-0.5 * hidden * hidden) * ((2.0 * np.pi) ** -0.5)
    slope_ref[...] = (cdf + hidden * density).astype(BF16)


def up_and_gelu(low, up_weight, up_bias):
    rows, width = low.shape
    ff = up_bias.shape[1]
    block = 512
    return pl.pallas_call(
        up_kernel,
        out_shape=[jax.ShapeDtypeStruct((rows, ff), BF16)] * 2,
        grid=(ff // block,),
        in_specs=[
            pl.BlockSpec((rows, width), lambda i: (0, 0)),
            pl.BlockSpec((width, block), lambda i: (0, i)),
            pl.BlockSpec((1, block), lambda i: (0, i)),
        ],
        out_specs=[pl.BlockSpec((rows, block), lambda i: (0, i))] * 2,
        cost_estimate=pl.CostEstimate(
            flops=2 * rows * width * ff,
            bytes_accessed=2 * (rows * width + width * ff + 2 * rows * ff),
            transcendentals=2 * rows * ff,
        ),
        compiler_params=pltpu.CompilerParams(vmem_limit_bytes=40 * 2**20),
        name="up_gelu",
    )(low, up_weight, up_bias)


def normed(values):
    centre = values - jnp.mean(values, axis=-1, keepdims=True)
    root = lax.rsqrt(jnp.mean(centre * centre, axis=-1, keepdims=True) + 1e-05)
    return centre * root, root


def norm_back(grad, unit, root, gain):
    scaled = grad * gain
    inner = jnp.mean(scaled * unit, axis=-1, keepdims=True)
    grad_in = root * (scaled - jnp.mean(scaled, axis=-1, keepdims=True) - unit * inner)
    return grad_in, jnp.sum(grad * unit, axis=0), jnp.sum(grad, axis=0)


class Ring:
    def __init__(self, count):
        depth = 4 if count % 4 == 0 else 2
        wide = count // depth
        order = []
        if wide > 1:
            for z in range(depth):
                ys = range(1, wide) if z % 2 == 0 else reversed(range(1, wide))
                order += [z * wide + y for y in ys]
            order += [z * wide for z in reversed(range(depth))]
        else:
            order = list(range(count))
        self.count = count
        self.pairs = []
        origin = np.zeros((2, count, count), np.int32)
        for core in range(2):
            sign = 1 if core == 0 else -1
            for place, chip in enumerate(order):
                self.pairs.append((core * count + chip, core * count + order[(place + sign) % count]))
                for step in range(count):
                    origin[core, chip, step] = order[(place - sign * step) % count]
        self.origin = origin

    def sources(self):
        table = jnp.asarray(self.origin.reshape(-1))
        at = (lax.axis_index("core") * self.count + lax.axis_index("f")) * self.count
        return [lax.dynamic_index_in_dim(table, at + k, 0, keepdims=False) for k in range(self.count)]

    def pass_on(self, block):
        return lax.ppermute(block, ("core", "f"), self.pairs)


def swap(value, axis):
    return lax.ppermute(value, axis, SWAP)


def pick(value, index, axis):
    return lax.dynamic_index_in_dim(value, index, axis, keepdims=False)


def two_sides(shards, side, groups):
    own = pick(shards, side, 0)
    other = swap(pick(shards, 1 - side, 0), "t")
    place = lax.broadcasted_iota(jnp.int32, (2, 1, 1), 0)
    block = jnp.where(place == side, own[None], other[None])
    if groups > 1:
        return lax.all_gather(block, "r", axis=0, tiled=False)
    return block[None]


def both_cores(own, other, core):
    place = lax.broadcasted_iota(jnp.int32, (1, 1, 2) + (1,) * (own.ndim - 2), 2)
    whole = jnp.where(place == core, own[:, :, None], other[:, :, None])
    return whole.reshape(-1, own.shape[-1])


def ring_gather(blocks, ring, sources):
    held = []
    for block in blocks:
        start = jnp.zeros(block.shape[:2] + (ring.count,) + block.shape[2:], block.dtype)
        held.append(lax.dynamic_update_index_in_dim(start, block, sources[0], 2))
    for step in range(1, ring.count):
        blocks = [ring.pass_on(block) for block in blocks]
        held = [
            lax.dynamic_update_index_in_dim(h, block, sources[step], 2)
            for h, block in zip(held, blocks)
        ]
    return held


def half_sums(grad, groups, ring, core):
    split = grad.reshape(groups, 2, 2, ring.count, -1, grad.shape[-1])
    own = pick(split, core, 2)
    other = swap(pick(split, 1 - core, 2), "core")
    return own, other


def ring_scatter(halves, ring, sources):
    own, other = halves

    def term(step):
        return pick(own, sources[step], 2).astype(F32) + pick(other, sources[step], 2).astype(F32)

    total = term(1)
    for step in range(2, ring.count + 1):
        arrived = ring.pass_on(total.astype(BF16))
        total = arrived.astype(F32) + term(step % ring.count)
    return total


def to_owners(total, side, groups):
    if groups > 1:
        total = lax.psum_scatter(total.astype(BF16), "r", scatter_dimension=0, tiled=True)
    total = total[0]
    own = pick(total, side, 0).astype(F32)
    other = swap(pick(total, 1 - side, 0).astype(BF16), "t").astype(F32)
    place = lax.broadcasted_iota(jnp.int32, (2, 1, 1), 0)
    return jnp.where(place == side, own[None], other[None])


def places(tags, model):
    member = (tags[:, 0] == model).astype(jnp.int32)
    ranking = jnp.cumsum(member) - 1
    slots = lax.broadcasted_iota(jnp.int32, (CAP, member.shape[0]), 0)
    return (slots == ranking[None, :]) & (member[None, :] == 1)


def take(chains, index):
    return jnp.stack([pick(chains, index[s], 0) for s in range(CAP)])


def columns(vectors, extra, rows):
    parts = [v[..., None] for v in vectors]
    if extra is not None:
        parts.append(extra.reshape(extra.shape[:-1] + (rows, -1)))
    block = jnp.concatenate(parts, axis=-1)
    pad = [(0, 0)] * (block.ndim - 1) + [(0, LANES - block.shape[-1])]
    return jnp.pad(block, pad)


def body(ring, groups, *args):
    (
        inputs,
        cotangent,
        lengths,
        tags,
        query_weight,
        query_bias,
        key_weight,
        value_weight,
        value_bias,
        output_projection_weight,
        out_bias,
        first_gain,
        first_shift,
        up_weight,
        up_bias,
        down_weight,
        down_bias,
        second_gain,
        second_shift,
    ) = args
    side, core = lax.axis_index("t"), lax.axis_index("core")
    sources = ring.sources()
    chains = lengths.shape[0]
    width = inputs.shape[1]
    ff = up_weight.shape[2]
    slots = inputs.shape[0] // chains
    shard = query_weight.shape[1]

    attention_shard = jnp.concatenate(
        [
            query_weight,
            key_weight,
            value_weight,
            output_projection_weight,
            columns([query_bias, value_bias, out_bias, first_gain, first_shift], None, shard),
        ],
        axis=-1,
    )
    up_shard = jnp.concatenate(
        [up_weight, columns([down_bias, second_gain, second_shift], up_bias, shard)], axis=-1
    )
    block_a = two_sides(attention_shard, side, groups)
    block_u = two_sides(up_shard, side, groups)
    block_d = two_sides(down_weight, side, groups)

    own_places, other_places = places(tags, side), places(tags, 1 - side)
    order = jnp.arange(chains, dtype=jnp.int32)[None, :]
    own_index = jnp.sum(jnp.where(own_places, order, 0), axis=1)
    other_index = jnp.sum(jnp.where(other_places, order, 0), axis=1)
    own_live, other_live = jnp.any(own_places, axis=1), jnp.any(other_places, axis=1)
    own_len = jnp.sum(jnp.where(own_places, lengths[None, :], 0), axis=1)
    other_len = jnp.sum(jnp.where(other_places, lengths[None, :], 0), axis=1)
    chain_rows = inputs.reshape(chains, slots, width)
    cot_rows = cotangent.reshape(chains, slots, width)
    sent = jnp.concatenate(
        [
            take(chain_rows, other_index).reshape(CAP * slots, width),
            jnp.broadcast_to(jnp.repeat(other_len, 16)[:, None], (CAP * 16, width)).astype(BF16),
        ],
        axis=0,
    )
    arrived = swap(sent, "t")
    rows_in = jnp.concatenate(
        [take(chain_rows, own_index).reshape(CAP * slots, width), arrived[: CAP * slots]], axis=0
    )
    lens = jnp.concatenate(
        [own_len, arrived[CAP * slots :: 16, 0].astype(jnp.int32)]
    )
    own_cot = jnp.where(own_live[:, None, None], take(cot_rows, own_index), 0)
    other_cot = swap(jnp.where(other_live[:, None, None], take(cot_rows, other_index), 0), "t")
    cot = jnp.concatenate([own_cot, other_cot], axis=0).reshape(2 * CAP * slots, width).astype(F32)

    gathered_d = lax.all_gather(
        block_d.reshape(groups * 2, -1, width), "f", axis=1, tiled=True
    ).reshape(groups, 2, -1, width)
    held_a, held_u = ring_gather([block_a, block_u], ring, sources)
    whole_a = both_cores(held_a, swap(held_a, "core"), core)
    whole_u = both_cores(held_u, swap(held_u, "core"), core)
    whole_d = both_cores(gathered_d, swap(gathered_d, "core"), core)

    qkv_weight = whole_a[:, : 3 * width]
    out_weight = whole_a[:, 3 * width : 4 * width]
    small_a = whole_a[:, 4 * width :].astype(F32).T
    small_u = whole_u[:, ff:].astype(F32)
    up_bias_row = small_u[:, 3 : 3 + ff // width].reshape(1, ff)
    small_u = small_u.T
    b_query, b_value, b_out, gain1, shift1 = [small_a[i : i + 1] for i in range(5)]
    b_down, gain2, shift2 = [small_u[i : i + 1] for i in range(3)]

    qkv_bias = jnp.concatenate([b_query, jnp.zeros_like(b_query), b_value], axis=1)
    qkv = (dot(rows_in, qkv_weight) + qkv_bias).astype(BF16)
    context = attention(qkv, lens, width)
    unit1, root1 = normed(rows_in.astype(F32) + dot(context, out_weight) + b_out)
    hidden1 = unit1 * gain1 + shift1
    low1 = hidden1.astype(BF16)
    active, slope = up_and_gelu(low1, whole_u, up_bias_row)
    unit2, root2 = normed(hidden1 + dot(active, whole_d) + b_down)
    result = (unit2 * gain2 + shift2).astype(BF16)

    dr2, g_gain2, g_shift2 = norm_back(cot, unit2, root2, gain2)
    df = dr2.astype(BF16)
    g_down_bias = jnp.sum(df.astype(F32), axis=0)
    g_down = dot(active, df, TN).astype(BF16)
    own_d, other_d = half_sums(g_down, groups, ring, core)
    half_d = (own_d.astype(F32) + other_d.astype(F32)).astype(BF16)
    half_d = jnp.moveaxis(half_d, 2, 0)
    total_d = lax.psum_scatter(
        half_d.reshape(-1, width), "f", scatter_dimension=0, tiled=True
    ).reshape(groups, 2, -1, width)

    du = (dot(df, whole_d, NT) * slope.astype(F32)).astype(BF16)
    g_up_bias = jnp.sum(du.astype(F32), axis=0)
    g_up = jnp.concatenate(
        [
            dot(low1, du, TN).astype(BF16),
            columns([g_down_bias, g_gain2, g_shift2], g_up_bias, width).astype(BF16),
        ],
        axis=1,
    )
    total_u = ring_scatter(half_sums(g_up, groups, ring, core), ring, sources)
    dh1 = dr2 + dot(du, whole_u[:, :ff], NT)
    dr1, g_gain1, g_shift1 = norm_back(dh1, unit1, root1, gain1)
    da = dr1.astype(BF16)
    g_out_bias = jnp.sum(da.astype(F32), axis=0)
    g_out = dot(context, da, TN)
    dctx = dot(da, out_weight, NT).astype(BF16)
    dqkv = attention_back(qkv, dctx, lens)
    g_qkv_bias = jnp.sum(dqkv.astype(F32), axis=0)
    g_attention = jnp.concatenate(
        [
            dot(rows_in, dqkv, TN).astype(BF16),
            g_out.astype(BF16),
            columns(
                [g_qkv_bias[:width], g_qkv_bias[2 * width :], g_out_bias, g_gain1, g_shift1],
                None,
                width,
            ).astype(BF16),
        ],
        axis=1,
    )
    total_a = ring_scatter(half_sums(g_attention, groups, ring, core), ring, sources)
    rows_grad = (dr1 + dot(dqkv, qkv_weight, NT)).astype(BF16)

    grads_d = to_owners(total_d, side, groups)
    grads_u = to_owners(total_u, side, groups)
    grads_a = to_owners(total_a, side, groups)

    own_rank = jnp.sum(jnp.where(own_places, order_of(CAP), 0), axis=0)
    other_rank = jnp.sum(jnp.where(other_places, order_of(CAP), 0), axis=0)

    def home(values):
        values = values.reshape(2, CAP, slots, width)
        back = swap(values[1], "t")
        out = [
            jnp.where(
                tags[i, 0] == side, pick(values[0], own_rank[i], 0), pick(back, other_rank[i], 0)
            )
            for i in range(chains)
        ]
        return jnp.concatenate(out, axis=0)

    small_a = grads_a[:, :, 4 * width :]
    small_u = grads_u[:, :, ff:]
    return (
        home(result),
        home(rows_grad),
        grads_a[:, :, :width],
        small_a[:, :, 0],
        grads_a[:, :, width : 2 * width],
        grads_a[:, :, 2 * width : 3 * width],
        small_a[:, :, 1],
        grads_a[:, :, 3 * width : 4 * width],
        small_a[:, :, 2],
        small_a[:, :, 3],
        small_a[:, :, 4],
        grads_u[:, :, :ff],
        small_u[:, :, 3 : 3 + ff // width].reshape(2, -1),
        grads_d,
        small_u[:, :, 0],
        small_u[:, :, 1],
        small_u[:, :, 2],
    )


def order_of(count):
    return jnp.arange(count, dtype=jnp.int32)[:, None]


def solution(mesh):
    dp, fsdp = mesh.shape["dp"], mesh.shape["fsdp"]
    groups = dp // 4
    inner = Mesh(mesh.devices.reshape(groups, 2, 2, fsdp), ("r", "t", "core", "f"))
    every = ("r", "t", "core", "f")
    rows, vector, matrix = P(every, None), P(None, every), P(None, every, None)
    weights = (
        matrix,
        vector,
        matrix,
        matrix,
        vector,
        matrix,
        vector,
        vector,
        vector,
        matrix,
        vector,
        matrix,
        vector,
        vector,
        vector,
    )
    return jax.shard_map(
        functools.partial(body, Ring(fsdp), groups),
        mesh=inner,
        in_specs=(rows, rows, P(every), rows) + weights,
        out_specs=(rows, rows) + weights,
        check_vma=False,
    )
```

```python
import functools

import jax
import jax.numpy as jnp
import numpy as np
from jax import lax
from jax.experimental import pallas as pl
from jax.experimental.pallas import tpu as pltpu
from jax.sharding import Mesh
from jax.sharding import PartitionSpec as P

HEADS = 12
HEAD_DIM = 64
CAP = 3
MIN_LEN = 96
LANES = 128
BF16 = jnp.bfloat16
F32 = jnp.float32
NN = (((1,), (0,)), ((), ()))
NT = (((1,), (1,)), ((), ()))
TN = (((0,), (0,)), ((), ()))
SWAP = [(0, 1), (1, 0)]
VMEM_LIMIT = 56 * 2**20
SMALL = 12


def dot(a, b, dims=NN):
    return lax.dot_general(a, b, dims, preferred_element_type=F32)


def tie(*values):
    return lax.optimization_barrier(values)


def params():
    return pltpu.CompilerParams(vmem_limit_bytes=VMEM_LIMIT)


def cost(flops, moved, exps=0):
    return pl.CostEstimate(flops=flops, bytes_accessed=moved, transcendentals=exps)


def whole_spec(shape):
    return pl.BlockSpec(shape, lambda *_: (0,) * len(shape))


def head_masks(value=1.0):
    lane = lax.broadcasted_iota(jnp.int32, (1, LANES), 1)
    first = jnp.where(lane < HEAD_DIM, value, 0.0).astype(BF16)
    second = jnp.where(lane >= HEAD_DIM, value, 0.0).astype(BF16)
    return first, second


def stacked(two_heads, masks):
    return jnp.concatenate([two_heads * masks[0], two_heads * masks[1]], axis=0)


def side_by_side(rows):
    half = rows.shape[0] // 2
    return jnp.concatenate([rows[:half], rows[half:]], axis=1)


def pair_probs(k_stack, q_pair, length):
    scores = dot(k_stack, q_pair, NT)
    keys = k_stack.shape[0] // 2
    scores = scores.reshape(2, keys, scores.shape[1])
    always = scores[:, :MIN_LEN]
    rest = scores[:, MIN_LEN:]
    slot = lax.broadcasted_iota(jnp.int32, rest.shape, 1) + MIN_LEN
    rest = jnp.where(slot < length, rest, -1000000000.0)
    scores = jnp.concatenate([always, rest], axis=1)
    exponent = jnp.exp(scores - jnp.max(scores, axis=1, keepdims=True))
    return exponent * (1.0 / jnp.sum(exponent, axis=1, keepdims=True))


def attention_rows(length, qkv_ref, ctx_ref, base, rows, width):
    masks, scaled = head_masks(), head_masks(HEAD_DIM**-0.5)
    at = slice(base, base + rows)
    for start in range(0, width, LANES):
        q_pair = qkv_ref[at, start : start + LANES]
        k_stack = stacked(qkv_ref[at, width + start : width + start + LANES], scaled)
        v_stack = stacked(qkv_ref[at, 2 * width + start : 2 * width + start + LANES], masks)
        probs = pair_probs(k_stack, q_pair, length)
        low = probs.astype(BF16).reshape(k_stack.shape[0], q_pair.shape[0])
        ctx_ref[at, start : start + LANES] = dot(low, v_stack, TN).astype(BF16)


def attention_kernel(
    lens_ref, rows_ref, weight_ref, vec_ref, qkv_ref, ctx_ref, unit_ref, root_ref, low_ref
):
    width = ctx_ref.shape[1]
    rows = qkv_ref.shape[0] // 2
    for part in range(3):
        columns = slice(part * width, (part + 1) * width)
        product = dot(rows_ref[...], weight_ref[:, columns])
        if part != 1:
            product = product + vec_ref[part // 2 : part // 2 + 1, :]
        qkv_ref[:, columns] = product.astype(BF16)
    for chain in range(2):
        length = lens_ref[2 * pl.program_id(0) + chain]
        attention_rows(length, qkv_ref, ctx_ref, chain * rows, rows, width)
    branch = dot(ctx_ref[...], weight_ref[:, 3 * width : 4 * width]) + vec_ref[2:3, :]
    unit, root = normed(rows_ref[...].astype(F32) + branch)
    unit_ref[...] = unit
    root_ref[...] = root
    low_ref[...] = (unit * vec_ref[3:4, :] + vec_ref[4:5, :]).astype(BF16)


def attention(rows_in, lens, whole_a, vectors):
    total, width = rows_in.shape
    rows = 2 * total // lens.shape[0]

    def tokens(lanes):
        return pl.BlockSpec((rows, lanes), lambda i, _: (i, 0))

    return pl.pallas_call(
        attention_kernel,
        out_shape=[
            jax.ShapeDtypeStruct((total, 3 * width), BF16),
            jax.ShapeDtypeStruct((total, width), BF16),
            jax.ShapeDtypeStruct((total, width), F32),
            jax.ShapeDtypeStruct((total, 1), F32),
            jax.ShapeDtypeStruct((total, width), BF16),
        ],
        grid_spec=pltpu.PrefetchScalarGridSpec(
            num_scalar_prefetch=1,
            grid=(total // rows,),
            in_specs=[tokens(width), whole_spec(whole_a.shape), whole_spec(vectors.shape)],
            out_specs=[tokens(3 * width), tokens(width), tokens(width), tokens(1), tokens(width)],
        ),
        compiler_params=params(),
        cost_estimate=cost(8 * total * width * (width + rows), 20 * total * width),
        name="attention_forward",
    )(lens, rows_in, whole_a, vectors)


def attention_back_kernel(lens_ref, *refs):
    qkv_ref, da_ref, out_weight_ref = refs[:3]
    dqkv_ref, sum_ref = refs[-2:]
    width = da_ref.shape[1]
    length = lens_ref[pl.program_id(0)]
    masks, scaled = head_masks(), head_masks(HEAD_DIM**-0.5)
    dctx = dot(da_ref[...], out_weight_ref[...], NT).astype(BF16)

    @pl.when(pl.program_id(0) == 0)
    def _():
        sum_ref[...] = jnp.zeros_like(sum_ref)

    def store(column, value):
        low = value.astype(BF16)
        dqkv_ref[:, column : column + LANES] = low
        sum_ref[:, column : column + LANES] += jnp.sum(low.astype(F32), axis=0, keepdims=True)

    for start in range(0, width, LANES):
        q_pair = qkv_ref[:, start : start + LANES]
        k_stack = stacked(qkv_ref[:, width + start : width + start + LANES], scaled)
        v_stack = stacked(qkv_ref[:, 2 * width + start : 2 * width + start + LANES], masks)
        d_pair = dctx[:, start : start + LANES]
        probs = pair_probs(k_stack, q_pair, length)
        low = probs.astype(BF16).reshape(k_stack.shape[0], q_pair.shape[0])
        dprobs = dot(v_stack, d_pair, NT).reshape(probs.shape)
        inner = jnp.sum(dprobs * probs, axis=1, keepdims=True)
        dscores = (probs * (dprobs - inner)).astype(BF16).reshape(low.shape)
        store(start, dot(dscores, k_stack, TN))
        store(width + start, dot(side_by_side(dscores), stacked(q_pair, scaled)))
        store(2 * width + start, dot(side_by_side(low), stacked(d_pair, masks)))


def attention_back(qkv, da, whole_a, lens, first, count, before=None):
    total, width = da.shape
    rows = total // lens.shape[0]
    extra = [] if before is None else [before]
    return pl.pallas_call(
        attention_back_kernel,
        out_shape=[
            jax.ShapeDtypeStruct((total, 3 * width), BF16),
            jax.ShapeDtypeStruct((1, 3 * width), F32),
        ],
        grid_spec=pltpu.PrefetchScalarGridSpec(
            num_scalar_prefetch=1,
            grid=(count,),
            in_specs=[
                pl.BlockSpec((rows, 3 * width), lambda i, _: (i + first, 0)),
                pl.BlockSpec((rows, width), lambda i, _: (i + first, 0)),
                pl.BlockSpec((width, width), lambda i, _: (0, 3)),
            ]
            + [pl.BlockSpec(memory_space=pl.ANY)] * len(extra),
            out_specs=[
                pl.BlockSpec((rows, 3 * width), lambda i, _: (i + first, 0)),
                pl.BlockSpec((1, 3 * width), lambda i, _: (0, 0)),
            ],
        ),
        input_output_aliases={4: 0} if extra else {},
        compiler_params=params(),
        cost_estimate=cost(count * rows * width * (20 * rows + 2 * width), 14 * count * rows * width),
        name="attention_backward",
    )(lax.slice_in_dim(lens, first, first + count), qkv, da, whole_a, *extra)


def join_halves(core, own_ref, other_ref, joined):
    joined[:, core] = own_ref[...]
    joined[:, 1 - core] = other_ref[...]
    return joined[...].reshape(-1, joined.shape[-1])


def up_kernel(core_ref, low_ref, own_ref, other_ref, small_ref, active_ref, slope_ref, joined):
    weight = join_halves(core_ref[0], own_ref, other_ref, joined)
    block = weight.shape[1]
    rows = small_ref.shape[0]
    fold = block // rows
    column = lax.broadcasted_iota(jnp.int32, (LANES, block), 0)
    lane = lax.broadcasted_iota(jnp.int32, (LANES, block), 1)
    spread = (column == SMALL - 4 + lane % fold).astype(F32).astype(BF16)
    row = lax.broadcasted_iota(jnp.int32, (rows, block), 0)
    at = lax.broadcasted_iota(jnp.int32, (rows, block), 1)
    bias = jnp.sum(
        jnp.where(at // fold == row, dot(small_ref[...], spread), 0.0), axis=0, keepdims=True
    )
    step = LANES
    for start in range(0, low_ref.shape[0], step):
        hidden = dot(low_ref[start : start + step, :], weight) + bias
        cdf = 0.5 * (1.0 + lax.erf(hidden * (2.0**-0.5)))
        active_ref[start : start + step, :] = (hidden * cdf).astype(BF16)
        density = jnp.exp(-0.5 * hidden * hidden) * ((2.0 * np.pi) ** -0.5)
        slope_ref[start : start + step, :] = (cdf + hidden * density).astype(BF16)


def up_and_gelu(low, own, other, whole_a, core):
    rows, width = low.shape
    parts, run, ff = own.shape
    block = 512
    half = pl.BlockSpec((parts, run, block), lambda i, _: (0, 0, i))
    return pl.pallas_call(
        up_kernel,
        out_shape=[jax.ShapeDtypeStruct((rows, ff), BF16)] * 2,
        grid_spec=pltpu.PrefetchScalarGridSpec(
            num_scalar_prefetch=1,
            grid=(ff // block,),
            in_specs=[
                whole_spec((rows, width)),
                half,
                half,
                pl.BlockSpec(
                    (width * block // ff, LANES), lambda i, _: (i, whole_a.shape[1] // LANES - 1)
                ),
            ],
            out_specs=[pl.BlockSpec((rows, block), lambda i, _: (0, i))] * 2,
            scratch_shapes=[pltpu.VMEM((parts, 2, run, block), BF16)],
        ),
        cost_estimate=cost(2 * rows * width * ff, 2 * (width * ff + 2 * rows * ff)),
        compiler_params=params(),
        name="up_gelu",
    )(core, low, own, other, whole_a)


def down_kernel(
    active_ref, down_ref, unit_ref, cot_ref, vec_ref, out_ref, dr2_ref, df_ref, sum_ref
):
    @pl.when(pl.program_id(0) == 0)
    def _():
        sum_ref[...] = jnp.zeros_like(sum_ref)

    bias, gain, shift = vec_ref[5:6, :], vec_ref[6:7, :], vec_ref[7:8, :]
    hidden = unit_ref[...] * vec_ref[3:4, :] + vec_ref[4:5, :]
    total = hidden + dot(active_ref[...], down_ref[...]) + bias
    unit, root = normed(total)
    out_ref[...] = (unit * gain + shift).astype(BF16)
    grad = cot_ref[...].astype(F32)
    dr2 = norm_back(grad, unit, root, gain)
    dr2_ref[...] = dr2
    df = dr2.astype(BF16)
    df_ref[...] = df
    sum_ref[0:1, :] += jnp.sum(df.astype(F32), axis=0, keepdims=True)
    sum_ref[1:2, :] += jnp.sum(grad * unit, axis=0, keepdims=True)
    sum_ref[2:3, :] += jnp.sum(grad, axis=0, keepdims=True)


def down_and_norm(active, down, unit, cot, vectors):
    rows, ff = active.shape
    width = down.shape[1]
    block = 256
    tokens = pl.BlockSpec((block, width), lambda i: (i, 0))
    return pl.pallas_call(
        down_kernel,
        out_shape=[
            jax.ShapeDtypeStruct((rows, width), BF16),
            jax.ShapeDtypeStruct((rows, width), F32),
            jax.ShapeDtypeStruct((rows, width), BF16),
            jax.ShapeDtypeStruct((8, width), F32),
        ],
        grid=(rows // block,),
        in_specs=[
            pl.BlockSpec((block, ff), lambda i: (i, 0)),
            whole_spec((ff, width)),
            tokens,
            tokens,
            whole_spec(vectors.shape),
        ],
        out_specs=[tokens, tokens, tokens, whole_spec((8, width))],
        compiler_params=params(),
        cost_estimate=cost(2 * rows * width * ff, 2 * (width * ff + rows * ff) + 14 * rows * width),
        name="down_norm",
    )(active, down, unit, cot, vectors)


def back_kernel(
    core_ref,
    df_ref,
    down_ref,
    slope_ref,
    own_ref,
    other_ref,
    dr2_ref,
    unit_ref,
    root_ref,
    vec_ref,
    du_ref,
    dr1_ref,
    da_ref,
    bias_ref,
    sum_ref,
    joined,
    total,
):
    at = pl.program_id(0)
    weight = join_halves(core_ref[0], own_ref, other_ref, joined)
    step = 384

    @pl.when(at == 0)
    def _():
        total[...] = dr2_ref[...]
        sum_ref[...] = jnp.zeros_like(sum_ref)

    bias = jnp.zeros(bias_ref.shape, F32)
    for start in range(0, df_ref.shape[0], step):
        rows = slice(start, start + step)
        du = dot(df_ref[rows, :], down_ref[...], NT) * slope_ref[rows, :].astype(F32)
        du = du.astype(BF16)
        du_ref[rows, :] = du
        bias += jnp.sum(du.astype(F32), axis=0, keepdims=True)
        total[rows, :] += dot(du, weight, NT)
    bias_ref[...] = bias

    @pl.when(at == pl.num_programs(0) - 1)
    def _():
        for start in range(0, df_ref.shape[0], step):
            rows = slice(start, start + step)
            grad, unit = total[rows, :], unit_ref[rows, :]
            dr1 = norm_back(grad, unit, root_ref[rows, :], vec_ref[3:4, :])
            dr1_ref[rows, :] = dr1
            da = dr1.astype(BF16)
            da_ref[rows, :] = da
            sum_ref[0:1, :] += jnp.sum(da.astype(F32), axis=0, keepdims=True)
            sum_ref[1:2, :] += jnp.sum(grad * unit, axis=0, keepdims=True)
            sum_ref[2:3, :] += jnp.sum(grad, axis=0, keepdims=True)


def feed_back(df, down, slope, own, other, dr2, unit, root, vectors, core):
    rows, width = df.shape
    parts, run, ff = own.shape
    block = 768
    half = pl.BlockSpec((parts, run, block), lambda i, _: (0, 0, i))
    columns = pl.BlockSpec((rows, block), lambda i, _: (0, i))
    tokens = whole_spec((rows, width))
    return pl.pallas_call(
        back_kernel,
        out_shape=[
            jax.ShapeDtypeStruct((rows, ff), BF16),
            jax.ShapeDtypeStruct((rows, width), F32),
            jax.ShapeDtypeStruct((rows, width), BF16),
            jax.ShapeDtypeStruct((1, ff), F32),
            jax.ShapeDtypeStruct((8, width), F32),
        ],
        grid_spec=pltpu.PrefetchScalarGridSpec(
            num_scalar_prefetch=1,
            grid=(ff // block,),
            in_specs=[
                tokens,
                pl.BlockSpec((block, width), lambda i, _: (i, 0)),
                columns,
                half,
                half,
                tokens,
                tokens,
                whole_spec(root.shape),
                whole_spec(vectors.shape),
            ],
            out_specs=[
                columns,
                tokens,
                tokens,
                pl.BlockSpec((1, block), lambda i, _: (0, i)),
                whole_spec((8, width)),
            ],
            scratch_shapes=[
                pltpu.VMEM((parts, 2, run, block), BF16),
                pltpu.VMEM((rows, width), F32),
            ],
        ),
        compiler_params=params(),
        cost_estimate=cost(4 * rows * width * ff, 4 * (width * ff + rows * ff) + 14 * rows * width),
        name="feed_forward_back",
    )(core, df, down, slope, own, other, dr2, unit, root, vectors)


def normed(values):
    centre = values - jnp.mean(values, axis=-1, keepdims=True)
    root = lax.rsqrt(jnp.mean(centre * centre, axis=-1, keepdims=True) + 1e-05)
    return centre * root, root


def norm_back(grad, unit, root, gain):
    scaled = grad * gain
    inner = jnp.mean(scaled * unit, axis=-1, keepdims=True)
    return root * (scaled - jnp.mean(scaled, axis=-1, keepdims=True) - unit * inner)


def transposed_rows(vectors):
    count, size = vectors.shape
    padded = jnp.concatenate([vectors, jnp.zeros((LANES - count, size), vectors.dtype)], axis=0)
    row = lax.broadcasted_iota(jnp.int32, (size, size), 0)
    column = lax.broadcasted_iota(jnp.int32, (size, size), 1)
    unit = (row == column).astype(F32).astype(BF16)
    return dot(unit, padded.astype(BF16), NT)


def folded(values, rows):
    size = values.shape[1]
    fold = size // rows
    row = lax.broadcasted_iota(jnp.int32, (rows, size), 0)
    at = lax.broadcasted_iota(jnp.int32, (rows, size), 1)
    spread = jnp.where(at // fold == row, values.astype(F32), 0.0).astype(BF16)
    column = lax.broadcasted_iota(jnp.int32, (LANES, size), 0)
    lane = lax.broadcasted_iota(jnp.int32, (LANES, size), 1)
    place = (column == SMALL - 4 + lane % fold).astype(F32).astype(BF16)
    return dot(spread, place, NT)


def pack_kernel(*refs):
    matrices, vectors, up_bias_ref, out_ref = refs[:4], refs[4:12], refs[12], refs[13]
    rows = out_ref.shape[1]
    for model in range(2):
        start = 0
        for matrix in matrices:
            out_ref[model, :, start : start + matrix.shape[2]] = matrix[model]
            start += matrix.shape[2]
        eight = jnp.concatenate([v[model : model + 1, :].astype(F32) for v in vectors], axis=0)
        small = transposed_rows(eight) + folded(up_bias_ref[model : model + 1, :].astype(F32), rows)
        out_ref[model, :, start:] = small.astype(BF16)


def pack(matrices, vectors, up_bias):
    models, rows, _ = matrices[0].shape
    lanes = sum(m.shape[2] for m in matrices) + LANES
    if rows % 8:
        parts = [v[..., None] for v in vectors] + [up_bias.reshape(models, rows, -1)]
        small = jnp.concatenate(parts, axis=-1)
        small = jnp.pad(small, [(0, 0), (0, 0), (0, LANES - small.shape[-1])])
        return jnp.concatenate(list(matrices) + [small], axis=-1)
    return pl.pallas_call(
        pack_kernel,
        out_shape=jax.ShapeDtypeStruct((models, rows, lanes), BF16),
        compiler_params=params(),
        name="pack_shard",
    )(*matrices, *vectors, up_bias)


def small_grads_kernel(down_ref, back_ref, bias_ref, qkv_ref, out_ref):
    rows = out_ref.shape[0]
    width = down_ref.shape[1]
    eight = jnp.concatenate(
        [
            qkv_ref[:, :width],
            qkv_ref[:, 2 * width :],
            back_ref[0:3, :],
            down_ref[0:3, :],
        ],
        axis=0,
    )
    out_ref[...] = transposed_rows(eight).astype(BF16)
    step = LANES
    fold = bias_ref.shape[1] // rows
    for start in range(0, rows, step):
        values = bias_ref[:, start * fold : (start + step) * fold]
        here = slice(start, start + step)
        out_ref[here, :] = (out_ref[here, :].astype(F32) + folded(values, step)).astype(BF16)


def small_grads(down_sums, back_sums, bias_sums, qkv_sums):
    width = down_sums.shape[1]
    return pl.pallas_call(
        small_grads_kernel,
        out_shape=jax.ShapeDtypeStruct((width, LANES), BF16),
        compiler_params=params(),
        name="small_gradients",
    )(down_sums, back_sums, bias_sums, qkv_sums)


class Ring:
    def __init__(self, count):
        depth = 4 if count % 4 == 0 else 2
        wide = count // depth
        order = []
        if wide > 1:
            for z in range(depth):
                ys = range(1, wide) if z % 2 == 0 else reversed(range(1, wide))
                order += [z * wide + y for y in ys]
            order += [z * wide for z in reversed(range(depth))]
        else:
            order = list(range(count))
        self.count, self.depth, self.wide = count, depth, wide
        self.long = count // 2
        self.short = count - 1 - self.long
        self.ahead, self.behind = [], []
        for core in range(2):
            sign = 1 if core == 0 else -1
            here = core * count
            for place, chip in enumerate(order):
                self.ahead.append((here + chip, here + order[(place + sign) % count]))
                self.behind.append((here + chip, here + order[(place - sign) % count]))

    def origins(self, core, chip):
        depth, turn = self.depth, self.wide - 1
        if turn == 0:
            place = chip
        else:
            z, y = lax.div(chip, self.wide), lax.rem(chip, self.wide)
            along = jnp.where(lax.rem(z, 2) == 0, y - 1, turn - y)
            place = jnp.where(y == 0, depth * turn + depth - 1 - z, z * turn + along)
        sign = 1 - 2 * core
        chips = []
        for k in range(self.count):
            off = -k if k <= self.long else k - self.long
            at = lax.rem(place + sign * off + self.count, self.count)
            if turn > 0:
                z, j = lax.div(at, turn), lax.rem(at, turn)
                y = jnp.where(lax.rem(z, 2) == 0, 1 + j, turn - j)
                at = jnp.where(
                    at < depth * turn, z * self.wide + y, (depth * (turn + 1) - 1 - at) * self.wide
                )
            chips.append(at)
        return chips

    def forth(self, block):
        return lax.ppermute(block, ("core", "f"), self.ahead)

    def back(self, block):
        return lax.ppermute(block, ("core", "f"), self.behind)


def swap(value, axis):
    return lax.ppermute(value, axis, SWAP)


def pick(value, index, axis):
    return lax.dynamic_index_in_dim(value, index, axis, keepdims=False)


def two_sides(own, other, side, groups):
    place = lax.broadcasted_iota(jnp.int32, (2, 1, 1), 0)
    block = jnp.where(place == side, own[None], other[None])
    if groups > 1:
        return lax.all_gather(block, "r", axis=0, tiled=False)
    return block[None]


def ring_gather(ring, block, works):
    forth, back = [block], [block]
    theirs = [swap(block, "core")]
    outs = []
    for k in range(1, ring.long + 1):
        a = ring.forth(forth[-1])
        b = ring.back(back[-1]) if k <= ring.short else None
        if k - 1 < len(works) and works[k - 1] is not None:
            done = works[k - 1](forth[-1], outs)
            if b is None:
                a, done = tie(a, done)
            else:
                a, b, done = tie(a, b, done)
            outs.append(done)
        forth.append(a)
        if b is not None:
            back.append(b)
    mine = forth + back[1:]
    theirs += [swap(b, "core") for b in mine[1:]]
    return mine, theirs, outs


def assemble_kernel(ring, with_vectors, at_ref, *refs):
    count = ring.count
    blocks, out_ref, sems = refs[: 2 * count], refs[2 * count], refs[-1]
    core, chip = at_ref[0], at_ref[1]
    here, there = ring.origins(core, chip), ring.origins(1 - core, chip)
    copies = []
    for i, (block, at) in enumerate(zip(blocks, here + there)):
        half = core if i < count else 1 - core
        for r in range(block.shape[0]):
            for x in range(2):
                copies.append(
                    pltpu.make_async_copy(
                        block.at[r, x], out_ref.at[r, x, half, at], sems.at[len(copies)]
                    )
                )
    for copy in copies:
        copy.start()
    for copy in copies:
        copy.wait()
    if with_vectors:
        rows = out_ref[:, :, :, :, :, out_ref.shape[-1] - LANES :]
        small = rows.astype(F32).reshape(-1, LANES)
        refs[2 * count + 1][...] = small.T[:16]


def assemble(ring, mine, theirs, core, with_vectors=False):
    groups, _, rows, lanes = mine[0].shape
    count = ring.count
    chip = lax.axis_index("f")
    shape = (groups, 2, 2, count, rows, lanes)
    width = shape[1] * shape[2] * groups * count * rows
    if rows % 8:
        whole = jnp.zeros(shape, BF16)
        at = ring.origins(core, chip) + ring.origins(1 - core, chip)
        for i, block in enumerate(mine + theirs):
            half = core if i < count else 1 - core
            where = (0, 0, half, at[i], 0, 0)
            whole = lax.dynamic_update_slice(whole, block[:, :, None, None], where)
        whole = whole.reshape(-1, lanes)
        return whole, (whole[:, lanes - LANES :].astype(F32).T[:16] if with_vectors else None)
    out_shape = [jax.ShapeDtypeStruct(shape, BF16)]
    if with_vectors:
        out_shape.append(jax.ShapeDtypeStruct((16, width), F32))
    out = pl.pallas_call(
        functools.partial(assemble_kernel, ring, with_vectors),
        out_shape=out_shape,
        in_specs=[pl.BlockSpec(memory_space=pltpu.SMEM)]
        + [pl.BlockSpec(memory_space=pl.ANY)] * (2 * count),
        scratch_shapes=[pltpu.SemaphoreType.DMA((4 * count * groups,))],
        compiler_params=params(),
        name="assemble",
    )(jnp.stack([core, chip]).astype(jnp.int32), *mine, *theirs)
    return out[0].reshape(-1, lanes), out[1] if with_vectors else None


def scatter_blocks(own, other, origins):
    def term(k):
        a = [pick(h, origins[k], 2) for h in own]
        b = [pick(h, origins[k], 2) for h in other]
        return tuple(x.astype(F32) + y.astype(F32) for x, y in zip(a, b))

    return term


def low(values):
    return tuple(v.astype(BF16) for v in values)


def plus(values, terms):
    return tuple(v.astype(F32) + t for v, t in zip(values, terms))


def ring_scatter(ring, term, works):
    long, short = ring.long, ring.short
    outs = []
    far = low(term(long))
    near = low(term(long + short)) if short else None
    work_at = 0
    for k in range(1, long + 1):
        sent_far = tuple(ring.back(v) for v in far)
        moving = near is not None and k > long - short
        sent_near = tuple(ring.forth(v) for v in near) if moving else None
        if work_at < len(works) and works[work_at] is not None:
            done = works[work_at](far, outs)
            if moving:
                sent_far, sent_near, done = tie(sent_far, sent_near, done)
            else:
                sent_far, done = tie(sent_far, done)
            outs.append(done)
        work_at += 1
        if k < long:
            far = low(plus(sent_far, term(long - k)))
            if moving:
                left = long - k
                near = low(plus(sent_near, term(long + left)))
    total = plus(sent_far, term(0))
    if short:
        total = plus(total, sent_near)
    return total, outs


def to_owners(total, side, groups):
    if groups > 1:
        total = lax.psum_scatter(total.astype(BF16), "r", scatter_dimension=0, tiled=True)
    total = total[0]
    own = pick(total, side, 0).astype(F32)
    other = swap(pick(total, 1 - side, 0).astype(BF16), "t").astype(F32)
    place = lax.broadcasted_iota(jnp.int32, (2, 1, 1), 0)
    return jnp.where(place == side, own[None], other[None])


def narrow_grad_kernel(core_ref, left_ref, right_ref, out_ref, turned):
    half, n = pl.program_id(0), right_ref.shape[1]
    parts, run = out_ref.shape[0], out_ref.shape[1]

    @pl.when(half == 0)
    def _():
        turned[...] = left_ref[...].T

    left = jnp.concatenate(
        [turned[pl.ds(pl.multiple_of((2 * i + core_ref[0]) * run, 16), run), :] for i in range(parts)],
        axis=0,
    )
    out_ref[...] = dot(left, right_ref[...]).astype(BF16).reshape(parts, run, n)


def wide_grad_kernel(core_ref, left_ref, right_ref, out_ref):
    blocks = (out_ref.shape[0],) + out_ref.shape[2:]
    out_ref[:, 0] = dot(left_ref[...], right_ref[...], TN).astype(BF16).reshape(blocks)


def half_grad(left, right, half, parts, count):
    tokens, size = left.shape
    run = size // (2 * parts)
    n = right.shape[1]
    flops = cost(size * tokens * n, 2 * (size * tokens + tokens * n) + size * n)
    if run % LANES == 0 and (run // count) % 16 == 0:
        return pl.pallas_call(
            wide_grad_kernel,
            out_shape=jax.ShapeDtypeStruct((count, parts, run // count, n), BF16),
            grid_spec=pltpu.PrefetchScalarGridSpec(
                num_scalar_prefetch=1,
                grid=(parts,),
                in_specs=[
                    pl.BlockSpec((tokens, run), lambda i, h: (0, 2 * i + h[0])),
                    whole_spec((tokens, n)),
                ],
                out_specs=pl.BlockSpec((count, 1, run // count, n), lambda i, h: (0, i, 0, 0)),
            ),
            compiler_params=params(),
            cost_estimate=flops,
            name="wide_gradient",
        )(half, left, right)
    if run % 16 == 0:
        block = 768
        return pl.pallas_call(
            narrow_grad_kernel,
            out_shape=jax.ShapeDtypeStruct((parts, run, n), BF16),
            grid_spec=pltpu.PrefetchScalarGridSpec(
                num_scalar_prefetch=1,
                grid=(n // block,),
                in_specs=[
                    whole_spec((tokens, size)),
                    pl.BlockSpec((tokens, block), lambda j, h: (0, j)),
                ],
                out_specs=pl.BlockSpec((parts, run, block), lambda j, h: (0, 0, j)),
                scratch_shapes=[pltpu.VMEM((size, tokens), BF16)],
            ),
            compiler_params=params(),
            cost_estimate=flops,
            name="narrow_gradient",
        )(half, left, right)
    full = dot(left, right, TN).astype(BF16).reshape(parts, 2, run, n)
    return pick(full, half[0], 1)


def both_halves(left, right, core1, parts, count):
    sent = half_grad(left, right, 1 - core1, parts, count)
    left, right, sent = tie(left, right, sent)
    arrived = swap(sent, "core")
    own = half_grad(left, right, core1, parts, count)
    return own, arrived


def places(tags, model):
    member = tags[:, 0] == model
    count = member.shape[0]
    before = lax.broadcasted_iota(jnp.int32, (count, count), 0) < lax.broadcasted_iota(
        jnp.int32, (count, count), 1
    )
    ranking = jnp.sum(jnp.where(before & member[:, None], 1, 0), axis=0)
    slots = lax.broadcasted_iota(jnp.int32, (CAP, count), 0)
    return (slots == ranking[None, :]) & member[None, :]


def route(chosen, chains):
    marked = jnp.where(chosen[:, :, None, None], chains[None], jnp.zeros((), chains.dtype))
    return jnp.sum(marked.astype(F32), axis=1).astype(chains.dtype)


def body(ring, groups, *args):
    (
        inputs,
        cotangent,
        lengths,
        tags,
        query_weight,
        query_bias,
        key_weight,
        value_weight,
        value_bias,
        output_projection_weight,
        out_bias,
        first_gain,
        first_shift,
        up_weight,
        up_bias,
        down_weight,
        down_bias,
        second_gain,
        second_shift,
    ) = args
    side, core = lax.axis_index("t"), lax.axis_index("core")
    core1 = core.astype(jnp.int32)[None]
    chains = lengths.shape[0]
    width = inputs.shape[1]
    ff = up_weight.shape[2]
    slots = inputs.shape[0] // chains
    tokens = 2 * CAP * slots
    parts = 2 * groups

    shard_a = pack(
        (query_weight, key_weight, value_weight, output_projection_weight),
        (
            query_bias,
            value_bias,
            out_bias,
            first_gain,
            first_shift,
            down_bias,
            second_gain,
            second_shift,
        ),
        up_bias,
    )
    block_a = two_sides(
        pick(shard_a, side, 0), swap(pick(shard_a, 1 - side, 0), "t"), side, groups
    )

    own_places, other_places = places(tags, side), places(tags, 1 - side)
    own_len = jnp.sum(jnp.where(own_places, lengths[None, :], 0), axis=1)
    other_len = jnp.sum(jnp.where(other_places, lengths[None, :], 0), axis=1)
    chain_rows = inputs.reshape(chains, slots, width)
    sent_lens = jnp.broadcast_to(other_len[:, None, None], (CAP, 16, width)).astype(BF16)
    sent = jnp.concatenate([route(other_places, chain_rows), sent_lens], axis=1)

    def exchanged(now, weight):
        _, weight = tie(now, weight)
        return two_sides(
            pick(weight, side, 0), swap(pick(weight, 1 - side, 0), "t"), side, groups
        )

    def exchange_up(now, outs):
        return exchanged(now, up_weight)

    def exchange_rows(now, outs):
        _, message = tie(now, sent)
        arrived = swap(message, "t")
        rows = jnp.concatenate([route(own_places, chain_rows), arrived[:, :slots]], axis=0)
        lens = jnp.concatenate([own_len, arrived[:, slots, 0].astype(jnp.int32)])
        return rows.reshape(tokens, width), lens

    def exchange_down(now, outs):
        return exchanged(now, down_weight)

    mine, theirs, outs = ring_gather(ring, block_a, [exchange_up, exchange_rows, exchange_down])
    block_u, (rows_in, lens), block_d = outs
    own_u = lax.all_gather(block_u.reshape(parts, -1, ff), "f", axis=1, tiled=True)

    def step_cot(now, outs):
        _, a, b = tie(now, mine, theirs)
        _, cot_rows = tie(now, cotangent.reshape(chains, slots, width))
        cot = jnp.concatenate(
            [route(own_places, cot_rows), swap(route(other_places, cot_rows), "t")], axis=0
        )
        return assemble(ring, a, b, core, True) + (cot.reshape(tokens, width),)

    def step_attention(now, outs):
        whole_a, vectors, _ = outs[0]
        _, own = tie(now, own_u)
        return (swap(own, "core"), own) + tuple(attention(rows_in, lens, whole_a, vectors))

    def step_up(now, outs):
        other, own = outs[1][:2]
        return up_and_gelu(outs[1][-1], own, other, outs[0][0], core1)

    block_d, mine[ring.long] = tie(block_d, mine[ring.long])
    mine_d, theirs_d, outs = ring_gather(ring, block_d, [step_cot, step_attention, step_up])
    whole_a, vectors, cot = outs[0]
    other_u, own_u, qkv, context, unit1, root1, low1 = outs[1]
    active, slope = outs[2]
    whole_d, _ = assemble(ring, mine_d, theirs_d, core)
    gain1 = vectors[3:4]

    result, dr2, df, down_sums = down_and_norm(active, whole_d, unit1, cot, vectors)

    own_d, arrived_d = both_halves(active, df, core1, parts, ring.count)
    half_d = (own_d.astype(F32) + arrived_d.astype(F32)).astype(BF16)
    if half_d.ndim == 3:
        half_d = jnp.moveaxis(half_d.reshape(parts, ring.count, -1, width), 1, 0)
    total_d = lax.psum_scatter(
        half_d.reshape(-1, width), "f", scatter_dimension=0, tiled=True
    ).reshape(groups, 2, -1, width)

    df_now, half_d = tie(df, half_d)
    du, dr1, da, bias_sums, back_sums = feed_back(
        df_now, whole_d, slope, own_u, other_u, dr2, unit1, root1, vectors, core1
    )
    origins = ring.origins(core, lax.axis_index("f"))

    def by_blocks(value):
        return value.reshape(groups, 2, ring.count, -1, value.shape[-1])

    own_half_u, other_half_u = both_halves(low1, du, core1, parts, ring.count)
    term_u = scatter_blocks([by_blocks(own_half_u)], [by_blocks(other_half_u)], origins)

    def back_first(now, outs):
        _, da_now, out_rows = tie(now, da, result.reshape(2, CAP, slots, width)[1])
        back = attention_back(qkv, da_now, whole_a, lens, 0, CAP)
        return back[0], back[1], swap(out_rows, "t")

    def back_second(now, outs):
        _, da_now, before = tie(now, da, outs[0][0])
        return attention_back(qkv, da_now, whole_a, lens, CAP, CAP, before)

    def out_grads(now, outs):
        _, ctx_now, dqkv = tie(now, context, outs[1][0])
        return both_halves(ctx_now, da, core1, parts, ring.count) + (dqkv,)

    total_u, outs = ring_scatter(ring, term_u, [back_first, back_second, out_grads])
    (_, sums_1, back_out), (_, sums_2), (own_o, other_o, dqkv) = outs
    own_qkv, other_qkv = both_halves(rows_in, dqkv, core1, parts, ring.count)
    small_grad = small_grads(down_sums, back_sums, bias_sums, sums_1 + sums_2)
    small_grad = small_grad.reshape(parts, 2, -1, LANES)
    other_small = swap(pick(small_grad, 1 - core, 1), "core")
    own_os = jnp.concatenate([own_o, pick(small_grad, core, 1)], axis=-1)
    other_os = jnp.concatenate([other_o, other_small], axis=-1)
    term_a = scatter_blocks(
        [by_blocks(own_qkv), by_blocks(own_os)], [by_blocks(other_qkv), by_blocks(other_os)], origins
    )

    def second_half(values):
        return values.reshape(2, CAP, slots, width)[1]

    def home(values, back):
        both = jnp.concatenate([values.reshape(2, CAP, slots, width)[0], back], axis=0)
        return route(jnp.concatenate([own_places, other_places], axis=0).T, both).reshape(-1, width)

    def owners_u(now, outs):
        _, total = tie(now, total_u[0])
        return to_owners(total, side, groups)

    def owners_d(now, outs):
        _, total = tie(now, total_d)
        return to_owners(total, side, groups)

    def begin(now, outs):
        _, dq = tie(now, dqkv)
        return (dr1 + dot(dq, whole_a[:, : 3 * width], NT)).astype(BF16)

    output = home(result, back_out)
    total_a, outs = ring_scatter(ring, term_a, [begin, owners_u, owners_d])
    rows_grad, grads_u, grads_d = outs
    back_rows = swap(second_half(rows_grad), "t")
    input_grad = home(rows_grad, back_rows)

    grads_qkv = to_owners(total_a[0], side, groups)
    grads_os = to_owners(total_a[1], side, groups)
    columns = jnp.swapaxes(grads_os[:, :, width : width + 16], 1, 2)
    return (
        output,
        input_grad,
        grads_qkv[:, :, :width],
        columns[:, 0],
        grads_qkv[:, :, width : 2 * width],
        grads_qkv[:, :, 2 * width :],
        columns[:, 1],
        grads_os[:, :, :width],
        columns[:, 2],
        columns[:, 3],
        columns[:, 4],
        grads_u,
        jnp.swapaxes(columns[:, 8:12], 1, 2).reshape(2, -1),
        grads_d,
        columns[:, 5],
        columns[:, 6],
        columns[:, 7],
    )


def solution(mesh):
    dp, fsdp = mesh.shape["dp"], mesh.shape["fsdp"]
    groups = dp // 4
    inner = Mesh(mesh.devices.reshape(groups, 2, 2, fsdp), ("r", "t", "core", "f"))
    every = ("r", "t", "core", "f")
    rows, vector, matrix = P(every, None), P(None, every), P(None, every, None)
    weights = (
        matrix,
        vector,
        matrix,
        matrix,
        vector,
        matrix,
        vector,
        vector,
        vector,
        matrix,
        vector,
        matrix,
        vector,
        vector,
        vector,
    )
    return jax.shard_map(
        functools.partial(body, Ring(fsdp), groups),
        mesh=inner,
        in_specs=(rows, rows, P(every), rows) + weights,
        out_specs=(rows, rows) + weights,
        check_vma=False,
    )
```

```python
import functools

import jax
import jax.numpy as jnp
import numpy as np
from jax import lax
from jax.experimental import pallas as pl
from jax.experimental.pallas import tpu as pltpu
from jax.sharding import Mesh
from jax.sharding import PartitionSpec as P

HEADS = 12
HEAD_DIM = 64
CAP = 3
MIN_LEN = 96
LANES = 128
BF16 = jnp.bfloat16
F32 = jnp.float32
NN = (((1,), (0,)), ((), ()))
NT = (((1,), (1,)), ((), ()))
TN = (((0,), (0,)), ((), ()))
SWAP = [(0, 1), (1, 0)]
VMEM_LIMIT = 56 * 2**20
VMEM_MOST = 56 * 2**20
SMALL = 12


def dot(a, b, dims=NN):
    return lax.dot_general(a, b, dims, preferred_element_type=F32)


def tie(*values):
    return lax.optimization_barrier(values)


def params(limit=VMEM_LIMIT):
    return pltpu.CompilerParams(vmem_limit_bytes=limit)


def cost(flops, moved, exps=0):
    return pl.CostEstimate(flops=flops, bytes_accessed=moved, transcendentals=exps)


def whole_spec(shape):
    return pl.BlockSpec(shape, lambda *_: (0,) * len(shape), pipeline_mode=pl.Buffered(1))


def fixed(shape):
    return pl.BlockSpec(shape, lambda *_: (0,) * len(shape))


def head_masks(value=1.0):
    lane = lax.broadcasted_iota(jnp.int32, (1, LANES), 1)
    first = jnp.where(lane < HEAD_DIM, value, 0.0).astype(BF16)
    second = jnp.where(lane >= HEAD_DIM, value, 0.0).astype(BF16)
    return first, second


def stacked(two_heads, masks):
    return jnp.concatenate([two_heads * masks[0], two_heads * masks[1]], axis=0)


def side_by_side(rows):
    half = rows.shape[0] // 2
    return jnp.concatenate([rows[:half], rows[half:]], axis=1)


def pair_probs(k_stack, q_pair, length):
    scores = dot(k_stack, q_pair, NT)
    keys = k_stack.shape[0] // 2
    scores = scores.reshape(2, keys, scores.shape[1])
    always = scores[:, :MIN_LEN]
    rest = scores[:, MIN_LEN:]
    slot = lax.broadcasted_iota(jnp.int32, rest.shape, 1) + MIN_LEN
    rest = jnp.where(slot < length, rest, -1000000000.0)
    scores = jnp.concatenate([always, rest], axis=1)
    exponent = jnp.exp(scores - jnp.max(scores, axis=1, keepdims=True))
    return exponent * (1.0 / jnp.sum(exponent, axis=1, keepdims=True))


def attention_rows(length, qkv_ref, ctx_ref, base, rows, width):
    masks, scaled = head_masks(), head_masks(HEAD_DIM**-0.5)
    at = slice(base, base + rows)
    for start in range(0, width, LANES):
        q_pair = qkv_ref[at, start : start + LANES]
        k_stack = stacked(qkv_ref[at, width + start : width + start + LANES], scaled)
        v_stack = stacked(qkv_ref[at, 2 * width + start : 2 * width + start + LANES], masks)
        probs = pair_probs(k_stack, q_pair, length)
        low = probs.astype(BF16).reshape(k_stack.shape[0], q_pair.shape[0])
        ctx_ref[at, start : start + LANES] = dot(low, v_stack, TN).astype(BF16)


def attention_kernel(
    lens_ref,
    rows_ref,
    weight_ref,
    vec_ref,
    qkv_ref,
    unit_ref,
    root_ref,
    low_ref,
    rows_t_ref,
    ctx_t_ref,
    low_t_ref,
    ctx_ref,
):
    width = ctx_ref.shape[1]
    rows_t_ref[...] = rows_ref[...].T
    rows = qkv_ref.shape[0] // 2
    for part in range(3):
        columns = slice(part * width, (part + 1) * width)
        product = dot(rows_ref[...], weight_ref[:, columns])
        if part != 1:
            product = product + vec_ref[part // 2 : part // 2 + 1, :]
        qkv_ref[:, columns] = product.astype(BF16)
    for chain in range(2):
        length = lens_ref[2 * pl.program_id(0) + chain]
        attention_rows(length, qkv_ref, ctx_ref, chain * rows, rows, width)
    branch = dot(ctx_ref[...], weight_ref[:, 3 * width : 4 * width]) + vec_ref[2:3, :]
    unit, root = normed(rows_ref[...].astype(F32) + branch)
    unit_ref[...] = unit
    root_ref[...] = root
    low = (unit * vec_ref[3:4, :] + vec_ref[4:5, :]).astype(BF16)
    low_ref[...] = low
    low_t_ref[...] = low.T
    ctx_t_ref[...] = ctx_ref[...].T


def attention(rows_in, lens, whole_a, vectors):
    total, width = rows_in.shape
    rows = 2 * total // lens.shape[0]

    def tokens(lanes):
        return pl.BlockSpec((rows, lanes), lambda i, _: (i, 0))

    return pl.pallas_call(
        attention_kernel,
        out_shape=[
            jax.ShapeDtypeStruct((total, 3 * width), BF16),
            jax.ShapeDtypeStruct((total, width), F32),
            jax.ShapeDtypeStruct((total, 1), F32),
            jax.ShapeDtypeStruct((total, width), BF16),
        ]
        + [jax.ShapeDtypeStruct((width, total), BF16)] * 3,
        grid_spec=pltpu.PrefetchScalarGridSpec(
            num_scalar_prefetch=1,
            grid=(total // rows,),
            in_specs=[tokens(width), whole_spec(whole_a.shape), whole_spec(vectors.shape)],
            out_specs=[tokens(3 * width), tokens(width), tokens(1), tokens(width)]
            + [pl.BlockSpec((width, rows), lambda i, _: (0, i))] * 3,
            scratch_shapes=[pltpu.VMEM((rows, width), BF16)],
        ),
        compiler_params=params(),
        cost_estimate=cost(8 * total * width * (width + rows), 20 * total * width),
        name="attention_forward",
    )(lens, rows_in, whole_a, vectors)


def attention_back_kernel(lens_ref, *refs):
    qkv_ref, da_ref, out_weight_ref = refs[:3]
    dqkv_ref, sum_ref = refs[-2:]
    width = da_ref.shape[1]
    length = lens_ref[pl.program_id(0)]
    masks, scaled = head_masks(), head_masks(HEAD_DIM**-0.5)
    dctx = dot(da_ref[...], out_weight_ref[...], NT).astype(BF16)

    @pl.when(pl.program_id(0) == 0)
    def _():
        sum_ref[...] = jnp.zeros_like(sum_ref)

    def store(column, value):
        low = value.astype(BF16)
        dqkv_ref[:, column : column + LANES] = low
        sum_ref[:, column : column + LANES] += jnp.sum(low.astype(F32), axis=0, keepdims=True)

    for start in range(0, width, LANES):
        q_pair = qkv_ref[:, start : start + LANES]
        k_stack = stacked(qkv_ref[:, width + start : width + start + LANES], scaled)
        v_stack = stacked(qkv_ref[:, 2 * width + start : 2 * width + start + LANES], masks)
        d_pair = dctx[:, start : start + LANES]
        probs = pair_probs(k_stack, q_pair, length)
        low = probs.astype(BF16).reshape(k_stack.shape[0], q_pair.shape[0])
        dprobs = dot(v_stack, d_pair, NT).reshape(probs.shape)
        inner = jnp.sum(dprobs * probs, axis=1, keepdims=True)
        dscores = (probs * (dprobs - inner)).astype(BF16).reshape(low.shape)
        store(start, dot(dscores, k_stack, TN))
        store(width + start, dot(side_by_side(dscores), stacked(q_pair, scaled)))
        store(2 * width + start, dot(side_by_side(low), stacked(d_pair, masks)))


def attention_back(qkv, da, whole_a, lens, first, count, before=None):
    total, width = da.shape
    rows = total // lens.shape[0]
    extra = [] if before is None else [before]
    return pl.pallas_call(
        attention_back_kernel,
        out_shape=[
            jax.ShapeDtypeStruct((total, 3 * width), BF16),
            jax.ShapeDtypeStruct((1, 3 * width), F32),
        ],
        grid_spec=pltpu.PrefetchScalarGridSpec(
            num_scalar_prefetch=1,
            grid=(count,),
            in_specs=[
                pl.BlockSpec((rows, 3 * width), lambda i, _: (i + first, 0)),
                pl.BlockSpec((rows, width), lambda i, _: (i + first, 0)),
                pl.BlockSpec((width, width), lambda i, _: (0, 3)),
            ]
            + [pl.BlockSpec(memory_space=pl.ANY)] * len(extra),
            out_specs=[
                pl.BlockSpec((rows, 3 * width), lambda i, _: (i + first, 0)),
                pl.BlockSpec((1, 3 * width), lambda i, _: (0, 0)),
            ],
        ),
        input_output_aliases={4: 0} if extra else {},
        compiler_params=params(),
        cost_estimate=cost(count * rows * width * (20 * rows + 2 * width), 14 * count * rows * width),
        name="attention_backward",
    )(lax.slice_in_dim(lens, first, first + count), qkv, da, whole_a, *extra)


def up_kernel(low_ref, up_ref, small_ref, active_ref, slope_ref):
    weight = up_ref[...]
    block = weight.shape[1]
    rows = small_ref.shape[0]
    fold = block // rows
    column = lax.broadcasted_iota(jnp.int32, (LANES, block), 0)
    lane = lax.broadcasted_iota(jnp.int32, (LANES, block), 1)
    spread = (column == SMALL - 4 + lane % fold).astype(F32).astype(BF16)
    row = lax.broadcasted_iota(jnp.int32, (rows, block), 0)
    at = lax.broadcasted_iota(jnp.int32, (rows, block), 1)
    bias = jnp.sum(
        jnp.where(at // fold == row, dot(small_ref[...], spread), 0.0), axis=0, keepdims=True
    )
    step = LANES
    for start in range(0, low_ref.shape[0], step):
        hidden = dot(low_ref[start : start + step, :], weight) + bias
        cdf = 0.5 * (1.0 + lax.erf(hidden * (2.0**-0.5)))
        active_ref[start : start + step, :] = (hidden * cdf).astype(BF16)
        density = jnp.exp(-0.5 * hidden * hidden) * ((2.0 * np.pi) ** -0.5)
        slope_ref[start : start + step, :] = (cdf + hidden * density).astype(BF16)


def up_and_gelu(low, up, whole_a):
    rows, width = low.shape
    ff = up.shape[1]
    block = 512
    return pl.pallas_call(
        up_kernel,
        out_shape=[jax.ShapeDtypeStruct((rows, ff), BF16)] * 2,
        grid=(ff // block,),
        in_specs=[
            whole_spec((rows, width)),
            pl.BlockSpec((width, block), lambda i: (0, i)),
            pl.BlockSpec(
                (width * block // ff, LANES), lambda i: (i, whole_a.shape[1] // LANES - 1)
            ),
        ],
        out_specs=[pl.BlockSpec((rows, block), lambda i: (0, i))] * 2,
        cost_estimate=cost(2 * rows * width * ff, 2 * (width * ff + 2 * rows * ff)),
        compiler_params=params(),
        name="up_gelu",
    )(low, up, whole_a)


def down_kernel(
    active_ref, down_ref, unit_ref, cot_ref, vec_ref, out_ref, dr2_ref, df_ref, sum_ref
):
    @pl.when(pl.program_id(0) == 0)
    def _():
        sum_ref[...] = jnp.zeros_like(sum_ref)

    bias, gain, shift = vec_ref[5:6, :], vec_ref[6:7, :], vec_ref[7:8, :]
    hidden = unit_ref[...] * vec_ref[3:4, :] + vec_ref[4:5, :]
    total = hidden + dot(active_ref[...], down_ref[...]) + bias
    unit, root = normed(total)
    out_ref[...] = (unit * gain + shift).astype(BF16)
    grad = cot_ref[...].astype(F32)
    dr2 = norm_back(grad, unit, root, gain)
    dr2_ref[...] = dr2
    df = dr2.astype(BF16)
    df_ref[...] = df
    sum_ref[0:1, :] += jnp.sum(df.astype(F32), axis=0, keepdims=True)
    sum_ref[1:2, :] += jnp.sum(grad * unit, axis=0, keepdims=True)
    sum_ref[2:3, :] += jnp.sum(grad, axis=0, keepdims=True)


def down_and_norm(active, down, unit, cot, vectors):
    rows, ff = active.shape
    width = down.shape[1]
    block = 256
    tokens = pl.BlockSpec((block, width), lambda i: (i, 0))
    return pl.pallas_call(
        down_kernel,
        out_shape=[
            jax.ShapeDtypeStruct((rows, width), BF16),
            jax.ShapeDtypeStruct((rows, width), F32),
            jax.ShapeDtypeStruct((rows, width), BF16),
            jax.ShapeDtypeStruct((8, width), F32),
        ],
        grid=(rows // block,),
        in_specs=[
            pl.BlockSpec((block, ff), lambda i: (i, 0)),
            whole_spec((ff, width)),
            tokens,
            tokens,
            whole_spec(vectors.shape),
        ],
        out_specs=[tokens, tokens, tokens, fixed((8, width))],
        compiler_params=params(),
        cost_estimate=cost(2 * rows * width * ff, 2 * (width * ff + rows * ff) + 14 * rows * width),
        name="down_norm",
    )(active, down, unit, cot, vectors)


def back_kernel(
    core_ref,
    df_ref,
    down_ref,
    slope_ref,
    up_ref,
    low_t_ref,
    dr2_ref,
    unit_ref,
    root_ref,
    vec_ref,
    send_ref,
    own_ref,
    dr1_ref,
    da_ref,
    bias_ref,
    sum_ref,
    total,
    grad,
):
    at = pl.program_id(0)
    step = 384

    @pl.when(at == 0)
    def _():
        total[...] = dr2_ref[...]
        sum_ref[...] = jnp.zeros_like(sum_ref)

    bias = jnp.zeros(bias_ref.shape, F32)
    for start in range(0, df_ref.shape[0], step):
        rows = slice(start, start + step)
        du = dot(df_ref[rows, :], down_ref[...], NT) * slope_ref[rows, :].astype(F32)
        du = du.astype(BF16)
        grad[rows, :] = du
        bias += jnp.sum(du.astype(F32), axis=0, keepdims=True)
        total[rows, :] += dot(du, up_ref[...], NT)
    bias_ref[...] = bias
    halves_kernel(core_ref[0], low_t_ref, grad, send_ref, own_ref)

    @pl.when(at == pl.num_programs(0) - 1)
    def _():
        for start in range(0, df_ref.shape[0], step):
            rows = slice(start, start + step)
            dh1, unit = total[rows, :], unit_ref[rows, :]
            dr1 = norm_back(dh1, unit, root_ref[rows, :], vec_ref[3:4, :])
            dr1_ref[rows, :] = dr1
            da = dr1.astype(BF16)
            da_ref[rows, :] = da
            sum_ref[0:1, :] += jnp.sum(da.astype(F32), axis=0, keepdims=True)
            sum_ref[1:2, :] += jnp.sum(dh1 * unit, axis=0, keepdims=True)
            sum_ref[2:3, :] += jnp.sum(dh1, axis=0, keepdims=True)


def halves_kernel(core, left_ref, right_ref, send_ref, own_ref):
    parts, _, run, tokens = left_ref.shape
    for half, out_ref in ((1 - core, send_ref), (core, own_ref)):
        left = left_ref[:, half].reshape(parts * run, tokens)
        out_ref[...] = dot(left, right_ref[...]).astype(BF16).reshape(out_ref.shape)


def feed_back(df, down, slope, up, low_t, dr2, unit, root, vectors, core1, parts):
    rows, width = df.shape
    ff = up.shape[1]
    block = 768
    run = width // (2 * parts)
    tokens = whole_spec((rows, width))
    half = pl.BlockSpec((parts, run, block), lambda i, _: (0, 0, i))
    return pl.pallas_call(
        back_kernel,
        out_shape=[
            jax.ShapeDtypeStruct((parts, run, ff), BF16),
            jax.ShapeDtypeStruct((parts, run, ff), BF16),
            jax.ShapeDtypeStruct((rows, width), F32),
            jax.ShapeDtypeStruct((rows, width), BF16),
            jax.ShapeDtypeStruct((1, ff), F32),
            jax.ShapeDtypeStruct((8, width), F32),
        ],
        grid_spec=pltpu.PrefetchScalarGridSpec(
            num_scalar_prefetch=1,
            grid=(ff // block,),
            in_specs=[
                tokens,
                pl.BlockSpec((block, width), lambda i, _: (i, 0)),
                pl.BlockSpec((rows, block), lambda i, _: (0, i)),
                pl.BlockSpec((width, block), lambda i, _: (0, i)),
                whole_spec((parts, 2, run, rows)),
                tokens,
                tokens,
                whole_spec(root.shape),
                whole_spec(vectors.shape),
            ],
            out_specs=[
                half,
                half,
                fixed((rows, width)),
                fixed((rows, width)),
                pl.BlockSpec((1, block), lambda i, _: (0, i)),
                fixed((8, width)),
            ],
            scratch_shapes=[pltpu.VMEM((rows, width), F32), pltpu.VMEM((rows, block), BF16)],
        ),
        compiler_params=params(),
        cost_estimate=cost(6 * rows * width * ff, 4 * (width * ff + rows * ff) + 14 * rows * width),
        name="feed_forward_back",
    )(core1, df, down, slope, up, low_t.reshape(parts, 2, run, rows), dr2, unit, root, vectors)


def normed(values):
    centre = values - jnp.mean(values, axis=-1, keepdims=True)
    root = lax.rsqrt(jnp.mean(centre * centre, axis=-1, keepdims=True) + 1e-05)
    return centre * root, root


def norm_back(grad, unit, root, gain):
    scaled = grad * gain
    inner = jnp.mean(scaled * unit, axis=-1, keepdims=True)
    return root * (scaled - jnp.mean(scaled, axis=-1, keepdims=True) - unit * inner)


def transposed_rows(vectors):
    count, size = vectors.shape
    padded = jnp.concatenate([vectors, jnp.zeros((LANES - count, size), vectors.dtype)], axis=0)
    row = lax.broadcasted_iota(jnp.int32, (size, size), 0)
    column = lax.broadcasted_iota(jnp.int32, (size, size), 1)
    unit = (row == column).astype(F32).astype(BF16)
    return dot(unit, padded.astype(BF16), NT)


def folded(values, rows):
    size = values.shape[1]
    fold = size // rows
    row = lax.broadcasted_iota(jnp.int32, (rows, size), 0)
    at = lax.broadcasted_iota(jnp.int32, (rows, size), 1)
    spread = jnp.where(at // fold == row, values.astype(F32), 0.0).astype(BF16)
    column = lax.broadcasted_iota(jnp.int32, (LANES, size), 0)
    lane = lax.broadcasted_iota(jnp.int32, (LANES, size), 1)
    place = (column == SMALL - 4 + lane % fold).astype(F32).astype(BF16)
    return dot(spread, place, NT)


def pack_kernel(*refs):
    matrices, vectors, up_bias_ref, out_ref = refs[:4], refs[4:12], refs[12], refs[13]
    rows = out_ref.shape[1]
    for model in range(2):
        start = 0
        for matrix in matrices:
            out_ref[model, :, start : start + matrix.shape[2]] = matrix[model]
            start += matrix.shape[2]
        eight = jnp.concatenate([v[model : model + 1, :].astype(F32) for v in vectors], axis=0)
        small = transposed_rows(eight) + folded(up_bias_ref[model : model + 1, :].astype(F32), rows)
        out_ref[model, :, start:] = small.astype(BF16)


def pack(matrices, vectors, up_bias):
    models, rows, _ = matrices[0].shape
    lanes = sum(m.shape[2] for m in matrices) + LANES
    if rows % 8:
        parts = [v[..., None] for v in vectors] + [up_bias.reshape(models, rows, -1)]
        small = jnp.concatenate(parts, axis=-1)
        small = jnp.pad(small, [(0, 0), (0, 0), (0, LANES - small.shape[-1])])
        return jnp.concatenate(list(matrices) + [small], axis=-1)
    return pl.pallas_call(
        pack_kernel,
        out_shape=jax.ShapeDtypeStruct((models, rows, lanes), BF16),
        compiler_params=params(VMEM_MOST),
        name="pack_shard",
    )(*matrices, *vectors, up_bias)


def small_grads_kernel(down_ref, back_ref, bias_ref, qkv_ref, out_ref):
    rows = out_ref.shape[0]
    width = down_ref.shape[1]
    eight = jnp.concatenate(
        [
            qkv_ref[:, :width],
            qkv_ref[:, 2 * width :],
            back_ref[0:3, :],
            down_ref[0:3, :],
        ],
        axis=0,
    )
    out_ref[...] = transposed_rows(eight).astype(BF16)
    step = LANES
    fold = bias_ref.shape[1] // rows
    for start in range(0, rows, step):
        values = bias_ref[:, start * fold : (start + step) * fold]
        here = slice(start, start + step)
        out_ref[here, :] = (out_ref[here, :].astype(F32) + folded(values, step)).astype(BF16)


def small_grads(down_sums, back_sums, bias_sums, qkv_sums):
    width = down_sums.shape[1]
    return pl.pallas_call(
        small_grads_kernel,
        out_shape=jax.ShapeDtypeStruct((width, LANES), BF16),
        compiler_params=params(),
        name="small_gradients",
    )(down_sums, back_sums, bias_sums, qkv_sums)


class Ring:
    def __init__(self, count):
        depth = 4 if count % 4 == 0 else 2
        wide = count // depth
        order = []
        if wide > 1:
            for z in range(depth):
                ys = range(1, wide) if z % 2 == 0 else reversed(range(1, wide))
                order += [z * wide + y for y in ys]
            order += [z * wide for z in reversed(range(depth))]
        else:
            order = list(range(count))
        self.count, self.depth, self.wide = count, depth, wide
        self.long = count // 2
        self.short = count - 1 - self.long
        self.ahead, self.behind = [], []
        for core in range(2):
            sign = 1 if core == 0 else -1
            here = core * count
            for place, chip in enumerate(order):
                self.ahead.append((here + chip, here + order[(place + sign) % count]))
                self.behind.append((here + chip, here + order[(place - sign) % count]))

    def origins(self, core, chip):
        depth, turn = self.depth, self.wide - 1
        if turn == 0:
            place = chip
        else:
            z, y = lax.div(chip, self.wide), lax.rem(chip, self.wide)
            along = jnp.where(lax.rem(z, 2) == 0, y - 1, turn - y)
            place = jnp.where(y == 0, depth * turn + depth - 1 - z, z * turn + along)
        sign = 1 - 2 * core
        chips = []
        for k in range(self.count):
            off = -k if k <= self.long else k - self.long
            at = lax.rem(place + sign * off + self.count, self.count)
            if turn > 0:
                z, j = lax.div(at, turn), lax.rem(at, turn)
                y = jnp.where(lax.rem(z, 2) == 0, 1 + j, turn - j)
                at = jnp.where(
                    at < depth * turn, z * self.wide + y, (depth * (turn + 1) - 1 - at) * self.wide
                )
            chips.append(at)
        return chips

    def forth(self, block):
        return lax.ppermute(block, ("core", "f"), self.ahead)

    def back(self, block):
        return lax.ppermute(block, ("core", "f"), self.behind)


def swap(value, axis):
    return lax.ppermute(value, axis, SWAP)


def pick(value, index, axis):
    return lax.dynamic_index_in_dim(value, index, axis, keepdims=False)


def two_sides(own, other, side, groups):
    place = lax.broadcasted_iota(jnp.int32, (2, 1, 1), 0)
    block = jnp.where(place == side, own[None], other[None])
    if groups > 1:
        return lax.all_gather(block, "r", axis=0, tiled=False)
    return block[None]


class Gather:
    def __init__(self, ring, block):
        self.ring, self.step = ring, 0
        self.forth, self.back = [block], [block]
        self.theirs_forth, self.theirs_back = [swap(block, "core")], []

    def launch(self):
        self.step += 1
        sent = [self.ring.forth(self.forth[-1])]
        if self.step <= self.ring.short:
            sent.append(self.ring.back(self.back[-1]))
        return sent

    def now(self):
        return self.forth[-1]

    def land(self, sent):
        self.forth.append(sent[0])
        self.theirs_forth.append(swap(sent[0], "core"))
        if len(sent) > 1:
            self.back.append(sent[1])
            self.theirs_back.append(swap(sent[1], "core"))

    def blocks(self):
        return self.forth + self.back[1:], self.theirs_forth + self.theirs_back


class Scatter:
    def __init__(self, ring, own, other, origins):
        self.ring, self.step = ring, 0
        self.own, self.other, self.origins = own, other, origins
        self.far = self.term(ring.long).astype(BF16)
        self.near = self.term(ring.long + ring.short).astype(BF16)
        self.total = None

    def term(self, k):
        a, b = pick(self.own, self.origins[k], 2), pick(self.other, self.origins[k], 2)
        return a.astype(F32) + b.astype(F32)

    def launch(self):
        self.step += 1
        sent = [self.ring.back(self.far)]
        if self.step > self.ring.long - self.ring.short:
            sent.append(self.ring.forth(self.near))
        return sent

    def now(self):
        return self.far

    def land(self, sent):
        left = self.ring.long - self.step
        if left:
            self.far = (sent[0].astype(F32) + self.term(left)).astype(BF16)
            if len(sent) > 1:
                near = sent[1].astype(F32) + self.term(self.ring.long + left)
                self.near = near.astype(BF16)
        else:
            self.total = sent[0].astype(F32) + sent[1].astype(F32) + self.term(0)


def slot(movers, work=None):
    now = [m.now() for m in movers]
    sent = [m.launch() for m in movers]
    done = None
    if work is not None:
        done = work(now)
        sent, done = tie(sent, done)
    for mover, arrived in zip(movers, sent):
        mover.land(arrived)
    return done


def assemble_kernel(ring, with_vectors, at_ref, *refs):
    count = ring.count
    blocks, out_ref, sems = refs[: 2 * count], refs[2 * count], refs[-1]
    core, chip = at_ref[0], at_ref[1]
    here, there = ring.origins(core, chip), ring.origins(1 - core, chip)
    copies = []
    for i, (block, at) in enumerate(zip(blocks, here + there)):
        half = core if i < count else 1 - core
        for r in range(block.shape[0]):
            for x in range(2):
                copies.append(
                    pltpu.make_async_copy(
                        block.at[r, x], out_ref.at[r, x, half, at], sems.at[len(copies)]
                    )
                )
    for copy in copies:
        copy.start()
    for copy in copies:
        copy.wait()
    if with_vectors:
        rows = out_ref[:, :, :, :, :, out_ref.shape[-1] - LANES :]
        small = rows.astype(F32).reshape(-1, LANES)
        refs[2 * count + 1][...] = small.T[:16]


def assemble(ring, mine, theirs, core, with_vectors=False):
    groups, _, rows, lanes = mine[0].shape
    count = ring.count
    chip = lax.axis_index("f")
    shape = (groups, 2, 2, count, rows, lanes)
    width = shape[1] * shape[2] * groups * count * rows
    if rows % 8:
        whole = jnp.zeros(shape, BF16)
        at = ring.origins(core, chip) + ring.origins(1 - core, chip)
        for i, block in enumerate(mine + theirs):
            half = core if i < count else 1 - core
            where = (0, 0, half, at[i], 0, 0)
            whole = lax.dynamic_update_slice(whole, block[:, :, None, None], where)
        whole = whole.reshape(-1, lanes)
        return whole, (whole[:, lanes - LANES :].astype(F32).T[:16] if with_vectors else None)
    out_shape = [jax.ShapeDtypeStruct(shape, BF16)]
    if with_vectors:
        out_shape.append(jax.ShapeDtypeStruct((16, width), F32))
    out = pl.pallas_call(
        functools.partial(assemble_kernel, ring, with_vectors),
        out_shape=out_shape,
        in_specs=[pl.BlockSpec(memory_space=pltpu.SMEM)]
        + [pl.BlockSpec(memory_space=pl.ANY)] * (2 * count),
        scratch_shapes=[pltpu.SemaphoreType.DMA((4 * count * groups,))],
        compiler_params=params(VMEM_MOST),
        name="assemble",
    )(jnp.stack([core, chip]).astype(jnp.int32), *mine, *theirs)
    return out[0].reshape(-1, lanes), out[1] if with_vectors else None


def to_owners(total, side, groups):
    if groups > 1:
        total = lax.psum_scatter(total.astype(BF16), "r", scatter_dimension=0, tiled=True)
    total = total[0]
    own = pick(total, side, 0).astype(F32)
    other = swap(pick(total, 1 - side, 0).astype(BF16), "t").astype(F32)
    place = lax.broadcasted_iota(jnp.int32, (2, 1, 1), 0)
    return jnp.where(place == side, own[None], other[None])


def mixed_kernel(core_ref, left_ref, ctx_ref, dqkv_ref, da_ref, small_ref, send_ref, own_ref):
    at, core = pl.program_id(0), core_ref[0]

    @pl.when(at < 3)
    def _():
        halves_kernel(core, left_ref, dqkv_ref, send_ref, own_ref)

    @pl.when(at == 3)
    def _():
        halves_kernel(core, ctx_ref, da_ref, send_ref, own_ref)

    @pl.when(at == 4)
    def _():
        send_ref[:, :, :LANES] = small_ref[:, 1 - core]
        own_ref[:, :, :LANES] = small_ref[:, core]


def mixed_grad(rows_t, ctx_t, dqkv, da, small, core1, parts):
    size, tokens = rows_t.shape
    run = size // (2 * parts)
    width = da.shape[1]
    small = small.reshape(parts, 2, run, LANES)
    lanes = 4 * width + LANES
    if run % 16:
        full = [dot(rows_t, dqkv), dot(ctx_t, da)]
        full = [f.astype(BF16).reshape(parts, 2, run, -1) for f in full] + [small]
        full = jnp.concatenate(full, axis=-1)
        return pick(full, 1 - core1[0], 1), pick(full, core1[0], 1)
    left = whole_spec((parts, 2, run, tokens))
    half = pl.BlockSpec((parts, run, width), lambda j, _: (0, 0, j))
    return pl.pallas_call(
        mixed_kernel,
        out_shape=[jax.ShapeDtypeStruct((parts, run, lanes), BF16)] * 2,
        grid_spec=pltpu.PrefetchScalarGridSpec(
            num_scalar_prefetch=1,
            grid=(5,),
            in_specs=[
                left,
                left,
                pl.BlockSpec((tokens, width), lambda j, _: (0, jnp.minimum(j, 2))),
                whole_spec(da.shape),
                whole_spec(small.shape),
            ],
            out_specs=[half, half],
        ),
        compiler_params=params(),
        cost_estimate=cost(8 * size * tokens * width, 4 * size * tokens + 16 * tokens * width),
        name="attention_gradients",
    )(
        core1,
        rows_t.reshape(parts, 2, run, tokens),
        ctx_t.reshape(parts, 2, run, tokens),
        dqkv,
        da,
        small,
    )


def wide_kernel(core_ref, left_ref, right_ref, send_ref, own_ref):
    out = dot(left_ref[...], right_ref[...], TN).astype(BF16)

    @pl.when(pl.program_id(0) == 0)
    def _():
        send_ref[...] = out.reshape(send_ref.shape)

    @pl.when(pl.program_id(0) == 1)
    def _():
        own_ref[...] = out.reshape(own_ref.shape)


def wide_grad(left, right, core1, parts):
    tokens, size = left.shape
    run = size // (2 * parts)
    n = right.shape[1]
    if run % LANES:
        full = dot(left, right, TN).astype(BF16).reshape(parts, 2, run, n)
        return pick(full, 1 - core1[0], 1), pick(full, core1[0], 1)

    def columns(h, i, core_ref):
        return (0, 2 * i + jnp.where(h == 0, 1 - core_ref[0], core_ref[0]))

    return pl.pallas_call(
        wide_kernel,
        out_shape=[jax.ShapeDtypeStruct((parts, run, n), BF16)] * 2,
        grid_spec=pltpu.PrefetchScalarGridSpec(
            num_scalar_prefetch=1,
            grid=(2, parts),
            in_specs=[pl.BlockSpec((tokens, run), columns), whole_spec((tokens, n))],
            out_specs=[
                pl.BlockSpec((1, run, n), lambda h, i, _: (jnp.where(h == 0, i, parts - 1), 0, 0)),
                pl.BlockSpec((1, run, n), lambda h, i, _: (jnp.where(h == 0, 0, i), 0, 0)),
            ],
        ),
        compiler_params=params(),
        cost_estimate=cost(2 * size * tokens * n, 2 * (size * tokens + tokens * n + size * n)),
        name="down_gradient",
    )(core1, left, right)


def places(tags, model):
    member = tags[:, 0] == model
    count = member.shape[0]
    before = lax.broadcasted_iota(jnp.int32, (count, count), 0) < lax.broadcasted_iota(
        jnp.int32, (count, count), 1
    )
    ranking = jnp.sum(jnp.where(before & member[:, None], 1, 0), axis=0)
    slots = lax.broadcasted_iota(jnp.int32, (CAP, count), 0)
    return (slots == ranking[None, :]) & member[None, :]


def route(chosen, chains):
    marked = jnp.where(chosen[:, :, None, None], chains[None], jnp.zeros((), chains.dtype))
    return jnp.sum(marked.astype(F32), axis=1).astype(chains.dtype)


def body(ring, groups, *args):
    (
        inputs,
        cotangent,
        lengths,
        tags,
        query_weight,
        query_bias,
        key_weight,
        value_weight,
        value_bias,
        output_projection_weight,
        out_bias,
        first_gain,
        first_shift,
        up_weight,
        up_bias,
        down_weight,
        down_bias,
        second_gain,
        second_shift,
    ) = args
    side, core = lax.axis_index("t"), lax.axis_index("core")
    core1 = core.astype(jnp.int32)[None]
    chains = lengths.shape[0]
    width = inputs.shape[1]
    ff = up_weight.shape[2]
    slots = inputs.shape[0] // chains
    tokens = 2 * CAP * slots
    parts = 2 * groups

    shard_a = pack(
        (query_weight, key_weight, value_weight, output_projection_weight),
        (
            query_bias,
            value_bias,
            out_bias,
            first_gain,
            first_shift,
            down_bias,
            second_gain,
            second_shift,
        ),
        up_bias,
    )
    block_a = two_sides(
        pick(shard_a, side, 0), swap(pick(shard_a, 1 - side, 0), "t"), side, groups
    )

    own_places, other_places = places(tags, side), places(tags, 1 - side)
    own_len = jnp.sum(jnp.where(own_places, lengths[None, :], 0), axis=1)
    other_len = jnp.sum(jnp.where(other_places, lengths[None, :], 0), axis=1)
    chain_rows = inputs.reshape(chains, slots, width)
    sent_lens = jnp.broadcast_to(other_len[:, None, None], (CAP, 16, width)).astype(BF16)
    sent = jnp.concatenate([route(other_places, chain_rows), sent_lens], axis=1)

    def exchanged(weight):
        return swap(pick(weight, 1 - side, 0), "t")

    def joined(weight, arrived):
        return two_sides(pick(weight, side, 0), arrived, side, groups)

    ring_a = Gather(ring, block_a)

    def work_exchange_up(now):
        return exchanged(tie(now, up_weight)[1])

    arrived = slot([ring_a], work_exchange_up)
    ring_u = Gather(ring, joined(up_weight, arrived))
    message = swap(slot([ring_a], lambda now: tie(now, sent)[1]), "t")

    def take_rows(now):
        return message, exchanged(tie(now, down_weight)[1])

    message, arrived = slot([ring_a, ring_u], take_rows)

    def make_rows(now):
        _, got, down, cots = tie(now, message, arrived, cotangent)
        rows = jnp.concatenate([route(own_places, chain_rows), got[:, :slots]], axis=0)
        lens = jnp.concatenate([own_len, got[:, slots, 0].astype(jnp.int32)])
        cots = cots.reshape(chains, slots, width)
        return rows.reshape(tokens, width), lens, down, route(other_places, cots), cots

    rows_in, lens, arrived, other_cot, cot_rows = slot([ring_a, ring_u], make_rows)
    other_cot = swap(other_cot, "t")
    ring_d = Gather(ring, joined(down_weight, arrived))
    for _ in range(ring.long - 4):
        slot([ring_a, ring_u, ring_d])

    def join_attention(now):
        _, blocks = tie(now, ring_a.blocks())
        return assemble(ring, *blocks, core, True)

    whole_a, vectors = slot([ring_u, ring_d], join_attention)

    def do_attention(now):
        _, whole = tie(now, whole_a)
        return attention(rows_in, lens, whole, vectors)

    qkv, unit1, root1, low1, rows_t, ctx_t, low_t = slot([ring_u, ring_d], do_attention)

    def join_up(now):
        _, blocks = tie(now, ring_u.blocks())
        return assemble(ring, *blocks, core)[0]

    whole_u = slot([ring_d], join_up)

    def do_up(now):
        _, whole, other = tie(now, whole_u, other_cot)
        cot = jnp.concatenate([route(own_places, cot_rows), other], axis=0)
        return (cot.reshape(tokens, width),) + tuple(up_and_gelu(low1, whole, whole_a))

    cot, active, slope = slot([ring_d], do_up)
    whole_d, _ = assemble(ring, *ring_d.blocks(), core)
    gain1 = vectors[3:4]

    result, dr2, df, down_sums = down_and_norm(active, whole_d, unit1, cot, vectors)

    origins = ring.origins(core, lax.axis_index("f"))

    def blocks_of(half):
        return half.reshape(groups, 2, ring.count, -1, half.shape[-1])

    def scatter(own, arrived):
        return Scatter(ring, blocks_of(own), blocks_of(arrived), origins)

    send_d, own_d = wide_grad(active, df, core1, parts)
    arrived_d = swap(send_d, "core")
    df_now, send_d = tie(df, send_d)
    send_u, own_u, dr1, da, bias_sums, back_sums = feed_back(
        df_now, whole_d, slope, whole_u, low_t, dr2, unit1, root1, vectors, core1, parts
    )
    arrived_d, send_u = tie(arrived_d, send_u)
    ring_d = scatter(own_d, arrived_d)
    arrived_u = swap(send_u, "core")

    def back_first(now):
        _, da_now = tie(now, da)
        return attention_back(qkv, da_now, whole_a, lens, 0, CAP), arrived_u

    (dqkv, sums_1), arrived_u = slot([ring_d], back_first)
    ring_u = scatter(own_u, arrived_u)

    def back_second(now):
        _, da_now, out_rows = tie(now, da, result.reshape(2, CAP, slots, width)[1])
        return attention_back(qkv, da_now, whole_a, lens, CAP, CAP, dqkv), out_rows

    (dqkv, sums_2), out_rows = slot([ring_d, ring_u], back_second)
    back_out = swap(out_rows, "t")

    def attention_grads(now):
        _, dqkv_now = tie(now, dqkv)
        small = small_grads(down_sums, back_sums, bias_sums, sums_1 + sums_2)
        return mixed_grad(rows_t, ctx_t, dqkv_now, da, small, core1, parts)

    send_a, own_a = slot([ring_d, ring_u], attention_grads)
    arrived_a = swap(send_a, "core")

    def second_half(values):
        return values.reshape(2, CAP, slots, width)[1]

    def home(values, back):
        both = jnp.concatenate([values.reshape(2, CAP, slots, width)[0], back], axis=0)
        return route(jnp.concatenate([own_places, other_places], axis=0).T, both).reshape(-1, width)

    def do_rows(now):
        _, dq = tie(now, dqkv)
        return (dr1 + dot(dq, whole_a[:, : 3 * width], NT)).astype(BF16), arrived_a

    rows_grad_in, arrived_a = slot([ring_d, ring_u], do_rows)
    for _ in range(ring.long - 4):
        slot([ring_d, ring_u])
    ring_a = scatter(own_a, arrived_a)

    def owners_d(now):
        _, total = tie(now, ring_d.total)
        return to_owners(total, side, groups)

    grads_d = slot([ring_u, ring_a], owners_d)

    def outputs(now):
        _, values = tie(now, result)
        return home(values, back_out)

    def owners_u(now):
        _, total = tie(now, ring_u.total)
        return to_owners(total, side, groups), second_half(tie(now, rows_grad_in)[1])

    grads_u, back_rows = slot([ring_a], owners_u)
    back_rows = swap(back_rows, "t")
    output = slot([ring_a], outputs)
    input_grad = slot([ring_a], lambda now: home(rows_grad_in, back_rows))
    for _ in range(ring.long - 4):
        slot([ring_a])

    grads_a = to_owners(ring_a.total, side, groups)
    columns = jnp.swapaxes(grads_a[:, :, 4 * width : 4 * width + 16], 1, 2)
    return (
        output,
        input_grad,
        grads_a[:, :, :width],
        columns[:, 0],
        grads_a[:, :, width : 2 * width],
        grads_a[:, :, 2 * width : 3 * width],
        columns[:, 1],
        grads_a[:, :, 3 * width : 4 * width],
        columns[:, 2],
        columns[:, 3],
        columns[:, 4],
        grads_u,
        jnp.swapaxes(columns[:, 8:12], 1, 2).reshape(2, -1),
        grads_d,
        columns[:, 5],
        columns[:, 6],
        columns[:, 7],
    )


def solution(mesh):
    dp, fsdp = mesh.shape["dp"], mesh.shape["fsdp"]
    groups = dp // 4
    inner = Mesh(mesh.devices.reshape(groups, 2, 2, fsdp), ("r", "t", "core", "f"))
    every = ("r", "t", "core", "f")
    rows, vector, matrix = P(every, None), P(None, every), P(None, every, None)
    weights = (
        matrix,
        vector,
        matrix,
        matrix,
        vector,
        matrix,
        vector,
        vector,
        vector,
        matrix,
        vector,
        matrix,
        vector,
        vector,
        vector,
    )
    return jax.shard_map(
        functools.partial(body, Ring(fsdp), groups),
        mesh=inner,
        in_specs=(rows, rows, P(every), rows) + weights,
        out_specs=(rows, rows) + weights,
        check_vma=False,
    )
```

```python
import functools

import jax
import jax.numpy as jnp
import numpy as np
from jax import lax
from jax.experimental import pallas as pl
from jax.experimental.pallas import tpu as pltpu
from jax.sharding import Mesh
from jax.sharding import PartitionSpec as P

HEADS = 12
HEAD_DIM = 64
CAP = 3
MIN_LEN = 96
LANES = 128
BF16 = jnp.bfloat16
F32 = jnp.float32
NN = (((1,), (0,)), ((), ()))
NT = (((1,), (1,)), ((), ()))
TN = (((0,), (0,)), ((), ()))
SWAP = [(0, 1), (1, 0)]
VMEM_LIMIT = 56 * 2**20
VMEM_MOST = 56 * 2**20
SMALL = 12


def dot(a, b, dims=NN):
    return lax.dot_general(a, b, dims, preferred_element_type=F32)


def tie(*values):
    return lax.optimization_barrier(values)


def params(limit=VMEM_LIMIT):
    return pltpu.CompilerParams(vmem_limit_bytes=limit)


def taking(micros):
    return pl.CostEstimate(flops=int(micros * 1.1e9), bytes_accessed=1, transcendentals=0)


def whole_spec(shape):
    return pl.BlockSpec(shape, lambda *_: (0,) * len(shape), pipeline_mode=pl.Buffered(1))


def fixed(shape):
    return pl.BlockSpec(shape, lambda *_: (0,) * len(shape))


def head_masks(value=1.0):
    lane = lax.broadcasted_iota(jnp.int32, (1, LANES), 1)
    first = jnp.where(lane < HEAD_DIM, value, 0.0).astype(BF16)
    second = jnp.where(lane >= HEAD_DIM, value, 0.0).astype(BF16)
    return first, second


def stacked(two_heads, masks):
    return jnp.concatenate([two_heads * masks[0], two_heads * masks[1]], axis=0)


def side_by_side(rows):
    half = rows.shape[0] // 2
    return jnp.concatenate([rows[:half], rows[half:]], axis=1)


def pair_probs(k_stack, q_pair, length):
    scores = dot(k_stack, q_pair, NT)
    keys = k_stack.shape[0] // 2
    scores = scores.reshape(2, keys, scores.shape[1])
    always = scores[:, :MIN_LEN]
    rest = scores[:, MIN_LEN:]
    slot = lax.broadcasted_iota(jnp.int32, rest.shape, 1) + MIN_LEN
    rest = jnp.where(slot < length, rest, -1000000000.0)
    scores = jnp.concatenate([always, rest], axis=1)
    exponent = jnp.exp(scores - jnp.max(scores, axis=1, keepdims=True))
    return exponent * (1.0 / jnp.sum(exponent, axis=1, keepdims=True))


def attention_rows(length, qkv_ref, ctx_ref, base, rows, width):
    masks, scaled = head_masks(), head_masks(HEAD_DIM**-0.5)
    at = slice(base, base + rows)
    for start in range(0, width, LANES):
        q_pair = qkv_ref[at, start : start + LANES]
        k_stack = stacked(qkv_ref[at, width + start : width + start + LANES], scaled)
        v_stack = stacked(qkv_ref[at, 2 * width + start : 2 * width + start + LANES], masks)
        probs = pair_probs(k_stack, q_pair, length)
        low = probs.astype(BF16).reshape(k_stack.shape[0], q_pair.shape[0])
        ctx_ref[at, start : start + LANES] = dot(low, v_stack, TN).astype(BF16)


def attention_kernel(
    lens_ref,
    rows_ref,
    weight_ref,
    vec_ref,
    qkv_ref,
    unit_ref,
    root_ref,
    low_ref,
    rows_t_ref,
    ctx_t_ref,
    low_t_ref,
    ctx_ref,
):
    width = ctx_ref.shape[1]
    rows_t_ref[...] = rows_ref[...].T
    rows = qkv_ref.shape[0] // 2
    for part in range(3):
        columns = slice(part * width, (part + 1) * width)
        product = dot(rows_ref[...], weight_ref[:, columns])
        if part != 1:
            product = product + vec_ref[part // 2 : part // 2 + 1, :]
        qkv_ref[:, columns] = product.astype(BF16)
    for chain in range(2):
        length = lens_ref[2 * pl.program_id(0) + chain]
        attention_rows(length, qkv_ref, ctx_ref, chain * rows, rows, width)
    branch = dot(ctx_ref[...], weight_ref[:, 3 * width : 4 * width]) + vec_ref[2:3, :]
    unit, root = normed(rows_ref[...].astype(F32) + branch)
    unit_ref[...] = unit
    root_ref[...] = root
    low = (unit * vec_ref[3:4, :] + vec_ref[4:5, :]).astype(BF16)
    low_ref[...] = low
    low_t_ref[...] = low.T
    ctx_t_ref[...] = ctx_ref[...].T


def attention(rows_in, lens, whole_a, vectors):
    total, width = rows_in.shape
    rows = 2 * total // lens.shape[0]

    def tokens(lanes):
        return pl.BlockSpec((rows, lanes), lambda i, _: (i, 0))

    return pl.pallas_call(
        attention_kernel,
        out_shape=[
            jax.ShapeDtypeStruct((total, 3 * width), BF16),
            jax.ShapeDtypeStruct((total, width), F32),
            jax.ShapeDtypeStruct((total, 1), F32),
            jax.ShapeDtypeStruct((total, width), BF16),
        ]
        + [jax.ShapeDtypeStruct((width, total), BF16)] * 3,
        grid_spec=pltpu.PrefetchScalarGridSpec(
            num_scalar_prefetch=1,
            grid=(total // rows,),
            in_specs=[tokens(width), whole_spec(whole_a.shape), whole_spec(vectors.shape)],
            out_specs=[tokens(3 * width), tokens(width), tokens(1), tokens(width)]
            + [pl.BlockSpec((width, rows), lambda i, _: (0, i))] * 3,
            scratch_shapes=[pltpu.VMEM((rows, width), BF16)],
        ),
        compiler_params=params(20 * 2**20),
        cost_estimate=taking(14),
        name="attention_forward",
    )(lens, rows_in, whole_a, vectors)


def attention_back_kernel(lens_ref, *refs):
    qkv_ref, da_ref, out_weight_ref = refs[:3]
    dqkv_ref, sum_ref = refs[-2:]
    width = da_ref.shape[1]
    length = lens_ref[pl.program_id(0)]
    masks, scaled = head_masks(), head_masks(HEAD_DIM**-0.5)
    dctx = dot(da_ref[...], out_weight_ref[...], NT).astype(BF16)

    @pl.when(pl.program_id(0) == 0)
    def _():
        sum_ref[...] = jnp.zeros_like(sum_ref)

    def store(column, value):
        low = value.astype(BF16)
        dqkv_ref[:, column : column + LANES] = low
        sum_ref[:, column : column + LANES] += jnp.sum(low.astype(F32), axis=0, keepdims=True)

    for start in range(0, width, LANES):
        q_pair = qkv_ref[:, start : start + LANES]
        k_stack = stacked(qkv_ref[:, width + start : width + start + LANES], scaled)
        v_stack = stacked(qkv_ref[:, 2 * width + start : 2 * width + start + LANES], masks)
        d_pair = dctx[:, start : start + LANES]
        probs = pair_probs(k_stack, q_pair, length)
        low = probs.astype(BF16).reshape(k_stack.shape[0], q_pair.shape[0])
        dprobs = dot(v_stack, d_pair, NT).reshape(probs.shape)
        inner = jnp.sum(dprobs * probs, axis=1, keepdims=True)
        dscores = (probs * (dprobs - inner)).astype(BF16).reshape(low.shape)
        store(start, dot(dscores, k_stack, TN))
        store(width + start, dot(side_by_side(dscores), stacked(q_pair, scaled)))
        store(2 * width + start, dot(side_by_side(low), stacked(d_pair, masks)))


def attention_back(qkv, da, out_weight, lens, first, count, before=None):
    total, width = da.shape
    rows = total // lens.shape[0]
    extra = [] if before is None else [before]
    return pl.pallas_call(
        attention_back_kernel,
        out_shape=[
            jax.ShapeDtypeStruct((total, 3 * width), BF16),
            jax.ShapeDtypeStruct((1, 3 * width), F32),
        ],
        grid_spec=pltpu.PrefetchScalarGridSpec(
            num_scalar_prefetch=1,
            grid=(count,),
            in_specs=[
                pl.BlockSpec((rows, 3 * width), lambda i, _: (i + first, 0)),
                pl.BlockSpec((rows, width), lambda i, _: (i + first, 0)),
                whole_spec((width, width)),
            ]
            + [pl.BlockSpec(memory_space=pl.ANY)] * len(extra),
            out_specs=[
                pl.BlockSpec((rows, 3 * width), lambda i, _: (i + first, 0)),
                pl.BlockSpec((1, 3 * width), lambda i, _: (0, 0)),
            ],
        ),
        input_output_aliases={4: 0} if extra else {},
        compiler_params=params(12 * 2**20),
        cost_estimate=taking(11),
        name="attention_backward",
    )(lax.slice_in_dim(lens, first, first + count), qkv, da, out_weight, *extra)


def up_kernel(low_ref, up_ref, small_ref, active_ref, slope_ref):
    weight = up_ref[...]
    block = weight.shape[1]
    rows = small_ref.shape[0]
    fold = block // rows
    column = lax.broadcasted_iota(jnp.int32, (LANES, block), 0)
    lane = lax.broadcasted_iota(jnp.int32, (LANES, block), 1)
    spread = (column == SMALL - 4 + lane % fold).astype(F32).astype(BF16)
    row = lax.broadcasted_iota(jnp.int32, (rows, block), 0)
    at = lax.broadcasted_iota(jnp.int32, (rows, block), 1)
    bias = jnp.sum(
        jnp.where(at // fold == row, dot(small_ref[...], spread), 0.0), axis=0, keepdims=True
    )
    step = LANES
    for start in range(0, low_ref.shape[0], step):
        hidden = dot(low_ref[start : start + step, :], weight) + bias
        cdf = 0.5 * (1.0 + lax.erf(hidden * (2.0**-0.5)))
        active_ref[start : start + step, :] = (hidden * cdf).astype(BF16)
        density = jnp.exp(-0.5 * hidden * hidden) * ((2.0 * np.pi) ** -0.5)
        slope_ref[start : start + step, :] = (cdf + hidden * density).astype(BF16)


def up_and_gelu(low, up, whole_a):
    rows, width = low.shape
    ff = up.shape[1]
    block = 512
    return pl.pallas_call(
        up_kernel,
        out_shape=[jax.ShapeDtypeStruct((rows, ff), BF16)] * 2,
        grid=(ff // block,),
        in_specs=[
            whole_spec((rows, width)),
            pl.BlockSpec((width, block), lambda i: (0, i)),
            pl.BlockSpec(
                (width * block // ff, LANES), lambda i: (i, whole_a.shape[1] // LANES - 1)
            ),
        ],
        out_specs=[pl.BlockSpec((rows, block), lambda i: (0, i))] * 2,
        cost_estimate=taking(10),
        compiler_params=params(12 * 2**20),
        name="up_gelu",
    )(low, up, whole_a)


def down_kernel(
    active_ref, down_ref, unit_ref, cot_ref, vec_ref, out_ref, dr2_ref, df_ref, sum_ref
):
    @pl.when(pl.program_id(0) == 0)
    def _():
        sum_ref[...] = jnp.zeros_like(sum_ref)

    bias, gain, shift = vec_ref[5:6, :], vec_ref[6:7, :], vec_ref[7:8, :]
    hidden = unit_ref[...] * vec_ref[3:4, :] + vec_ref[4:5, :]
    total = hidden + dot(active_ref[...], down_ref[...]) + bias
    unit, root = normed(total)
    out_ref[...] = (unit * gain + shift).astype(BF16)
    grad = cot_ref[...].astype(F32)
    dr2 = norm_back(grad, unit, root, gain)
    dr2_ref[...] = dr2
    df = dr2.astype(BF16)
    df_ref[...] = df
    sum_ref[0:1, :] += jnp.sum(df.astype(F32), axis=0, keepdims=True)
    sum_ref[1:2, :] += jnp.sum(grad * unit, axis=0, keepdims=True)
    sum_ref[2:3, :] += jnp.sum(grad, axis=0, keepdims=True)


def down_and_norm(active, down, unit, cot, vectors):
    rows, ff = active.shape
    width = down.shape[1]
    block = 256
    tokens = pl.BlockSpec((block, width), lambda i: (i, 0))
    return pl.pallas_call(
        down_kernel,
        out_shape=[
            jax.ShapeDtypeStruct((rows, width), BF16),
            jax.ShapeDtypeStruct((rows, width), F32),
            jax.ShapeDtypeStruct((rows, width), BF16),
            jax.ShapeDtypeStruct((8, width), F32),
        ],
        grid=(rows // block,),
        in_specs=[
            pl.BlockSpec((block, ff), lambda i: (i, 0)),
            whole_spec((ff, width)),
            tokens,
            tokens,
            whole_spec(vectors.shape),
        ],
        out_specs=[tokens, tokens, tokens, fixed((8, width))],
        compiler_params=params(18 * 2**20),
        cost_estimate=taking(10),
        name="down_norm",
    )(active, down, unit, cot, vectors)


def back_kernel(
    core_ref,
    df_ref,
    down_ref,
    slope_ref,
    up_ref,
    low_t_ref,
    dr2_ref,
    unit_ref,
    root_ref,
    vec_ref,
    send_ref,
    own_ref,
    dr1_ref,
    da_ref,
    bias_ref,
    sum_ref,
    total,
    grad,
):
    at = pl.program_id(0)
    step = 384

    @pl.when(at == 0)
    def _():
        total[...] = dr2_ref[...]
        sum_ref[...] = jnp.zeros_like(sum_ref)

    bias = jnp.zeros(bias_ref.shape, F32)
    for start in range(0, df_ref.shape[0], step):
        rows = slice(start, start + step)
        du = dot(df_ref[rows, :], down_ref[...], NT) * slope_ref[rows, :].astype(F32)
        du = du.astype(BF16)
        grad[rows, :] = du
        bias += jnp.sum(du.astype(F32), axis=0, keepdims=True)
        total[rows, :] += dot(du, up_ref[...], NT)
    bias_ref[...] = bias
    halves_kernel(core_ref[0], low_t_ref, grad, send_ref, own_ref)

    @pl.when(at == pl.num_programs(0) - 1)
    def _():
        for start in range(0, df_ref.shape[0], step):
            rows = slice(start, start + step)
            dh1, unit = total[rows, :], unit_ref[rows, :]
            dr1 = norm_back(dh1, unit, root_ref[rows, :], vec_ref[3:4, :])
            dr1_ref[rows, :] = dr1
            da = dr1.astype(BF16)
            da_ref[rows, :] = da
            sum_ref[0:1, :] += jnp.sum(da.astype(F32), axis=0, keepdims=True)
            sum_ref[1:2, :] += jnp.sum(dh1 * unit, axis=0, keepdims=True)
            sum_ref[2:3, :] += jnp.sum(dh1, axis=0, keepdims=True)


def halves_kernel(core, left_ref, right_ref, send_ref, own_ref):
    parts, _, run, tokens = left_ref.shape
    for half, out_ref in ((1 - core, send_ref), (core, own_ref)):
        left = left_ref[:, half].reshape(parts * run, tokens)
        out_ref[...] = dot(left, right_ref[...]).astype(BF16).reshape(out_ref.shape)


def feed_back(df, down, slope, up, low_t, dr2, unit, root, vectors, core1, parts):
    rows, width = df.shape
    ff = up.shape[1]
    block = 768
    run = width // (2 * parts)
    tokens = whole_spec((rows, width))
    half = pl.BlockSpec((parts, run, block), lambda i, _: (0, 0, i))
    return pl.pallas_call(
        back_kernel,
        out_shape=[
            jax.ShapeDtypeStruct((parts, run, ff), BF16),
            jax.ShapeDtypeStruct((parts, run, ff), BF16),
            jax.ShapeDtypeStruct((rows, width), F32),
            jax.ShapeDtypeStruct((rows, width), BF16),
            jax.ShapeDtypeStruct((1, ff), F32),
            jax.ShapeDtypeStruct((8, width), F32),
        ],
        grid_spec=pltpu.PrefetchScalarGridSpec(
            num_scalar_prefetch=1,
            grid=(ff // block,),
            in_specs=[
                tokens,
                pl.BlockSpec((block, width), lambda i, _: (i, 0)),
                pl.BlockSpec((rows, block), lambda i, _: (0, i)),
                pl.BlockSpec((width, block), lambda i, _: (0, i)),
                whole_spec((parts, 2, run, rows)),
                tokens,
                tokens,
                whole_spec(root.shape),
                whole_spec(vectors.shape),
            ],
            out_specs=[
                half,
                half,
                fixed((rows, width)),
                fixed((rows, width)),
                pl.BlockSpec((1, block), lambda i, _: (0, i)),
                fixed((8, width)),
            ],
            scratch_shapes=[pltpu.VMEM((rows, width), F32), pltpu.VMEM((rows, block), BF16)],
        ),
        compiler_params=params(30 * 2**20),
        cost_estimate=taking(21),
        name="feed_forward_back",
    )(core1, df, down, slope, up, low_t.reshape(parts, 2, run, rows), dr2, unit, root, vectors)


def normed(values):
    centre = values - jnp.mean(values, axis=-1, keepdims=True)
    root = lax.rsqrt(jnp.mean(centre * centre, axis=-1, keepdims=True) + 1e-05)
    return centre * root, root


def norm_back(grad, unit, root, gain):
    scaled = grad * gain
    inner = jnp.mean(scaled * unit, axis=-1, keepdims=True)
    return root * (scaled - jnp.mean(scaled, axis=-1, keepdims=True) - unit * inner)


def transposed_rows(vectors):
    count, size = vectors.shape
    padded = jnp.concatenate([vectors, jnp.zeros((LANES - count, size), vectors.dtype)], axis=0)
    row = lax.broadcasted_iota(jnp.int32, (size, size), 0)
    column = lax.broadcasted_iota(jnp.int32, (size, size), 1)
    unit = (row == column).astype(F32).astype(BF16)
    return dot(unit, padded.astype(BF16), NT)


def folded(values, rows):
    size = values.shape[1]
    fold = size // rows
    row = lax.broadcasted_iota(jnp.int32, (rows, size), 0)
    at = lax.broadcasted_iota(jnp.int32, (rows, size), 1)
    spread = jnp.where(at // fold == row, values.astype(F32), 0.0).astype(BF16)
    column = lax.broadcasted_iota(jnp.int32, (LANES, size), 0)
    lane = lax.broadcasted_iota(jnp.int32, (LANES, size), 1)
    place = (column == SMALL - 4 + lane % fold).astype(F32).astype(BF16)
    return dot(spread, place, NT)


def pack_kernel(*refs):
    matrices, vectors, up_bias_ref, out_ref = refs[:4], refs[4:12], refs[12], refs[13]
    rows = out_ref.shape[1]
    for model in range(2):
        start = 0
        for matrix in matrices:
            out_ref[model, :, start : start + matrix.shape[2]] = matrix[model]
            start += matrix.shape[2]
        eight = jnp.concatenate([v[model : model + 1, :].astype(F32) for v in vectors], axis=0)
        small = transposed_rows(eight) + folded(up_bias_ref[model : model + 1, :].astype(F32), rows)
        out_ref[model, :, start:] = small.astype(BF16)


def pack(matrices, vectors, up_bias):
    models, rows, _ = matrices[0].shape
    lanes = sum(m.shape[2] for m in matrices) + LANES
    if rows % 8:
        parts = [v[..., None] for v in vectors] + [up_bias.reshape(models, rows, -1)]
        small = jnp.concatenate(parts, axis=-1)
        small = jnp.pad(small, [(0, 0), (0, 0), (0, LANES - small.shape[-1])])
        return jnp.concatenate(list(matrices) + [small], axis=-1)
    return pl.pallas_call(
        pack_kernel,
        out_shape=jax.ShapeDtypeStruct((models, rows, lanes), BF16),
        compiler_params=params(VMEM_MOST),
        name="pack_shard",
    )(*matrices, *vectors, up_bias)


def small_grads_kernel(down_ref, back_ref, bias_ref, qkv_ref, out_ref):
    rows = out_ref.shape[0]
    width = down_ref.shape[1]
    eight = jnp.concatenate(
        [
            qkv_ref[:, :width],
            qkv_ref[:, 2 * width :],
            back_ref[0:3, :],
            down_ref[0:3, :],
        ],
        axis=0,
    )
    out_ref[...] = transposed_rows(eight).astype(BF16)
    step = LANES
    fold = bias_ref.shape[1] // rows
    for start in range(0, rows, step):
        values = bias_ref[:, start * fold : (start + step) * fold]
        here = slice(start, start + step)
        out_ref[here, :] = (out_ref[here, :].astype(F32) + folded(values, step)).astype(BF16)


def small_grads(down_sums, back_sums, bias_sums, qkv_sums):
    width = down_sums.shape[1]
    return pl.pallas_call(
        small_grads_kernel,
        out_shape=jax.ShapeDtypeStruct((width, LANES), BF16),
        compiler_params=params(8 * 2**20),
        name="small_gradients",
    )(down_sums, back_sums, bias_sums, qkv_sums)


class Ring:
    def __init__(self, count):
        depth = 4 if count % 4 == 0 else 2
        wide = count // depth
        order = []
        if wide > 1:
            for z in range(depth):
                ys = range(1, wide) if z % 2 == 0 else reversed(range(1, wide))
                order += [z * wide + y for y in ys]
            order += [z * wide for z in reversed(range(depth))]
        else:
            order = list(range(count))
        self.count, self.depth, self.wide = count, depth, wide
        self.long = count // 2
        self.short = count - 1 - self.long
        self.ahead, self.behind = [], []
        for core in range(2):
            sign = 1 if core == 0 else -1
            here = core * count
            for place, chip in enumerate(order):
                self.ahead.append((here + chip, here + order[(place + sign) % count]))
                self.behind.append((here + chip, here + order[(place - sign) % count]))

    def origins(self, core, chip):
        depth, turn = self.depth, self.wide - 1
        if turn == 0:
            place = chip
        else:
            z, y = lax.div(chip, self.wide), lax.rem(chip, self.wide)
            along = jnp.where(lax.rem(z, 2) == 0, y - 1, turn - y)
            place = jnp.where(y == 0, depth * turn + depth - 1 - z, z * turn + along)
        sign = 1 - 2 * core
        chips = []
        for k in range(self.count):
            off = -k if k <= self.long else k - self.long
            at = lax.rem(place + sign * off + self.count, self.count)
            if turn > 0:
                z, j = lax.div(at, turn), lax.rem(at, turn)
                y = jnp.where(lax.rem(z, 2) == 0, 1 + j, turn - j)
                at = jnp.where(
                    at < depth * turn, z * self.wide + y, (depth * (turn + 1) - 1 - at) * self.wide
                )
            chips.append(at)
        return chips

    def forth(self, block):
        return lax.ppermute(block, ("core", "f"), self.ahead)

    def back(self, block):
        return lax.ppermute(block, ("core", "f"), self.behind)


def swap(value, axis):
    return lax.ppermute(value, axis, SWAP)


def pick(value, index, axis):
    return lax.dynamic_index_in_dim(value, index, axis, keepdims=False)


def two_sides(own, other, side, groups):
    place = lax.broadcasted_iota(jnp.int32, (2, 1, 1), 0)
    block = jnp.where(place == side, own[None], other[None])
    if groups > 1:
        return lax.all_gather(block, "r", axis=0, tiled=False)
    return block[None]


class Gather:
    def __init__(self, ring, block):
        self.ring, self.step = ring, 0
        self.forth, self.back = [block], [block]
        self.theirs_forth, self.theirs_back = [swap(block, "core")], []

    def launch(self):
        self.step += 1
        sent = [self.ring.forth(self.forth[-1])]
        if self.step <= self.ring.short:
            sent.append(self.ring.back(self.back[-1]))
        return sent

    def now(self):
        return self.forth[-1]

    def land(self, sent):
        self.forth.append(sent[0])
        self.theirs_forth.append(swap(sent[0], "core"))
        if len(sent) > 1:
            self.back.append(sent[1])
            self.theirs_back.append(swap(sent[1], "core"))

    def settle(self, values):
        for kept, value in zip((self.theirs_forth, self.theirs_back), values):
            kept[:] = value

    def blocks(self):
        return self.forth + self.back[1:], self.theirs_forth + self.theirs_back


class Scatter:
    def __init__(self, ring, own, other, origins):
        self.ring, self.step = ring, 0
        self.own, self.other, self.origins = own, other, origins
        self.far = self.term(ring.long).astype(BF16)
        self.near = self.term(ring.long + ring.short).astype(BF16)
        self.total = None

    def term(self, k):
        a, b = pick(self.own, self.origins[k], 2), pick(self.other, self.origins[k], 2)
        return a.astype(F32) + b.astype(F32)

    def launch(self):
        self.step += 1
        sent = [self.ring.back(self.far)]
        if self.step > self.ring.long - self.ring.short:
            sent.append(self.ring.forth(self.near))
        return sent

    def now(self):
        return self.far

    def land(self, sent):
        left = self.ring.long - self.step
        if left:
            self.far = (sent[0].astype(F32) + self.term(left)).astype(BF16)
            if len(sent) > 1:
                near = sent[1].astype(F32) + self.term(self.ring.long + left)
                self.near = near.astype(BF16)
        else:
            self.total = sent[0].astype(F32) + sent[1].astype(F32) + self.term(0)


class Trip:
    def __init__(self, value, axis):
        self.value, self.axis, self.got = value, axis, None

    def launch(self):
        return [swap(self.value, self.axis)]

    def now(self):
        return self.value

    def land(self, sent):
        self.got = sent[0]


def slot(movers, work=None):
    now = [m.now() for m in movers]
    sent = [m.launch() for m in movers]
    gathers = [m for m in movers if isinstance(m, Gather)]
    before = [(m.theirs_forth, m.theirs_back) for m in gathers]
    done = None if work is None else work((now, before))
    sent, done, before = tie(sent, done, before)
    for mover, settled in zip(gathers, before):
        mover.settle(settled)
    for mover, arrived in zip(movers, sent):
        mover.land(arrived)
    return done


def assemble_kernel(ring, with_vectors, at_ref, *refs):
    count = ring.count
    blocks, out_ref = refs[: 2 * count], refs[2 * count]
    held, sems_in, sems_out = refs[-3:]
    core, chip = at_ref[0], at_ref[1]
    here, there = ring.origins(core, chip), ring.origins(1 - core, chip)
    incoming, outgoing = [], []
    for i, (block, at) in enumerate(zip(blocks, here + there)):
        half = core if i < count else 1 - core
        for r in range(block.shape[0]):
            inside, outside = held.at[r, :, half, at], out_ref.at[r, :, half, at]
            n = len(incoming)
            incoming.append(pltpu.make_async_copy(block.at[r], inside, sems_in.at[n]))
            outgoing.append(pltpu.make_async_copy(inside, outside, sems_out.at[n]))
    for copy in incoming:
        copy.start()
    for copy, after in zip(incoming, outgoing):
        copy.wait()
        after.start()
    if with_vectors:
        rows = held[:, :, :, :, :, held.shape[-1] - LANES :]
        small = rows.astype(F32).reshape(-1, LANES)
        refs[2 * count + 1][...] = small.T[:16]
    for copy in outgoing:
        copy.wait()


def assemble(ring, mine, theirs, core, with_vectors=False):
    groups, _, rows, lanes = mine[0].shape
    count = ring.count
    chip = lax.axis_index("f")
    shape = (groups, 2, 2, count, rows, lanes)
    width = shape[1] * shape[2] * groups * count * rows
    if rows % 8:
        whole = jnp.zeros(shape, BF16)
        at = ring.origins(core, chip) + ring.origins(1 - core, chip)
        for i, block in enumerate(mine + theirs):
            half = core if i < count else 1 - core
            where = (0, 0, half, at[i], 0, 0)
            whole = lax.dynamic_update_slice(whole, block[:, :, None, None], where)
        whole = whole.reshape(-1, lanes)
        return whole, (whole[:, lanes - LANES :].astype(F32).T[:16] if with_vectors else None)
    out_shape = [jax.ShapeDtypeStruct(shape, BF16)]
    if with_vectors:
        out_shape.append(jax.ShapeDtypeStruct((16, width), F32))
    out = pl.pallas_call(
        functools.partial(assemble_kernel, ring, with_vectors),
        out_shape=out_shape,
        in_specs=[pl.BlockSpec(memory_space=pltpu.SMEM)]
        + [pl.BlockSpec(memory_space=pl.ANY)] * (2 * count),
        out_specs=[pl.BlockSpec(memory_space=pl.ANY)]
        + [pl.BlockSpec(memory_space=pltpu.VMEM)] * with_vectors,
        scratch_shapes=[
            pltpu.VMEM(shape, BF16),
            pltpu.SemaphoreType.DMA((2 * count * groups,)),
            pltpu.SemaphoreType.DMA((2 * count * groups,)),
        ],
        cost_estimate=taking(4),
        compiler_params=params(VMEM_MOST if with_vectors else 8 * 2**20),
        name="assemble",
    )(jnp.stack([core, chip]).astype(jnp.int32), *mine, *theirs)
    return out[0].reshape(-1, lanes), out[1] if with_vectors else None


class Owners:
    def __init__(self, total, side, groups):
        if groups > 1:
            total = lax.psum_scatter(total.astype(BF16), "r", scatter_dimension=0, tiled=True)
        self.side, self.own = side, pick(total[0], side, 0).astype(F32)
        self.trip = Trip(pick(total[0], 1 - side, 0).astype(BF16), "t")

    def by_model(self):
        place = lax.broadcasted_iota(jnp.int32, (2, 1, 1), 0)
        return jnp.where(place == self.side, self.own[None], self.trip.got.astype(F32)[None])


def mixed_kernel(core_ref, left_ref, ctx_ref, dqkv_ref, da_ref, small_ref, send_ref, own_ref):
    at, core = pl.program_id(0), core_ref[0]

    @pl.when(at < 3)
    def _():
        halves_kernel(core, left_ref, dqkv_ref, send_ref, own_ref)

    @pl.when(at == 3)
    def _():
        halves_kernel(core, ctx_ref, da_ref, send_ref, own_ref)

    @pl.when(at == 4)
    def _():
        send_ref[:, :, :LANES] = small_ref[:, 1 - core]
        own_ref[:, :, :LANES] = small_ref[:, core]


def mixed_grad(rows_t, ctx_t, dqkv, da, small, core1, parts):
    size, tokens = rows_t.shape
    run = size // (2 * parts)
    width = da.shape[1]
    small = small.reshape(parts, 2, run, LANES)
    lanes = 4 * width + LANES
    if run % 16:
        full = [dot(rows_t, dqkv), dot(ctx_t, da)]
        full = [f.astype(BF16).reshape(parts, 2, run, -1) for f in full] + [small]
        full = jnp.concatenate(full, axis=-1)
        return pick(full, 1 - core1[0], 1), pick(full, core1[0], 1)
    left = whole_spec((parts, 2, run, tokens))
    half = pl.BlockSpec((parts, run, width), lambda j, _: (0, 0, j))
    return pl.pallas_call(
        mixed_kernel,
        out_shape=[jax.ShapeDtypeStruct((parts, run, lanes), BF16)] * 2,
        grid_spec=pltpu.PrefetchScalarGridSpec(
            num_scalar_prefetch=1,
            grid=(5,),
            in_specs=[
                left,
                left,
                pl.BlockSpec((tokens, width), lambda j, _: (0, jnp.minimum(j, 2))),
                whole_spec(da.shape),
                whole_spec(small.shape),
            ],
            out_specs=[half, half],
        ),
        compiler_params=params(16 * 2**20),
        cost_estimate=taking(8),
        name="attention_gradients",
    )(
        core1,
        rows_t.reshape(parts, 2, run, tokens),
        ctx_t.reshape(parts, 2, run, tokens),
        dqkv,
        da,
        small,
    )


def wide_kernel(half_ref, left_ref, right_ref, out_ref):
    out = dot(left_ref[...], right_ref[...], TN).astype(BF16)
    out_ref[...] = out.reshape(out_ref.shape)


def wide_grad(left, right, half, parts):
    tokens, size = left.shape
    run = size // (2 * parts)
    n = right.shape[1]
    if run % LANES:
        full = dot(left, right, TN).astype(BF16).reshape(parts, 2, run, n)
        return pick(full, half[0], 1)
    return pl.pallas_call(
        wide_kernel,
        out_shape=jax.ShapeDtypeStruct((parts, run, n), BF16),
        grid_spec=pltpu.PrefetchScalarGridSpec(
            num_scalar_prefetch=1,
            grid=(parts,),
            in_specs=[
                pl.BlockSpec((tokens, run), lambda i, h: (0, 2 * i + h[0])),
                whole_spec((tokens, n)),
            ],
            out_specs=pl.BlockSpec((1, run, n), lambda i, h: (i, 0, 0)),
        ),
        compiler_params=params(12 * 2**20),
        cost_estimate=taking(5),
        name="down_gradient",
    )(half, left, right)


def places(tags, model):
    member = tags[:, 0] == model
    count = member.shape[0]
    before = lax.broadcasted_iota(jnp.int32, (count, count), 0) < lax.broadcasted_iota(
        jnp.int32, (count, count), 1
    )
    ranking = jnp.sum(jnp.where(before & member[:, None], 1, 0), axis=0)
    slots = lax.broadcasted_iota(jnp.int32, (CAP, count), 0)
    return (slots == ranking[None, :]) & member[None, :]


def route(chosen, chains):
    marked = jnp.where(chosen[:, :, None, None], chains[None], jnp.zeros((), chains.dtype))
    return jnp.sum(marked.astype(F32), axis=1).astype(chains.dtype)


def body(ring, groups, *args):
    (
        inputs,
        cotangent,
        lengths,
        tags,
        query_weight,
        query_bias,
        key_weight,
        value_weight,
        value_bias,
        output_projection_weight,
        out_bias,
        first_gain,
        first_shift,
        up_weight,
        up_bias,
        down_weight,
        down_bias,
        second_gain,
        second_shift,
    ) = args
    side, core = lax.axis_index("t"), lax.axis_index("core")
    core1 = core.astype(jnp.int32)[None]
    chains = lengths.shape[0]
    width = inputs.shape[1]
    ff = up_weight.shape[2]
    slots = inputs.shape[0] // chains
    tokens = 2 * CAP * slots
    parts = 2 * groups

    shard_a = pack(
        (query_weight, key_weight, value_weight, output_projection_weight),
        (
            query_bias,
            value_bias,
            out_bias,
            first_gain,
            first_shift,
            down_bias,
            second_gain,
            second_shift,
        ),
        up_bias,
    )
    block_a = two_sides(
        pick(shard_a, side, 0), swap(pick(shard_a, 1 - side, 0), "t"), side, groups
    )

    own_places, other_places = places(tags, side), places(tags, 1 - side)
    own_len = jnp.sum(jnp.where(own_places, lengths[None, :], 0), axis=1)
    other_len = jnp.sum(jnp.where(other_places, lengths[None, :], 0), axis=1)
    chain_rows = inputs.reshape(chains, slots, width)
    sent_lens = jnp.broadcast_to(other_len[:, None, None], (CAP, 16, width)).astype(BF16)
    sent = jnp.concatenate([route(other_places, chain_rows), sent_lens], axis=1)

    def other_side(weight):
        return Trip(pick(weight, 1 - side, 0), "t")

    def joined(weight, trip):
        return two_sides(pick(weight, side, 0), trip.got, side, groups)

    ring_a, trip = Gather(ring, block_a), other_side(up_weight)
    message = slot([ring_a, trip], lambda now: tie(now, sent)[1])
    ring_u = Gather(ring, joined(up_weight, trip))
    down_weight = slot([ring_a], lambda now: tie(now, down_weight)[1])
    trip_rows, trip = Trip(message, "t"), other_side(down_weight)
    slot([ring_a, ring_u, trip_rows])

    def make_rows(now):
        _, got, cots = tie(now, trip_rows.got, cotangent.reshape(chains, slots, width))
        rows = jnp.concatenate([route(own_places, chain_rows), got[:, :slots]], axis=0)
        lens = jnp.concatenate([own_len, got[:, slots, 0].astype(jnp.int32)])
        return rows.reshape(tokens, width), lens, route(other_places, cots), cots

    rows_in, lens, other_cot, cot_rows = slot([ring_a, ring_u, trip], make_rows)
    ring_d, trip_cot = Gather(ring, joined(down_weight, trip)), Trip(other_cot, "t")
    for _ in range(ring.long - 4):
        slot([ring_a, ring_u, ring_d])

    def join_attention(now):
        _, blocks = tie(now, ring_a.blocks())
        return assemble(ring, *blocks, core, True)

    whole_a, vectors = slot([ring_u, ring_d, trip_cot], join_attention)

    def do_attention(now):
        _, whole = tie(now, whole_a)
        return attention(rows_in, lens, whole, vectors)

    qkv, unit1, root1, low1, rows_t, ctx_t, low_t = slot([ring_u, ring_d], do_attention)

    def join_up(now):
        _, blocks, own, other = tie(now, ring_u.blocks(), cot_rows, trip_cot.got)
        cot = jnp.concatenate([route(own_places, own), other], axis=0)
        return assemble(ring, *blocks, core)[0], cot.reshape(tokens, width)

    whole_u, cot = slot([ring_d], join_up)
    out_weight = whole_a[:, 3 * width : 4 * width]

    def do_up(now):
        _, whole = tie(now, whole_u)
        return up_and_gelu(low1, whole, whole_a)

    active, slope = slot([ring_d], do_up)
    whole_d, _ = assemble(ring, *ring_d.blocks(), core)
    gain1 = vectors[3:4]

    result, dr2, df, down_sums = down_and_norm(active, whole_d, unit1, cot, vectors)

    origins = ring.origins(core, lax.axis_index("f"))

    def blocks_of(half):
        return half.reshape(groups, 2, ring.count, -1, half.shape[-1])

    def scatter(own, arrived):
        return Scatter(ring, blocks_of(own), blocks_of(arrived), origins)

    trip = Trip(wide_grad(active, df, 1 - core1, parts), "core")

    def down_own(now):
        _, df_now = tie(now, df)
        return wide_grad(active, df_now, core1, parts)

    ring_d = scatter(slot([trip], down_own), trip.got)

    def do_feed_back(now):
        _, df_now = tie(now, df)
        return feed_back(
            df_now, whole_d, slope, whole_u, low_t, dr2, unit1, root1, vectors, core1, parts
        )

    send_u, own_u, dr1, da, bias_sums, back_sums = slot([ring_d], do_feed_back)

    def back_first(now):
        _, da_now = tie(now, da)
        return attention_back(qkv, da_now, out_weight, lens, 0, CAP)

    trip = Trip(send_u, "core")
    dqkv, sums_1 = slot([ring_d, trip], back_first)
    ring_u = scatter(own_u, trip.got)

    def second_half(values):
        return values.reshape(2, CAP, slots, width)[1]

    def back_second(now):
        _, da_now, rows = tie(now, da, result)
        return attention_back(qkv, da_now, out_weight, lens, CAP, CAP, dqkv), second_half(rows)

    (dqkv, sums_2), rows = slot([ring_d, ring_u], back_second)
    trip_result = Trip(rows, "t")

    def attention_grads(now):
        _, dqkv_now = tie(now, dqkv)
        small = small_grads(down_sums, back_sums, bias_sums, sums_1 + sums_2)
        return mixed_grad(rows_t, ctx_t, dqkv_now, da, small, core1, parts)

    send_a, own_a = slot([ring_d, ring_u, trip_result], attention_grads)
    for _ in range(ring.long - 4):
        slot([ring_d, ring_u])

    def do_rows(now):
        _, dq = tie(now, dqkv)
        rows = (dr1 + dot(dq, whole_a[:, : 3 * width], NT)).astype(BF16)
        return rows, second_half(rows)

    trip, owners_d = Trip(send_a, "core"), Owners(ring_d.total, side, groups)
    rows_grad, rows = slot([ring_u, trip, owners_d.trip], do_rows)
    ring_a, trip_rows = scatter(own_a, trip.got), Trip(rows, "t")
    to_home = jnp.concatenate([own_places, other_places], axis=0).T

    def home(values, back):
        both = jnp.concatenate([values.reshape(2, CAP, slots, width)[0], back], axis=0)
        return route(to_home, both).reshape(-1, width)

    def outputs(now):
        _, values, back = tie(now, result, trip_result.got)
        return home(values, back), owners_d.by_model()

    output, grads_d = slot([ring_u, ring_a, trip_rows], outputs)
    owners_u = Owners(ring_u.total, side, groups)

    def input_grads(now):
        _, values, back = tie(now, rows_grad, trip_rows.got)
        return home(values, back)

    input_grad = slot([ring_a, owners_u.trip], input_grads)
    grads_u = slot([ring_a], lambda now: owners_u.by_model())
    for _ in range(ring.long - 3):
        slot([ring_a])

    owners_a = Owners(ring_a.total, side, groups)
    slot([owners_a.trip])
    grads_a = owners_a.by_model()
    columns = jnp.swapaxes(grads_a[:, :, 4 * width : 4 * width + 16], 1, 2)
    return (
        output,
        input_grad,
        grads_a[:, :, :width],
        columns[:, 0],
        grads_a[:, :, width : 2 * width],
        grads_a[:, :, 2 * width : 3 * width],
        columns[:, 1],
        grads_a[:, :, 3 * width : 4 * width],
        columns[:, 2],
        columns[:, 3],
        columns[:, 4],
        grads_u,
        jnp.swapaxes(columns[:, 8:12], 1, 2).reshape(2, -1),
        grads_d,
        columns[:, 5],
        columns[:, 6],
        columns[:, 7],
    )


def solution(mesh):
    dp, fsdp = mesh.shape["dp"], mesh.shape["fsdp"]
    groups = dp // 4
    inner = Mesh(mesh.devices.reshape(groups, 2, 2, fsdp), ("r", "t", "core", "f"))
    every = ("r", "t", "core", "f")
    rows, vector, matrix = P(every, None), P(None, every), P(None, every, None)
    weights = (
        matrix,
        vector,
        matrix,
        matrix,
        vector,
        matrix,
        vector,
        vector,
        vector,
        matrix,
        vector,
        matrix,
        vector,
        vector,
        vector,
    )
    return jax.shard_map(
        functools.partial(body, Ring(fsdp), groups),
        mesh=inner,
        in_specs=(rows, rows, P(every), rows) + weights,
        out_specs=(rows, rows) + weights,
        check_vma=False,
    )
```

```python
import functools

import jax
import jax.numpy as jnp
import numpy as np
from jax import lax
from jax.experimental import pallas as pl
from jax.experimental.pallas import tpu as pltpu
from jax.sharding import Mesh
from jax.sharding import PartitionSpec as P

HEADS = 12
HEAD_DIM = 64
CAP = 3
MIN_LEN = 96
LANES = 128
PAIRS = 3
BF16 = jnp.bfloat16
F32 = jnp.float32
NN = (((1,), (0,)), ((), ()))
NT = (((1,), (1,)), ((), ()))
TN = (((0,), (0,)), ((), ()))
SWAP = [(0, 1), (1, 0)]
VMEM_LIMIT = 56 * 2**20
VMEM_MOST = 56 * 2**20
SMALL = 12


def dot(a, b, dims=NN):
    return lax.dot_general(a, b, dims, preferred_element_type=F32)


def tie(*values):
    return lax.optimization_barrier(values)


def params(limit=VMEM_LIMIT):
    return pltpu.CompilerParams(vmem_limit_bytes=limit)


def taking(micros):
    return pl.CostEstimate(flops=int(micros * 1.1e9), bytes_accessed=1, transcendentals=0)


def whole_spec(shape):
    return pl.BlockSpec(shape, lambda *_: (0,) * len(shape), pipeline_mode=pl.Buffered(1))


def fixed(shape):
    return pl.BlockSpec(shape, lambda *_: (0,) * len(shape))


def head_masks(value=1.0):
    lane = lax.broadcasted_iota(jnp.int32, (1, LANES), 1)
    first = jnp.where(lane < HEAD_DIM, value, 0.0).astype(BF16)
    second = jnp.where(lane >= HEAD_DIM, value, 0.0).astype(BF16)
    return first, second


def stacked(two_heads, masks):
    return jnp.concatenate([two_heads * masks[0], two_heads * masks[1]], axis=0)


def side_by_side(rows):
    half = rows.shape[0] // 2
    return jnp.concatenate([rows[:half], rows[half:]], axis=1)


def probs_of(scores, length):
    keys = scores.shape[0] // 2
    scores = scores.reshape(2, keys, scores.shape[1])
    rest = scores[:, MIN_LEN:]
    slot = lax.broadcasted_iota(jnp.int32, rest.shape, 1) + MIN_LEN
    rest = jnp.where(slot < length, rest, -1000000000.0)
    scores = jnp.concatenate([scores[:, :MIN_LEN], rest], axis=1)
    exponent = jnp.exp(scores - jnp.max(scores, axis=1, keepdims=True))
    return exponent * (1.0 / jnp.sum(exponent, axis=1, keepdims=True))


def as_rows(probs):
    return probs.astype(BF16).reshape(-1, probs.shape[-1])


def in_groups(width, pairs):
    starts = list(range(0, width, LANES))
    return [starts[i : i + pairs] for i in range(0, len(starts), pairs)]


def attention_rows(length, qkv_ref, ctx_ref, base, rows, width):
    masks, scaled = head_masks(), head_masks(HEAD_DIM**-0.5)
    at = slice(base, base + rows)

    def part(index, start):
        return qkv_ref[at, index * width + start : index * width + start + LANES]

    for starts in in_groups(width, 1):
        scores = [dot(stacked(part(1, s), scaled), part(0, s), NT) for s in starts]
        probs = [as_rows(probs_of(s, length)) for s in scores]
        for start, low in zip(starts, probs):
            context = dot(low, stacked(part(2, start), masks), TN)
            ctx_ref[at, start : start + LANES] = context.astype(BF16)


def attention_kernel(
    lens_ref,
    rows_ref,
    weight_ref,
    vec_ref,
    qkv_ref,
    unit_ref,
    root_ref,
    low_ref,
    rows_t_ref,
    ctx_t_ref,
    low_t_ref,
    out_weight_ref,
    ctx_ref,
):
    width = ctx_ref.shape[1]
    rows_t_ref[...] = rows_ref[...].T

    @pl.when(pl.program_id(0) == 0)
    def _():
        out_weight_ref[...] = weight_ref[:, 3 * width : 4 * width]

    rows = qkv_ref.shape[0] // 2
    for part in range(3):
        columns = slice(part * width, (part + 1) * width)
        product = dot(rows_ref[...], weight_ref[:, columns])
        if part != 1:
            product = product + vec_ref[part // 2 : part // 2 + 1, :]
        qkv_ref[:, columns] = product.astype(BF16)
    for chain in range(2):
        length = lens_ref[2 * pl.program_id(0) + chain]
        attention_rows(length, qkv_ref, ctx_ref, chain * rows, rows, width)
    branch = dot(ctx_ref[...], weight_ref[:, 3 * width : 4 * width]) + vec_ref[2:3, :]
    unit, root = normed(rows_ref[...].astype(F32) + branch)
    unit_ref[...] = unit.astype(BF16)
    root_ref[...] = root
    low = (unit * vec_ref[3:4, :] + vec_ref[4:5, :]).astype(BF16)
    low_ref[...] = low
    low_t_ref[...] = low.T
    ctx_t_ref[...] = ctx_ref[...].T


def attention(rows_in, lens, whole_a, vectors):
    total, width = rows_in.shape
    rows = 2 * total // lens.shape[0]

    def tokens(lanes):
        return pl.BlockSpec((rows, lanes), lambda i, _: (i, 0))

    return pl.pallas_call(
        attention_kernel,
        out_shape=[
            jax.ShapeDtypeStruct((total, 3 * width), BF16),
            jax.ShapeDtypeStruct((total, width), BF16),
            jax.ShapeDtypeStruct((total, 1), F32),
            jax.ShapeDtypeStruct((total, width), BF16),
        ]
        + [jax.ShapeDtypeStruct((width, total), BF16)] * 3
        + [jax.ShapeDtypeStruct((width, width), BF16)],
        grid_spec=pltpu.PrefetchScalarGridSpec(
            num_scalar_prefetch=1,
            grid=(total // rows,),
            in_specs=[tokens(width), whole_spec(whole_a.shape), whole_spec(vectors.shape)],
            out_specs=[tokens(3 * width), tokens(width), tokens(1), tokens(width)]
            + [pl.BlockSpec((width, rows), lambda i, _: (0, i))] * 3
            + [fixed((width, width))],
            scratch_shapes=[pltpu.VMEM((rows, width), BF16)],
        ),
        compiler_params=params(20 * 2**20),
        cost_estimate=taking(14),
        name="attention_forward",
    )(lens, rows_in, whole_a, vectors)


def attention_back_kernel(lens_ref, qkv_ref, da_ref, out_weight_ref, dqkv_ref, sum_ref):
    width = da_ref.shape[1]
    length = lens_ref[pl.program_id(0)]
    masks, scaled = head_masks(), head_masks(HEAD_DIM**-0.5)
    dctx = dot(da_ref[...], out_weight_ref[...], NT).astype(BF16)

    @pl.when(pl.program_id(0) == 0)
    def _():
        sum_ref[...] = jnp.zeros_like(sum_ref)

    def store(column, value):
        low = value.astype(BF16)
        dqkv_ref[:, column : column + LANES] = low
        sum_ref[:, column : column + LANES] += jnp.sum(low.astype(F32), axis=0, keepdims=True)

    def part(index, start):
        return qkv_ref[:, index * width + start : index * width + start + LANES]

    for starts in in_groups(width, PAIRS):
        queries = [part(0, s) for s in starts]
        keys = [stacked(part(1, s), scaled) for s in starts]
        grads = [dctx[:, s : s + LANES] for s in starts]
        scores = [dot(k, q, NT) for k, q in zip(keys, queries)]
        dprobs = [dot(stacked(part(2, s), masks), d, NT) for s, d in zip(starts, grads)]
        probs = [probs_of(s, length) for s in scores]
        dprobs = [d.reshape(p.shape) for d, p in zip(dprobs, probs)]
        dscores = [
            as_rows(p * (d - jnp.sum(d * p, axis=1, keepdims=True)))
            for p, d in zip(probs, dprobs)
        ]
        for start, p, d in zip(starts, probs, grads):
            store(2 * width + start, dot(side_by_side(as_rows(p)), stacked(d, masks)))
        for start, d, q in zip(starts, dscores, queries):
            store(width + start, dot(side_by_side(d), stacked(q, scaled)))
        for start, d, k in zip(starts, dscores, keys):
            store(start, dot(d, k, TN))


def attention_back(qkv, da, out_weight, lens):
    total, width = da.shape
    rows = total // lens.shape[0]

    def tokens(lanes):
        return pl.BlockSpec((rows, lanes), lambda i, _: (i, 0))

    return pl.pallas_call(
        attention_back_kernel,
        out_shape=[
            jax.ShapeDtypeStruct((total, 3 * width), BF16),
            jax.ShapeDtypeStruct((1, 3 * width), F32),
        ],
        grid_spec=pltpu.PrefetchScalarGridSpec(
            num_scalar_prefetch=1,
            grid=(lens.shape[0],),
            in_specs=[tokens(3 * width), tokens(width), whole_spec((width, width))],
            out_specs=[tokens(3 * width), fixed((1, 3 * width))],
        ),
        compiler_params=params(12 * 2**20),
        cost_estimate=taking(11),
        name="attention_backward",
    )(lens, qkv, da, out_weight)


def up_kernel(low_ref, up_ref, small_ref, active_ref, slope_ref):
    weight = up_ref[...]
    block = weight.shape[1]
    rows = small_ref.shape[0]
    fold = block // rows
    column = lax.broadcasted_iota(jnp.int32, (LANES, block), 0)
    lane = lax.broadcasted_iota(jnp.int32, (LANES, block), 1)
    spread = (column == SMALL - 4 + lane % fold).astype(F32).astype(BF16)
    row = lax.broadcasted_iota(jnp.int32, (rows, block), 0)
    at = lax.broadcasted_iota(jnp.int32, (rows, block), 1)
    bias = jnp.sum(
        jnp.where(at // fold == row, dot(small_ref[...], spread), 0.0), axis=0, keepdims=True
    )
    step = LANES
    for start in range(0, low_ref.shape[0], step):
        hidden = dot(low_ref[start : start + step, :], weight) + bias
        cdf = 0.5 * (1.0 + lax.erf(hidden * (2.0**-0.5)))
        active_ref[start : start + step, :] = (hidden * cdf).astype(BF16)
        density = jnp.exp(-0.5 * hidden * hidden) * ((2.0 * np.pi) ** -0.5)
        slope_ref[start : start + step, :] = (cdf + hidden * density).astype(BF16)


def up_and_gelu(low, up, whole_a):
    rows, width = low.shape
    ff = up.shape[1]
    block = 512
    return pl.pallas_call(
        up_kernel,
        out_shape=[jax.ShapeDtypeStruct((rows, ff), BF16)] * 2,
        grid=(ff // block,),
        in_specs=[
            whole_spec((rows, width)),
            pl.BlockSpec((width, block), lambda i: (0, i)),
            pl.BlockSpec(
                (width * block // ff, LANES), lambda i: (i, whole_a.shape[1] // LANES - 1)
            ),
        ],
        out_specs=[pl.BlockSpec((rows, block), lambda i: (0, i))] * 2,
        cost_estimate=taking(10),
        compiler_params=params(12 * 2**20),
        name="up_gelu",
    )(low, up, whole_a)


def down_kernel(
    active_ref, down_ref, unit_ref, cot_ref, vec_ref, out_ref, df_ref, sum_ref
):
    @pl.when(pl.program_id(0) == 0)
    def _():
        sum_ref[...] = jnp.zeros_like(sum_ref)

    bias, gain, shift = vec_ref[5:6, :], vec_ref[6:7, :], vec_ref[7:8, :]
    hidden = unit_ref[...].astype(F32) * vec_ref[3:4, :] + vec_ref[4:5, :]
    total = hidden + dot(active_ref[...], down_ref[...]) + bias
    unit, root = normed(total)
    out_ref[...] = (unit * gain + shift).astype(BF16)
    grad = cot_ref[...].astype(F32)
    df = norm_back(grad, unit, root, gain).astype(BF16)
    df_ref[...] = df
    sum_ref[0:1, :] += jnp.sum(df.astype(F32), axis=0, keepdims=True)
    sum_ref[1:2, :] += jnp.sum(grad * unit, axis=0, keepdims=True)
    sum_ref[2:3, :] += jnp.sum(grad, axis=0, keepdims=True)


def down_and_norm(active, down, unit, cot, vectors):
    rows, ff = active.shape
    width = down.shape[1]
    block = 256
    tokens = pl.BlockSpec((block, width), lambda i: (i, 0))
    return pl.pallas_call(
        down_kernel,
        out_shape=[
            jax.ShapeDtypeStruct((rows, width), BF16),
            jax.ShapeDtypeStruct((rows, width), BF16),
            jax.ShapeDtypeStruct((8, width), F32),
        ],
        grid=(rows // block,),
        in_specs=[
            pl.BlockSpec((block, ff), lambda i: (i, 0)),
            whole_spec((ff, width)),
            tokens,
            tokens,
            whole_spec(vectors.shape),
        ],
        out_specs=[tokens, tokens, fixed((8, width))],
        compiler_params=params(18 * 2**20),
        cost_estimate=taking(10),
        name="down_norm",
    )(active, down, unit, cot, vectors)


def back_kernel(
    core_ref,
    df_ref,
    down_ref,
    slope_ref,
    up_ref,
    low_t_ref,
    unit_ref,
    root_ref,
    vec_ref,
    send_ref,
    own_ref,
    da_ref,
    bias_ref,
    sum_ref,
    total,
    grad,
):
    at = pl.program_id(0)
    step = 384

    @pl.when(at == 0)
    def _():
        total[...] = df_ref[...].astype(F32)
        sum_ref[...] = jnp.zeros_like(sum_ref)

    bias = jnp.zeros(bias_ref.shape, F32)
    for start in range(0, df_ref.shape[0], step):
        rows = slice(start, start + step)
        du = dot(df_ref[rows, :], down_ref[...], NT) * slope_ref[rows, :].astype(F32)
        du = du.astype(BF16)
        grad[rows, :] = du
        bias += jnp.sum(du.astype(F32), axis=0, keepdims=True)
        total[rows, :] += dot(du, up_ref[...], NT)
    bias_ref[...] = bias
    halves_kernel(core_ref[0], low_t_ref, grad, send_ref, own_ref)

    @pl.when(at == pl.num_programs(0) - 1)
    def _():
        for start in range(0, df_ref.shape[0], step):
            rows = slice(start, start + step)
            dh1, unit = total[rows, :], unit_ref[rows, :].astype(F32)
            da = norm_back(dh1, unit, root_ref[rows, :], vec_ref[3:4, :]).astype(BF16)
            da_ref[rows, :] = da
            sum_ref[0:1, :] += jnp.sum(da.astype(F32), axis=0, keepdims=True)
            sum_ref[1:2, :] += jnp.sum(dh1 * unit, axis=0, keepdims=True)
            sum_ref[2:3, :] += jnp.sum(dh1, axis=0, keepdims=True)


def halves_kernel(core, left_ref, right_ref, send_ref, own_ref):
    parts, _, run, tokens = left_ref.shape
    for half, out_ref in ((1 - core, send_ref), (core, own_ref)):
        left = left_ref[:, half].reshape(parts * run, tokens)
        out_ref[...] = dot(left, right_ref[...]).astype(BF16).reshape(out_ref.shape)


def feed_back(df, down, slope, up, low_t, unit, root, vectors, core1, parts):
    rows, width = df.shape
    ff = up.shape[1]
    block = 768
    run = width // (2 * parts)
    tokens = whole_spec((rows, width))
    half = pl.BlockSpec((parts, run, block), lambda i, _: (0, 0, i))
    return pl.pallas_call(
        back_kernel,
        out_shape=[
            jax.ShapeDtypeStruct((parts, run, ff), BF16),
            jax.ShapeDtypeStruct((parts, run, ff), BF16),
            jax.ShapeDtypeStruct((rows, width), BF16),
            jax.ShapeDtypeStruct((1, ff), F32),
            jax.ShapeDtypeStruct((8, width), F32),
        ],
        grid_spec=pltpu.PrefetchScalarGridSpec(
            num_scalar_prefetch=1,
            grid=(ff // block,),
            in_specs=[
                tokens,
                pl.BlockSpec((block, width), lambda i, _: (i, 0)),
                pl.BlockSpec((rows, block), lambda i, _: (0, i)),
                pl.BlockSpec((width, block), lambda i, _: (0, i)),
                whole_spec((parts, 2, run, rows)),
                tokens,
                whole_spec(root.shape),
                whole_spec(vectors.shape),
            ],
            out_specs=[
                half,
                half,
                fixed((rows, width)),
                pl.BlockSpec((1, block), lambda i, _: (0, i)),
                fixed((8, width)),
            ],
            scratch_shapes=[pltpu.VMEM((rows, width), F32), pltpu.VMEM((rows, block), BF16)],
        ),
        compiler_params=params(30 * 2**20),
        cost_estimate=taking(21),
        name="feed_forward_back",
    )(core1, df, down, slope, up, low_t.reshape(parts, 2, run, rows), unit, root, vectors)


def normed(values):
    centre = values - jnp.mean(values, axis=-1, keepdims=True)
    root = lax.rsqrt(jnp.mean(centre * centre, axis=-1, keepdims=True) + 1e-05)
    return centre * root, root


def norm_back(grad, unit, root, gain):
    scaled = grad * gain
    inner = jnp.mean(scaled * unit, axis=-1, keepdims=True)
    return root * (scaled - jnp.mean(scaled, axis=-1, keepdims=True) - unit * inner)


def transposed_rows(vectors):
    count, size = vectors.shape
    padded = jnp.concatenate([vectors, jnp.zeros((LANES - count, size), vectors.dtype)], axis=0)
    row = lax.broadcasted_iota(jnp.int32, (size, size), 0)
    column = lax.broadcasted_iota(jnp.int32, (size, size), 1)
    unit = (row == column).astype(F32).astype(BF16)
    return dot(unit, padded.astype(BF16), NT)


def folded(values, rows):
    size = values.shape[1]
    fold = size // rows
    row = lax.broadcasted_iota(jnp.int32, (rows, size), 0)
    at = lax.broadcasted_iota(jnp.int32, (rows, size), 1)
    spread = jnp.where(at // fold == row, values.astype(F32), 0.0).astype(BF16)
    column = lax.broadcasted_iota(jnp.int32, (LANES, size), 0)
    lane = lax.broadcasted_iota(jnp.int32, (LANES, size), 1)
    place = (column == SMALL - 4 + lane % fold).astype(F32).astype(BF16)
    return dot(spread, place, NT)


def pack_kernel(*refs):
    matrices, vectors, up_bias_ref, out_ref = refs[:4], refs[4:12], refs[12], refs[13]
    rows = out_ref.shape[1]
    for model in range(2):
        start = 0
        for matrix in matrices:
            out_ref[model, :, start : start + matrix.shape[2]] = matrix[model]
            start += matrix.shape[2]
        eight = jnp.concatenate([v[model : model + 1, :].astype(F32) for v in vectors], axis=0)
        small = transposed_rows(eight) + folded(up_bias_ref[model : model + 1, :].astype(F32), rows)
        out_ref[model, :, start:] = small.astype(BF16)


def pack(matrices, vectors, up_bias):
    models, rows, _ = matrices[0].shape
    lanes = sum(m.shape[2] for m in matrices) + LANES
    if rows % 8:
        parts = [v[..., None] for v in vectors] + [up_bias.reshape(models, rows, -1)]
        small = jnp.concatenate(parts, axis=-1)
        small = jnp.pad(small, [(0, 0), (0, 0), (0, LANES - small.shape[-1])])
        return jnp.concatenate(list(matrices) + [small], axis=-1)
    return pl.pallas_call(
        pack_kernel,
        out_shape=jax.ShapeDtypeStruct((models, rows, lanes), BF16),
        compiler_params=params(VMEM_MOST),
        name="pack_shard",
    )(*matrices, *vectors, up_bias)


def small_grads_kernel(down_ref, back_ref, bias_ref, qkv_ref, out_ref):
    rows = out_ref.shape[0]
    width = down_ref.shape[1]
    eight = jnp.concatenate(
        [
            qkv_ref[:, :width],
            qkv_ref[:, 2 * width :],
            back_ref[0:3, :],
            down_ref[0:3, :],
        ],
        axis=0,
    )
    out_ref[...] = transposed_rows(eight).astype(BF16)
    step = LANES
    fold = bias_ref.shape[1] // rows
    for start in range(0, rows, step):
        values = bias_ref[:, start * fold : (start + step) * fold]
        here = slice(start, start + step)
        out_ref[here, :] = (out_ref[here, :].astype(F32) + folded(values, step)).astype(BF16)


def small_grads(down_sums, back_sums, bias_sums, qkv_sums):
    width = down_sums.shape[1]
    return pl.pallas_call(
        small_grads_kernel,
        out_shape=jax.ShapeDtypeStruct((width, LANES), BF16),
        compiler_params=params(8 * 2**20),
        name="small_gradients",
    )(down_sums, back_sums, bias_sums, qkv_sums)


class Ring:
    def __init__(self, count):
        depth = 4 if count % 4 == 0 else 2
        wide = count // depth
        order = []
        if wide > 1:
            for z in range(depth):
                ys = range(1, wide) if z % 2 == 0 else reversed(range(1, wide))
                order += [z * wide + y for y in ys]
            order += [z * wide for z in reversed(range(depth))]
        else:
            order = list(range(count))
        self.count, self.depth, self.wide = count, depth, wide
        self.long = count // 2
        self.short = count - 1 - self.long
        self.ahead, self.behind = [], []
        for core in range(2):
            sign = 1 if core == 0 else -1
            here = core * count
            for place, chip in enumerate(order):
                self.ahead.append((here + chip, here + order[(place + sign) % count]))
                self.behind.append((here + chip, here + order[(place - sign) % count]))

    def origins(self, core, chip):
        depth, turn = self.depth, self.wide - 1
        if turn == 0:
            place = chip
        else:
            z, y = lax.div(chip, self.wide), lax.rem(chip, self.wide)
            along = jnp.where(lax.rem(z, 2) == 0, y - 1, turn - y)
            place = jnp.where(y == 0, depth * turn + depth - 1 - z, z * turn + along)
        sign = 1 - 2 * core
        chips = []
        for k in range(self.count):
            off = -k if k <= self.long else k - self.long
            at = lax.rem(place + sign * off + self.count, self.count)
            if turn > 0:
                z, j = lax.div(at, turn), lax.rem(at, turn)
                y = jnp.where(lax.rem(z, 2) == 0, 1 + j, turn - j)
                at = jnp.where(
                    at < depth * turn, z * self.wide + y, (depth * (turn + 1) - 1 - at) * self.wide
                )
            chips.append(at)
        return chips

    def forth(self, block):
        return lax.ppermute(block, ("core", "f"), self.ahead)

    def back(self, block):
        return lax.ppermute(block, ("core", "f"), self.behind)


def swap(value, axis):
    return lax.ppermute(value, axis, SWAP)


def pick(value, index, axis):
    return lax.dynamic_index_in_dim(value, index, axis, keepdims=False)


def two_sides(own, other, side, groups):
    place = lax.broadcasted_iota(jnp.int32, (2, 1, 1), 0)
    block = jnp.where(place == side, own[None], other[None])
    if groups > 1:
        return lax.all_gather(block, "r", axis=0, tiled=False)
    return block[None]


class Gather:
    def __init__(self, ring, block):
        self.ring, self.step = ring, 0
        self.forth, self.back = [block], [block]
        self.theirs_forth, self.theirs_back = [swap(block, "core")], []

    def launch(self):
        self.step += 1
        sent = [self.ring.forth(self.forth[-1])]
        if self.step <= self.ring.short:
            sent.append(self.ring.back(self.back[-1]))
        return sent

    def now(self):
        return self.forth[-1]

    def land(self, sent):
        self.forth.append(sent[0])
        self.theirs_forth.append(swap(sent[0], "core"))
        if len(sent) > 1:
            self.back.append(sent[1])
            self.theirs_back.append(swap(sent[1], "core"))

    def settle(self, values):
        for kept, value in zip((self.theirs_forth, self.theirs_back), values):
            kept[:] = value

    def blocks(self):
        return self.forth + self.back[1:], self.theirs_forth + self.theirs_back


class Scatter:
    def __init__(self, ring, own, other, origins):
        self.ring, self.step = ring, 0
        self.own, self.other, self.origins = own, other, origins
        self.far = self.term(ring.long).astype(BF16)
        self.near = self.term(ring.long + ring.short).astype(BF16)
        self.total = None

    def term(self, k):
        a, b = pick(self.own, self.origins[k], 2), pick(self.other, self.origins[k], 2)
        return a.astype(F32) + b.astype(F32)

    def launch(self):
        self.step += 1
        sent = [self.ring.back(self.far)]
        if self.step > self.ring.long - self.ring.short:
            sent.append(self.ring.forth(self.near))
        return sent

    def now(self):
        return self.far

    def land(self, sent):
        left = self.ring.long - self.step
        if left:
            self.far = (sent[0].astype(F32) + self.term(left)).astype(BF16)
            if len(sent) > 1:
                near = sent[1].astype(F32) + self.term(self.ring.long + left)
                self.near = near.astype(BF16)
        else:
            self.total = sent[0].astype(F32) + sent[1].astype(F32) + self.term(0)


class Trip:
    def __init__(self, value, axis):
        self.value, self.axis, self.got = value, axis, None

    def launch(self):
        return [swap(self.value, self.axis)]

    def now(self):
        return self.value

    def land(self, sent):
        self.got = sent[0]


def slot(movers, work=None):
    now = [m.now() for m in movers]
    sent = [m.launch() for m in movers]
    gathers = [m for m in movers if isinstance(m, Gather)]
    before = [(m.theirs_forth, m.theirs_back) for m in gathers]
    done = None if work is None else work((now, before))
    sent, done, before = tie(sent, done, before)
    for mover, settled in zip(gathers, before):
        mover.settle(settled)
    for mover, arrived in zip(movers, sent):
        mover.land(arrived)
    return done


def assemble_kernel(ring, with_vectors, at_ref, *refs):
    count = ring.count
    blocks, out_ref = refs[: 2 * count], refs[2 * count]
    held, sems_in, sems_out = refs[-3:]
    core, chip = at_ref[0], at_ref[1]
    here, there = ring.origins(core, chip), ring.origins(1 - core, chip)
    incoming, outgoing = [], []
    for i, (block, at) in enumerate(zip(blocks, here + there)):
        half = core if i < count else 1 - core
        for r in range(block.shape[0]):
            inside, outside = held.at[r, :, half, at], out_ref.at[r, :, half, at]
            n = len(incoming)
            incoming.append(pltpu.make_async_copy(block.at[r], inside, sems_in.at[n]))
            outgoing.append(pltpu.make_async_copy(inside, outside, sems_out.at[n]))
    for copy in incoming:
        copy.start()
    for copy, after in zip(incoming, outgoing):
        copy.wait()
        after.start()
    if with_vectors:
        rows = held[:, :, :, :, :, held.shape[-1] - LANES :]
        small = rows.astype(F32).reshape(-1, LANES)
        refs[2 * count + 1][...] = small.T[:16]
    for copy in outgoing:
        copy.wait()


def assemble(ring, mine, theirs, core, with_vectors=False):
    groups, _, rows, lanes = mine[0].shape
    count = ring.count
    chip = lax.axis_index("f")
    shape = (groups, 2, 2, count, rows, lanes)
    width = shape[1] * shape[2] * groups * count * rows
    if rows % 8:
        whole = jnp.zeros(shape, BF16)
        at = ring.origins(core, chip) + ring.origins(1 - core, chip)
        for i, block in enumerate(mine + theirs):
            half = core if i < count else 1 - core
            where = (0, 0, half, at[i], 0, 0)
            whole = lax.dynamic_update_slice(whole, block[:, :, None, None], where)
        whole = whole.reshape(-1, lanes)
        return whole, (whole[:, lanes - LANES :].astype(F32).T[:16] if with_vectors else None)
    out_shape = [jax.ShapeDtypeStruct(shape, BF16)]
    if with_vectors:
        out_shape.append(jax.ShapeDtypeStruct((16, width), F32))
    out = pl.pallas_call(
        functools.partial(assemble_kernel, ring, with_vectors),
        out_shape=out_shape,
        in_specs=[pl.BlockSpec(memory_space=pltpu.SMEM)]
        + [pl.BlockSpec(memory_space=pl.ANY)] * (2 * count),
        out_specs=[pl.BlockSpec(memory_space=pl.ANY)]
        + [pl.BlockSpec(memory_space=pltpu.VMEM)] * with_vectors,
        scratch_shapes=[
            pltpu.VMEM(shape, BF16),
            pltpu.SemaphoreType.DMA((2 * count * groups,)),
            pltpu.SemaphoreType.DMA((2 * count * groups,)),
        ],
        cost_estimate=taking(4),
        compiler_params=params((36 if with_vectors else 8) * 2**20),
        name="assemble",
    )(jnp.stack([core, chip]).astype(jnp.int32), *mine, *theirs)
    return out[0].reshape(-1, lanes), out[1] if with_vectors else None


class Owners:
    def __init__(self, total, side, groups):
        if groups > 1:
            total = lax.psum_scatter(total.astype(BF16), "r", scatter_dimension=0, tiled=True)
        self.side, self.own = side, pick(total[0], side, 0).astype(F32)
        self.trip = Trip(pick(total[0], 1 - side, 0).astype(BF16), "t")

    def by_model(self):
        place = lax.broadcasted_iota(jnp.int32, (2, 1, 1), 0)
        return jnp.where(place == self.side, self.own[None], self.trip.got.astype(F32)[None])


def mixed_kernel(core_ref, left_ref, ctx_ref, dqkv_ref, da_ref, small_ref, send_ref, own_ref):
    at, core = pl.program_id(0), core_ref[0]

    @pl.when(at < 3)
    def _():
        halves_kernel(core, left_ref, dqkv_ref, send_ref, own_ref)

    @pl.when(at == 3)
    def _():
        halves_kernel(core, ctx_ref, da_ref, send_ref, own_ref)

    @pl.when(at == 4)
    def _():
        send_ref[:, :, :LANES] = small_ref[:, 1 - core]
        own_ref[:, :, :LANES] = small_ref[:, core]


def mixed_grad(rows_t, ctx_t, dqkv, da, small, core1, parts):
    size, tokens = rows_t.shape
    run = size // (2 * parts)
    width = da.shape[1]
    small = small.reshape(parts, 2, run, LANES)
    lanes = 4 * width + LANES
    if run % 16:
        full = [dot(rows_t, dqkv), dot(ctx_t, da)]
        full = [f.astype(BF16).reshape(parts, 2, run, -1) for f in full] + [small]
        full = jnp.concatenate(full, axis=-1)
        return pick(full, 1 - core1[0], 1), pick(full, core1[0], 1)
    left = whole_spec((parts, 2, run, tokens))
    half = pl.BlockSpec((parts, run, width), lambda j, _: (0, 0, j))
    return pl.pallas_call(
        mixed_kernel,
        out_shape=[jax.ShapeDtypeStruct((parts, run, lanes), BF16)] * 2,
        grid_spec=pltpu.PrefetchScalarGridSpec(
            num_scalar_prefetch=1,
            grid=(5,),
            in_specs=[
                left,
                left,
                pl.BlockSpec((tokens, width), lambda j, _: (0, jnp.minimum(j, 2))),
                whole_spec(da.shape),
                whole_spec(small.shape),
            ],
            out_specs=[half, half],
        ),
        compiler_params=params(16 * 2**20),
        cost_estimate=taking(8),
        name="attention_gradients",
    )(
        core1,
        rows_t.reshape(parts, 2, run, tokens),
        ctx_t.reshape(parts, 2, run, tokens),
        dqkv,
        da,
        small,
    )


def wide_kernel(core_ref, left_ref, right_ref, send_ref, own_ref):
    out = dot(left_ref[...], right_ref[...], TN).astype(BF16)

    @pl.when(pl.program_id(0) == 0)
    def _():
        send_ref[...] = out.reshape(send_ref.shape)

    @pl.when(pl.program_id(0) == 1)
    def _():
        own_ref[...] = out.reshape(own_ref.shape)


def wide_grad(left, right, core1, parts):
    tokens, size = left.shape
    run = size // (2 * parts)
    n = right.shape[1]
    if run % LANES:
        full = dot(left, right, TN).astype(BF16).reshape(parts, 2, run, n)
        return pick(full, 1 - core1[0], 1), pick(full, core1[0], 1)

    def columns(h, i, core_ref):
        return (0, 2 * i + jnp.where(h == 0, 1 - core_ref[0], core_ref[0]))

    return pl.pallas_call(
        wide_kernel,
        out_shape=[jax.ShapeDtypeStruct((parts, run, n), BF16)] * 2,
        grid_spec=pltpu.PrefetchScalarGridSpec(
            num_scalar_prefetch=1,
            grid=(2, parts),
            in_specs=[pl.BlockSpec((tokens, run), columns), whole_spec((tokens, n))],
            out_specs=[
                pl.BlockSpec((1, run, n), lambda h, i, _: (jnp.where(h == 0, i, parts - 1), 0, 0)),
                pl.BlockSpec((1, run, n), lambda h, i, _: (jnp.where(h == 0, 0, i), 0, 0)),
            ],
        ),
        compiler_params=params(14 * 2**20),
        cost_estimate=taking(5),
        name="down_gradient",
    )(core1, left, right)


def places(tags, model):
    member = tags[:, 0] == model
    count = member.shape[0]
    before = lax.broadcasted_iota(jnp.int32, (count, count), 0) < lax.broadcasted_iota(
        jnp.int32, (count, count), 1
    )
    ranking = jnp.sum(jnp.where(before & member[:, None], 1, 0), axis=0)
    slots = lax.broadcasted_iota(jnp.int32, (CAP, count), 0)
    return (slots == ranking[None, :]) & member[None, :]


def route(chosen, chains):
    marked = jnp.where(chosen[:, :, None, None], chains[None], jnp.zeros((), chains.dtype))
    return jnp.sum(marked.astype(F32), axis=1).astype(chains.dtype)


def body(ring, groups, *args):
    (
        inputs,
        cotangent,
        lengths,
        tags,
        query_weight,
        query_bias,
        key_weight,
        value_weight,
        value_bias,
        output_projection_weight,
        out_bias,
        first_gain,
        first_shift,
        up_weight,
        up_bias,
        down_weight,
        down_bias,
        second_gain,
        second_shift,
    ) = args
    side, core = lax.axis_index("t"), lax.axis_index("core")
    core1 = core.astype(jnp.int32)[None]
    chains = lengths.shape[0]
    width = inputs.shape[1]
    ff = up_weight.shape[2]
    slots = inputs.shape[0] // chains
    tokens = 2 * CAP * slots
    parts = 2 * groups

    shard_a = pack(
        (query_weight, key_weight, value_weight, output_projection_weight),
        (
            query_bias,
            value_bias,
            out_bias,
            first_gain,
            first_shift,
            down_bias,
            second_gain,
            second_shift,
        ),
        up_bias,
    )
    block_a = two_sides(
        pick(shard_a, side, 0), swap(pick(shard_a, 1 - side, 0), "t"), side, groups
    )

    own_places, other_places = places(tags, side), places(tags, 1 - side)
    own_len = jnp.sum(jnp.where(own_places, lengths[None, :], 0), axis=1)
    other_len = jnp.sum(jnp.where(other_places, lengths[None, :], 0), axis=1)
    chain_rows = inputs.reshape(chains, slots, width)
    sent_lens = jnp.broadcast_to(other_len[:, None, None], (CAP, 16, width)).astype(BF16)
    sent = jnp.concatenate([route(other_places, chain_rows), sent_lens], axis=1)

    def other_side(weight):
        return Trip(pick(weight, 1 - side, 0), "t")

    def joined(weight, trip):
        return two_sides(pick(weight, side, 0), trip.got, side, groups)

    ring_a, trip = Gather(ring, block_a), other_side(up_weight)
    message = slot([ring_a, trip], lambda now: tie(now, sent)[1])
    ring_u = Gather(ring, joined(up_weight, trip))
    down_weight = slot([ring_a], lambda now: tie(now, down_weight)[1])
    trip_rows, trip = Trip(message, "t"), other_side(down_weight)
    slot([ring_a, ring_u, trip_rows])

    def make_rows(now):
        _, got, cots = tie(now, trip_rows.got, cotangent.reshape(chains, slots, width))
        rows = jnp.concatenate([route(own_places, chain_rows), got[:, :slots]], axis=0)
        lens = jnp.concatenate([own_len, got[:, slots, 0].astype(jnp.int32)])
        return rows.reshape(tokens, width), lens, route(other_places, cots), cots

    rows_in, lens, other_cot, cot_rows = slot([ring_a, ring_u, trip], make_rows)
    ring_d, trip_cot = Gather(ring, joined(down_weight, trip)), Trip(other_cot, "t")
    for _ in range(ring.long - 4):
        slot([ring_a, ring_u, ring_d])

    def join_attention(now):
        _, blocks = tie(now, ring_a.blocks())
        return assemble(ring, *blocks, core, True)

    whole_a, vectors = slot([ring_u, ring_d, trip_cot], join_attention)

    def do_attention(now):
        _, whole = tie(now, whole_a)
        return attention(rows_in, lens, whole, vectors)

    qkv, unit1, root1, low1, rows_t, ctx_t, low_t, out_weight = slot([ring_u, ring_d], do_attention)

    def join_up(now):
        _, blocks, own, other = tie(now, ring_u.blocks(), cot_rows, trip_cot.got)
        cot = jnp.concatenate([route(own_places, own), other], axis=0)
        return assemble(ring, *blocks, core)[0], cot.reshape(tokens, width)

    whole_u, cot = slot([ring_d], join_up)

    def do_up(now):
        _, whole = tie(now, whole_u)
        return up_and_gelu(low1, whole, whole_a)

    active, slope = slot([ring_d], do_up)
    whole_d, _ = assemble(ring, *ring_d.blocks(), core)
    gain1 = vectors[3:4]

    result, df, down_sums = down_and_norm(active, whole_d, unit1, cot, vectors)

    origins = ring.origins(core, lax.axis_index("f"))

    def blocks_of(half):
        return half.reshape(groups, 2, ring.count, -1, half.shape[-1])

    def scatter(own, arrived):
        return Scatter(ring, blocks_of(own), blocks_of(arrived), origins)

    send_d, own_d = wide_grad(active, df, core1, parts)
    trip = Trip(send_d, "core")

    def do_feed_back(now):
        _, df_now = tie(now, df)
        return feed_back(
            df_now, whole_d, slope, whole_u, low_t, unit1, root1, vectors, core1, parts
        )

    send_u, own_u, da, bias_sums, back_sums = slot([trip], do_feed_back)
    ring_d = scatter(own_d, trip.got)

    def do_attention_back(now):
        _, da_now = tie(now, da)
        return attention_back(qkv, da_now, out_weight, lens)

    def second_half(values):
        return values.reshape(2, CAP, slots, width)[1]

    trip, trip_result = Trip(send_u, "core"), Trip(second_half(tie(result, da)[0]), "t")
    dqkv, qkv_sums = slot([ring_d, trip, trip_result], do_attention_back)
    ring_u = scatter(own_u, trip.got)

    def attention_grads(now):
        _, dqkv_now = tie(now, dqkv)
        small = small_grads(down_sums, back_sums, bias_sums, qkv_sums)
        return mixed_grad(rows_t, ctx_t, dqkv_now, da, small, core1, parts)

    send_a, own_a = slot([ring_d, ring_u], attention_grads)
    def do_rows(now):
        _, dq = tie(now, dqkv)
        rows = (da.astype(F32) + dot(dq, whole_a[:, : 3 * width], NT)).astype(BF16)
        return rows, second_half(rows)

    trip = Trip(send_a, "core")
    rows_grad, rows = slot([ring_d, ring_u, trip], do_rows)
    trip_rows = Trip(rows, "t")
    to_home = jnp.concatenate([own_places, other_places], axis=0).T

    def home(values, back):
        both = jnp.concatenate([values.reshape(2, CAP, slots, width)[0], back], axis=0)
        return route(to_home, both).reshape(-1, width)

    def outputs(now):
        _, values, back = tie(now, result, trip_result.got)
        return home(values, back)

    output = slot([ring_d, ring_u, trip_rows], outputs)
    for _ in range(ring.long - 4):
        slot([ring_d, ring_u])
    ring_a = scatter(own_a, trip.got)
    owners_d = Owners(ring_d.total, side, groups)

    def input_grads(now):
        _, values, back = tie(now, rows_grad, trip_rows.got)
        return home(values, back)

    input_grad = slot([ring_u, ring_a, owners_d.trip], input_grads)
    owners_u = Owners(ring_u.total, side, groups)
    grads_d = slot([ring_a, owners_u.trip], lambda now: owners_d.by_model())
    grads_u = slot([ring_a], lambda now: owners_u.by_model())
    for _ in range(ring.long - 3):
        slot([ring_a])

    owners_a = Owners(ring_a.total, side, groups)
    slot([owners_a.trip])
    grads_a = owners_a.by_model()
    columns = jnp.swapaxes(grads_a[:, :, 4 * width : 4 * width + 16], 1, 2)
    return (
        output,
        input_grad,
        grads_a[:, :, :width],
        columns[:, 0],
        grads_a[:, :, width : 2 * width],
        grads_a[:, :, 2 * width : 3 * width],
        columns[:, 1],
        grads_a[:, :, 3 * width : 4 * width],
        columns[:, 2],
        columns[:, 3],
        columns[:, 4],
        grads_u,
        jnp.swapaxes(columns[:, 8:12], 1, 2).reshape(2, -1),
        grads_d,
        columns[:, 5],
        columns[:, 6],
        columns[:, 7],
    )


def solution(mesh):
    dp, fsdp = mesh.shape["dp"], mesh.shape["fsdp"]
    groups = dp // 4
    inner = Mesh(mesh.devices.reshape(groups, 2, 2, fsdp), ("r", "t", "core", "f"))
    every = ("r", "t", "core", "f")
    rows, vector, matrix = P(every, None), P(None, every), P(None, every, None)
    weights = (
        matrix,
        vector,
        matrix,
        matrix,
        vector,
        matrix,
        vector,
        vector,
        vector,
        matrix,
        vector,
        matrix,
        vector,
        vector,
        vector,
    )
    return jax.shard_map(
        functools.partial(body, Ring(fsdp), groups),
        mesh=inner,
        in_specs=(rows, rows, P(every), rows) + weights,
        out_specs=(rows, rows) + weights,
        check_vma=False,
    )
```

```python
import functools

import jax
import jax.numpy as jnp
import numpy as np
from jax import lax
from jax.experimental import pallas as pl
from jax.experimental.pallas import tpu as pltpu
from jax.sharding import Mesh
from jax.sharding import PartitionSpec as P

HEADS = 12
HEAD_DIM = 64
CAP = 3
MIN_LEN = 96
LANES = 128
PAIRS = 3
BF16 = jnp.bfloat16
F32 = jnp.float32
NN = (((1,), (0,)), ((), ()))
NT = (((1,), (1,)), ((), ()))
TN = (((0,), (0,)), ((), ()))
SWAP = [(0, 1), (1, 0)]
VMEM_LIMIT = 56 * 2**20
VMEM_MOST = 56 * 2**20
SMALL = 12


def dot(a, b, dims=NN):
    return lax.dot_general(a, b, dims, preferred_element_type=F32)


def tie(*values):
    return lax.optimization_barrier(values)


def params(limit=VMEM_LIMIT):
    return pltpu.CompilerParams(vmem_limit_bytes=limit)


def taking(micros):
    return pl.CostEstimate(flops=int(micros * 1.1e9), bytes_accessed=1, transcendentals=0)


def whole_spec(shape):
    return pl.BlockSpec(shape, lambda *_: (0,) * len(shape), pipeline_mode=pl.Buffered(1))


def fixed(shape):
    return pl.BlockSpec(shape, lambda *_: (0,) * len(shape))


def head_masks(value=1.0):
    lane = lax.broadcasted_iota(jnp.int32, (1, LANES), 1)
    first = jnp.where(lane < HEAD_DIM, value, 0.0).astype(BF16)
    second = jnp.where(lane >= HEAD_DIM, value, 0.0).astype(BF16)
    return first, second


def stacked(two_heads, masks):
    return jnp.concatenate([two_heads * masks[0], two_heads * masks[1]], axis=0)


def side_by_side(rows):
    half = rows.shape[0] // 2
    return jnp.concatenate([rows[:half], rows[half:]], axis=1)


def probs_of(scores, length):
    keys = scores.shape[0] // 2
    scores = scores.reshape(2, keys, scores.shape[1])
    rest = scores[:, MIN_LEN:]
    slot = lax.broadcasted_iota(jnp.int32, rest.shape, 1) + MIN_LEN
    rest = jnp.where(slot < length, rest, -1000000000.0)
    scores = jnp.concatenate([scores[:, :MIN_LEN], rest], axis=1)
    exponent = jnp.exp(scores - jnp.max(scores, axis=1, keepdims=True))
    return exponent * (1.0 / jnp.sum(exponent, axis=1, keepdims=True))


def as_rows(probs):
    return probs.astype(BF16).reshape(-1, probs.shape[-1])


def in_groups(width, pairs):
    starts = list(range(0, width, LANES))
    return [starts[i : i + pairs] for i in range(0, len(starts), pairs)]


def attention_rows(length, qkv_ref, ctx_ref, base, rows, width):
    masks, scaled = head_masks(), head_masks(HEAD_DIM**-0.5)
    at = slice(base, base + rows)

    def part(index, start):
        return qkv_ref[at, index * width + start : index * width + start + LANES]

    for starts in in_groups(width, 1):
        scores = [dot(stacked(part(1, s), scaled), part(0, s), NT) for s in starts]
        probs = [as_rows(probs_of(s, length)) for s in scores]
        for start, low in zip(starts, probs):
            context = dot(low, stacked(part(2, start), masks), TN)
            ctx_ref[at, start : start + LANES] = context.astype(BF16)


def attention_kernel(
    lens_ref,
    rows_ref,
    weight_ref,
    vec_ref,
    qkv_ref,
    unit_ref,
    root_ref,
    low_ref,
    ctx_t_ref,
    low_t_ref,
    ctx_ref,
):
    width = ctx_ref.shape[1]
    rows = qkv_ref.shape[0] // 2
    for part in range(3):
        columns = slice(part * width, (part + 1) * width)
        product = dot(rows_ref[...], weight_ref[:, columns])
        if part != 1:
            product = product + vec_ref[part // 2 : part // 2 + 1, :]
        qkv_ref[:, columns] = product.astype(BF16)
    for chain in range(2):
        length = lens_ref[2 * pl.program_id(0) + chain]
        attention_rows(length, qkv_ref, ctx_ref, chain * rows, rows, width)
    branch = dot(ctx_ref[...], weight_ref[:, 3 * width : 4 * width]) + vec_ref[2:3, :]
    unit, root = normed(rows_ref[...].astype(F32) + branch)
    unit_ref[...] = unit.astype(BF16)
    root_ref[...] = root
    low = (unit * vec_ref[3:4, :] + vec_ref[4:5, :]).astype(BF16)
    low_ref[...] = low
    low_t_ref[...] = low.T
    ctx_t_ref[...] = ctx_ref[...].T


def turn_kernel(rows_ref, out_ref):
    out_ref[...] = rows_ref[...].T


def turned(rows):
    return pl.pallas_call(
        turn_kernel,
        out_shape=jax.ShapeDtypeStruct(rows.shape[::-1], rows.dtype),
        compiler_params=params(12 * 2**20),
        cost_estimate=taking(2),
        name="turn_rows",
    )(rows)


def attention(rows_in, lens, whole_a, vectors):
    total, width = rows_in.shape
    rows = 2 * total // lens.shape[0]

    def tokens(lanes):
        return pl.BlockSpec((rows, lanes), lambda i, _: (i, 0))

    return pl.pallas_call(
        attention_kernel,
        out_shape=[
            jax.ShapeDtypeStruct((total, 3 * width), BF16),
            jax.ShapeDtypeStruct((total, width), BF16),
            jax.ShapeDtypeStruct((total, 1), F32),
            jax.ShapeDtypeStruct((total, width), BF16),
        ]
        + [jax.ShapeDtypeStruct((width, total), BF16)] * 2,
        grid_spec=pltpu.PrefetchScalarGridSpec(
            num_scalar_prefetch=1,
            grid=(total // rows,),
            in_specs=[tokens(width), whole_spec(whole_a.shape), whole_spec(vectors.shape)],
            out_specs=[tokens(3 * width), tokens(width), tokens(1), tokens(width)]
            + [pl.BlockSpec((width, rows), lambda i, _: (0, i))] * 2,
            scratch_shapes=[pltpu.VMEM((rows, width), BF16)],
        ),
        compiler_params=params(20 * 2**20),
        cost_estimate=taking(14),
        name="attention_forward",
    )(lens, rows_in, whole_a, vectors)


def attention_back_kernel(lens_ref, qkv_ref, da_ref, out_weight_ref, dqkv_ref, sum_ref):
    width = da_ref.shape[1]
    length = lens_ref[pl.program_id(0)]
    masks, scaled = head_masks(), head_masks(HEAD_DIM**-0.5)
    dctx = dot(da_ref[...], out_weight_ref[...], NT).astype(BF16)

    @pl.when(pl.program_id(0) == 0)
    def _():
        sum_ref[...] = jnp.zeros_like(sum_ref)

    def store(column, value):
        low = value.astype(BF16)
        dqkv_ref[:, column : column + LANES] = low
        sum_ref[:, column : column + LANES] += jnp.sum(low.astype(F32), axis=0, keepdims=True)

    def part(index, start):
        return qkv_ref[:, index * width + start : index * width + start + LANES]

    for starts in in_groups(width, PAIRS):
        queries = [part(0, s) for s in starts]
        keys = [stacked(part(1, s), scaled) for s in starts]
        grads = [dctx[:, s : s + LANES] for s in starts]
        scores = [dot(k, q, NT) for k, q in zip(keys, queries)]
        dprobs = [dot(stacked(part(2, s), masks), d, NT) for s, d in zip(starts, grads)]
        probs = [probs_of(s, length) for s in scores]
        dprobs = [d.reshape(p.shape) for d, p in zip(dprobs, probs)]
        dscores = [
            as_rows(p * (d - jnp.sum(d * p, axis=1, keepdims=True)))
            for p, d in zip(probs, dprobs)
        ]
        for start, p, d in zip(starts, probs, grads):
            store(2 * width + start, dot(side_by_side(as_rows(p)), stacked(d, masks)))
        for start, d, q in zip(starts, dscores, queries):
            store(width + start, dot(side_by_side(d), stacked(q, scaled)))
        for start, d, k in zip(starts, dscores, keys):
            store(start, dot(d, k, TN))


def attention_back(qkv, da, out_weight, lens):
    total, width = da.shape
    rows = total // lens.shape[0]

    def tokens(lanes):
        return pl.BlockSpec((rows, lanes), lambda i, _: (i, 0))

    return pl.pallas_call(
        attention_back_kernel,
        out_shape=[
            jax.ShapeDtypeStruct((total, 3 * width), BF16),
            jax.ShapeDtypeStruct((1, 3 * width), F32),
        ],
        grid_spec=pltpu.PrefetchScalarGridSpec(
            num_scalar_prefetch=1,
            grid=(lens.shape[0],),
            in_specs=[tokens(3 * width), tokens(width), whole_spec((width, width))],
            out_specs=[tokens(3 * width), fixed((1, 3 * width))],
        ),
        compiler_params=params(12 * 2**20),
        cost_estimate=taking(11),
        name="attention_backward",
    )(lens, qkv, da, out_weight)


def up_kernel(low_ref, up_ref, small_ref, active_ref, slope_ref):
    weight = up_ref[...]
    block = weight.shape[1]
    rows = small_ref.shape[0]
    fold = block // rows
    column = lax.broadcasted_iota(jnp.int32, (LANES, block), 0)
    lane = lax.broadcasted_iota(jnp.int32, (LANES, block), 1)
    spread = (column == SMALL - 4 + lane % fold).astype(F32).astype(BF16)
    row = lax.broadcasted_iota(jnp.int32, (rows, block), 0)
    at = lax.broadcasted_iota(jnp.int32, (rows, block), 1)
    bias = jnp.sum(
        jnp.where(at // fold == row, dot(small_ref[...], spread), 0.0), axis=0, keepdims=True
    )
    step = LANES
    for start in range(0, low_ref.shape[0], step):
        hidden = dot(low_ref[start : start + step, :], weight) + bias
        cdf = 0.5 * (1.0 + lax.erf(hidden * (2.0**-0.5)))
        active_ref[start : start + step, :] = (hidden * cdf).astype(BF16)
        density = jnp.exp(-0.5 * hidden * hidden) * ((2.0 * np.pi) ** -0.5)
        slope_ref[start : start + step, :] = (cdf + hidden * density).astype(BF16)


def up_and_gelu(low, up, whole_a):
    rows, width = low.shape
    ff = up.shape[1]
    block = 512
    return pl.pallas_call(
        up_kernel,
        out_shape=[jax.ShapeDtypeStruct((rows, ff), BF16)] * 2,
        grid=(ff // block,),
        in_specs=[
            whole_spec((rows, width)),
            pl.BlockSpec((width, block), lambda i: (0, i)),
            pl.BlockSpec(
                (width * block // ff, LANES), lambda i: (i, whole_a.shape[1] // LANES - 1)
            ),
        ],
        out_specs=[pl.BlockSpec((rows, block), lambda i: (0, i))] * 2,
        cost_estimate=taking(10),
        compiler_params=params(12 * 2**20),
        name="up_gelu",
    )(low, up, whole_a)


def down_kernel(
    active_ref, down_ref, unit_ref, cot_ref, vec_ref, out_ref, df_ref, sum_ref
):
    @pl.when(pl.program_id(0) == 0)
    def _():
        sum_ref[...] = jnp.zeros_like(sum_ref)

    bias, gain, shift = vec_ref[5:6, :], vec_ref[6:7, :], vec_ref[7:8, :]
    hidden = unit_ref[...].astype(F32) * vec_ref[3:4, :] + vec_ref[4:5, :]
    total = hidden + dot(active_ref[...], down_ref[...]) + bias
    unit, root = normed(total)
    out_ref[...] = (unit * gain + shift).astype(BF16)
    grad = cot_ref[...].astype(F32)
    df = norm_back(grad, unit, root, gain).astype(BF16)
    df_ref[...] = df
    sum_ref[0:1, :] += jnp.sum(df.astype(F32), axis=0, keepdims=True)
    sum_ref[1:2, :] += jnp.sum(grad * unit, axis=0, keepdims=True)
    sum_ref[2:3, :] += jnp.sum(grad, axis=0, keepdims=True)


def down_and_norm(active, down, unit, cot, vectors):
    rows, ff = active.shape
    width = down.shape[1]
    block = 256
    tokens = pl.BlockSpec((block, width), lambda i: (i, 0))
    return pl.pallas_call(
        down_kernel,
        out_shape=[
            jax.ShapeDtypeStruct((rows, width), BF16),
            jax.ShapeDtypeStruct((rows, width), BF16),
            jax.ShapeDtypeStruct((8, width), F32),
        ],
        grid=(rows // block,),
        in_specs=[
            pl.BlockSpec((block, ff), lambda i: (i, 0)),
            whole_spec((ff, width)),
            tokens,
            tokens,
            whole_spec(vectors.shape),
        ],
        out_specs=[tokens, tokens, fixed((8, width))],
        compiler_params=params(18 * 2**20),
        cost_estimate=taking(10),
        name="down_norm",
    )(active, down, unit, cot, vectors)


def back_kernel(
    core_ref,
    df_ref,
    down_ref,
    slope_ref,
    up_ref,
    low_t_ref,
    unit_ref,
    root_ref,
    vec_ref,
    send_ref,
    own_ref,
    da_ref,
    bias_ref,
    sum_ref,
    total,
    grad,
):
    at = pl.program_id(0)
    step = 384

    @pl.when(at == 0)
    def _():
        total[...] = df_ref[...].astype(F32)
        sum_ref[...] = jnp.zeros_like(sum_ref)

    bias = jnp.zeros(bias_ref.shape, F32)
    for start in range(0, df_ref.shape[0], step):
        rows = slice(start, start + step)
        du = dot(df_ref[rows, :], down_ref[...], NT) * slope_ref[rows, :].astype(F32)
        du = du.astype(BF16)
        grad[rows, :] = du
        bias += jnp.sum(du.astype(F32), axis=0, keepdims=True)
        total[rows, :] += dot(du, up_ref[...], NT)
    bias_ref[...] = bias
    halves_kernel(core_ref[0], low_t_ref, grad, send_ref, own_ref)

    @pl.when(at == pl.num_programs(0) - 1)
    def _():
        for start in range(0, df_ref.shape[0], step):
            rows = slice(start, start + step)
            dh1, unit = total[rows, :], unit_ref[rows, :].astype(F32)
            da = norm_back(dh1, unit, root_ref[rows, :], vec_ref[3:4, :]).astype(BF16)
            da_ref[rows, :] = da
            sum_ref[0:1, :] += jnp.sum(da.astype(F32), axis=0, keepdims=True)
            sum_ref[1:2, :] += jnp.sum(dh1 * unit, axis=0, keepdims=True)
            sum_ref[2:3, :] += jnp.sum(dh1, axis=0, keepdims=True)


def halves_kernel(core, left_ref, right_ref, send_ref, own_ref):
    parts, _, run, tokens = left_ref.shape
    for half, out_ref in ((1 - core, send_ref), (core, own_ref)):
        left = left_ref[:, half].reshape(parts * run, tokens)
        out_ref[...] = dot(left, right_ref[...]).astype(BF16).reshape(out_ref.shape)


def feed_back(df, down, slope, up, low_t, unit, root, vectors, core1, parts):
    rows, width = df.shape
    ff = up.shape[1]
    block = 768
    run = width // (2 * parts)
    tokens = whole_spec((rows, width))
    half = pl.BlockSpec((parts, run, block), lambda i, _: (0, 0, i))
    return pl.pallas_call(
        back_kernel,
        out_shape=[
            jax.ShapeDtypeStruct((parts, run, ff), BF16),
            jax.ShapeDtypeStruct((parts, run, ff), BF16),
            jax.ShapeDtypeStruct((rows, width), BF16),
            jax.ShapeDtypeStruct((1, ff), F32),
            jax.ShapeDtypeStruct((8, width), F32),
        ],
        grid_spec=pltpu.PrefetchScalarGridSpec(
            num_scalar_prefetch=1,
            grid=(ff // block,),
            in_specs=[
                tokens,
                pl.BlockSpec((block, width), lambda i, _: (i, 0)),
                pl.BlockSpec((rows, block), lambda i, _: (0, i)),
                pl.BlockSpec((width, block), lambda i, _: (0, i)),
                whole_spec((parts, 2, run, rows)),
                tokens,
                whole_spec(root.shape),
                whole_spec(vectors.shape),
            ],
            out_specs=[
                half,
                half,
                fixed((rows, width)),
                pl.BlockSpec((1, block), lambda i, _: (0, i)),
                fixed((8, width)),
            ],
            scratch_shapes=[pltpu.VMEM((rows, width), F32), pltpu.VMEM((rows, block), BF16)],
        ),
        compiler_params=params(30 * 2**20),
        cost_estimate=taking(21),
        name="feed_forward_back",
    )(core1, df, down, slope, up, low_t.reshape(parts, 2, run, rows), unit, root, vectors)


def normed(values):
    centre = values - jnp.mean(values, axis=-1, keepdims=True)
    root = lax.rsqrt(jnp.mean(centre * centre, axis=-1, keepdims=True) + 1e-05)
    return centre * root, root


def norm_back(grad, unit, root, gain):
    scaled = grad * gain
    inner = jnp.mean(scaled * unit, axis=-1, keepdims=True)
    return root * (scaled - jnp.mean(scaled, axis=-1, keepdims=True) - unit * inner)


def transposed_rows(vectors):
    count, size = vectors.shape
    padded = jnp.concatenate([vectors, jnp.zeros((LANES - count, size), vectors.dtype)], axis=0)
    row = lax.broadcasted_iota(jnp.int32, (size, size), 0)
    column = lax.broadcasted_iota(jnp.int32, (size, size), 1)
    unit = (row == column).astype(F32).astype(BF16)
    return dot(unit, padded.astype(BF16), NT)


def folded(values, rows):
    size = values.shape[1]
    fold = size // rows
    row = lax.broadcasted_iota(jnp.int32, (rows, size), 0)
    at = lax.broadcasted_iota(jnp.int32, (rows, size), 1)
    spread = jnp.where(at // fold == row, values.astype(F32), 0.0).astype(BF16)
    column = lax.broadcasted_iota(jnp.int32, (LANES, size), 0)
    lane = lax.broadcasted_iota(jnp.int32, (LANES, size), 1)
    place = (column == SMALL - 4 + lane % fold).astype(F32).astype(BF16)
    return dot(spread, place, NT)


def pack_kernel(side_ref, *refs):
    matrices, vectors, up_bias_ref = refs[:4], refs[4:12], refs[12]
    rows = refs[13].shape[0]
    for model, out_ref in ((side_ref[0], refs[13]), (1 - side_ref[0], refs[14])):

        def row(vector):
            both = vector[...].astype(F32)
            return jnp.where(model == 0, both[0:1, :], both[1:2, :])

        start = 0
        for matrix in matrices:
            out_ref[:, start : start + matrix.shape[2]] = matrix[model]
            start += matrix.shape[2]
        eight = jnp.concatenate([row(v) for v in vectors], axis=0)
        small = transposed_rows(eight) + folded(row(up_bias_ref), rows)
        out_ref[:, start:] = small.astype(BF16)


def pack(matrices, vectors, up_bias, side):
    models, rows, _ = matrices[0].shape
    lanes = sum(m.shape[2] for m in matrices) + LANES
    if rows % 8:
        parts = [v[..., None] for v in vectors] + [up_bias.reshape(models, rows, -1)]
        small = jnp.concatenate(parts, axis=-1)
        small = jnp.pad(small, [(0, 0), (0, 0), (0, LANES - small.shape[-1])])
        both = jnp.concatenate(list(matrices) + [small], axis=-1)
        return pick(both, side, 0), pick(both, 1 - side, 0)
    return pl.pallas_call(
        pack_kernel,
        out_shape=[jax.ShapeDtypeStruct((rows, lanes), BF16)] * 2,
        in_specs=[pl.BlockSpec(memory_space=pltpu.SMEM)]
        + [pl.BlockSpec(memory_space=pltpu.VMEM)] * 13,
        compiler_params=params(VMEM_MOST),
        name="pack_shard",
    )(side.astype(jnp.int32)[None], *matrices, *vectors, up_bias)


def small_grads_kernel(down_ref, back_ref, bias_ref, qkv_ref, out_ref):
    rows = out_ref.shape[0]
    width = down_ref.shape[1]
    eight = jnp.concatenate(
        [
            qkv_ref[:, :width],
            qkv_ref[:, 2 * width :],
            back_ref[0:3, :],
            down_ref[0:3, :],
        ],
        axis=0,
    )
    out_ref[...] = transposed_rows(eight).astype(BF16)
    step = LANES
    fold = bias_ref.shape[1] // rows
    for start in range(0, rows, step):
        values = bias_ref[:, start * fold : (start + step) * fold]
        here = slice(start, start + step)
        out_ref[here, :] = (out_ref[here, :].astype(F32) + folded(values, step)).astype(BF16)


def small_grads(down_sums, back_sums, bias_sums, qkv_sums):
    width = down_sums.shape[1]
    return pl.pallas_call(
        small_grads_kernel,
        out_shape=jax.ShapeDtypeStruct((width, LANES), BF16),
        compiler_params=params(8 * 2**20),
        name="small_gradients",
    )(down_sums, back_sums, bias_sums, qkv_sums)


class Ring:
    def __init__(self, count):
        depth = 4 if count % 4 == 0 else 2
        wide = count // depth
        order = []
        if wide > 1:
            for z in range(depth):
                ys = range(1, wide) if z % 2 == 0 else reversed(range(1, wide))
                order += [z * wide + y for y in ys]
            order += [z * wide for z in reversed(range(depth))]
        else:
            order = list(range(count))
        self.count, self.depth, self.wide = count, depth, wide
        self.long = count // 2
        self.short = count - 1 - self.long
        self.ahead, self.behind = [], []
        for core in range(2):
            sign = 1 if core == 0 else -1
            here = core * count
            for place, chip in enumerate(order):
                self.ahead.append((here + chip, here + order[(place + sign) % count]))
                self.behind.append((here + chip, here + order[(place - sign) % count]))

    def origins(self, core, chip):
        depth, turn = self.depth, self.wide - 1
        if turn == 0:
            place = chip
        else:
            z, y = lax.div(chip, self.wide), lax.rem(chip, self.wide)
            along = jnp.where(lax.rem(z, 2) == 0, y - 1, turn - y)
            place = jnp.where(y == 0, depth * turn + depth - 1 - z, z * turn + along)
        sign = 1 - 2 * core
        chips = []
        for k in range(self.count):
            off = -k if k <= self.long else k - self.long
            at = lax.rem(place + sign * off + self.count, self.count)
            if turn > 0:
                z, j = lax.div(at, turn), lax.rem(at, turn)
                y = jnp.where(lax.rem(z, 2) == 0, 1 + j, turn - j)
                at = jnp.where(
                    at < depth * turn, z * self.wide + y, (depth * (turn + 1) - 1 - at) * self.wide
                )
            chips.append(at)
        return chips

    def forth(self, block):
        return lax.ppermute(block, ("core", "f"), self.ahead)

    def back(self, block):
        return lax.ppermute(block, ("core", "f"), self.behind)


def swap(value, axis):
    return lax.ppermute(value, axis, SWAP)


def pick(value, index, axis):
    return lax.dynamic_index_in_dim(value, index, axis, keepdims=False)


def two_sides(own, other, side, groups):
    place = lax.broadcasted_iota(jnp.int32, (2, 1, 1), 0)
    block = jnp.where(place == side, own[None], other[None])
    if groups > 1:
        return lax.all_gather(block, "r", axis=0, tiled=False)
    return block[None]


class Gather:
    def __init__(self, ring, block):
        self.ring, self.step = ring, 0
        self.forth, self.back = [block], [block]
        self.theirs_forth, self.theirs_back = [swap(block, "core")], []

    def launch(self):
        self.step += 1
        sent = [self.ring.forth(self.forth[-1])]
        if self.step <= self.ring.short:
            sent.append(self.ring.back(self.back[-1]))
        return sent

    def now(self):
        return self.forth[-1]

    def land(self, sent):
        self.forth.append(sent[0])
        self.theirs_forth.append(swap(sent[0], "core"))
        if len(sent) > 1:
            self.back.append(sent[1])
            self.theirs_back.append(swap(sent[1], "core"))

    def settle(self, values):
        for kept, value in zip((self.theirs_forth, self.theirs_back), values):
            kept[:] = value

    def blocks(self):
        return self.forth + self.back[1:], self.theirs_forth + self.theirs_back


class Scatter:
    def __init__(self, ring, own, other, origins):
        self.ring, self.step = ring, 0
        self.own, self.other, self.origins = own, other, origins
        self.far = self.term(ring.long).astype(BF16)
        self.near = self.term(ring.long + ring.short).astype(BF16)
        self.total = None

    def term(self, k):
        a, b = pick(self.own, self.origins[k], 2), pick(self.other, self.origins[k], 2)
        return a.astype(F32) + b.astype(F32)

    def launch(self):
        self.step += 1
        sent = [self.ring.back(self.far)]
        if self.step > self.ring.long - self.ring.short:
            sent.append(self.ring.forth(self.near))
        return sent

    def now(self):
        return self.far

    def land(self, sent):
        left = self.ring.long - self.step
        if left:
            self.far = (sent[0].astype(F32) + self.term(left)).astype(BF16)
            if len(sent) > 1:
                near = sent[1].astype(F32) + self.term(self.ring.long + left)
                self.near = near.astype(BF16)
        else:
            self.total = sent[0].astype(F32) + sent[1].astype(F32) + self.term(0)


class Trip:
    def __init__(self, value, axis):
        self.value, self.axis, self.got = value, axis, None

    def launch(self):
        return [swap(self.value, self.axis)]

    def now(self):
        return self.value

    def land(self, sent):
        self.got = sent[0]


class Kept:
    def __init__(self, small, *rest):
        self.small, self.rest = small, rest


def slot(movers, work=None):
    now = [m.now() for m in movers]
    sent = [m.launch() for m in movers]
    gathers = [m for m in movers if isinstance(m, Gather)]
    before = [(m.theirs_forth, m.theirs_back) for m in gathers]
    done = None if work is None else work((now, before))
    if isinstance(done, Kept):
        kept, done = done.rest, done.small
    else:
        kept = None
    sent, done, before = tie(sent, done, before)
    for mover, settled in zip(gathers, before):
        mover.settle(settled)
    for mover, arrived in zip(movers, sent):
        mover.land(arrived)
    return done if kept is None else (done,) + tuple(kept)


def assemble_kernel(ring, with_vectors, at_ref, *refs):
    count = ring.count
    blocks, out_ref = refs[: 2 * count], refs[2 * count]
    held, sems_in, sems_out = refs[-3:]
    core, chip = at_ref[0], at_ref[1]
    here, there = ring.origins(core, chip), ring.origins(1 - core, chip)
    incoming, outgoing = [], []
    for i, (block, at) in enumerate(zip(blocks, here + there)):
        half = core if i < count else 1 - core
        for r in range(block.shape[0]):
            inside, outside = held.at[r, :, half, at], out_ref.at[r, :, half, at]
            n = len(incoming)
            incoming.append(pltpu.make_async_copy(block.at[r], inside, sems_in.at[n]))
            outgoing.append(pltpu.make_async_copy(inside, outside, sems_out.at[n]))
    for copy in incoming:
        copy.start()
    for copy, after in zip(incoming, outgoing):
        copy.wait()
        after.start()
    if with_vectors:
        rows = held[:, :, :, :, :, held.shape[-1] - LANES :]
        small = rows.astype(F32).reshape(-1, LANES)
        refs[2 * count + 1][...] = small.T[:16]
        width = refs[2 * count + 2].shape[0]
        output = held[:, :, :, :, :, 3 * width : 4 * width]
        refs[2 * count + 2][...] = output.astype(F32).reshape(-1, width).astype(BF16)
    for copy in outgoing:
        copy.wait()


def assemble(ring, mine, theirs, core, with_vectors=False):
    groups, _, rows, lanes = mine[0].shape
    count = ring.count
    chip = lax.axis_index("f")
    shape = (groups, 2, 2, count, rows, lanes)
    width = shape[1] * shape[2] * groups * count * rows
    if rows % 8:
        whole = jnp.zeros(shape, BF16)
        at = ring.origins(core, chip) + ring.origins(1 - core, chip)
        for i, block in enumerate(mine + theirs):
            half = core if i < count else 1 - core
            where = (0, 0, half, at[i], 0, 0)
            whole = lax.dynamic_update_slice(whole, block[:, :, None, None], where)
        whole = whole.reshape(-1, lanes)
        if not with_vectors:
            return whole, None
        vectors = whole[:, lanes - LANES :].astype(F32).T[:16]
        return whole, vectors, whole[:, 3 * width : 4 * width]
    out_shape = [jax.ShapeDtypeStruct(shape, BF16)]
    if with_vectors:
        out_shape.append(jax.ShapeDtypeStruct((16, width), F32))
        out_shape.append(jax.ShapeDtypeStruct((width, width), BF16))
    out = pl.pallas_call(
        functools.partial(assemble_kernel, ring, with_vectors),
        out_shape=out_shape,
        in_specs=[pl.BlockSpec(memory_space=pltpu.SMEM)]
        + [pl.BlockSpec(memory_space=pl.ANY)] * (2 * count),
        out_specs=[pl.BlockSpec(memory_space=pl.ANY)]
        + [pl.BlockSpec(memory_space=pltpu.VMEM)] * (2 * with_vectors),
        scratch_shapes=[
            pltpu.VMEM(shape, BF16),
            pltpu.SemaphoreType.DMA((2 * count * groups,)),
            pltpu.SemaphoreType.DMA((2 * count * groups,)),
        ],
        cost_estimate=taking(4),
        compiler_params=params((56 if with_vectors else 8) * 2**20),
        name="assemble",
    )(jnp.stack([core, chip]).astype(jnp.int32), *mine, *theirs)
    whole = out[0].reshape(-1, lanes)
    return (whole,) + (tuple(out[1:]) if with_vectors else (None,))


class Owners:
    def __init__(self, total, side, groups):
        if groups > 1:
            total = lax.psum_scatter(total.astype(BF16), "r", scatter_dimension=0, tiled=True)
        self.side, self.own = side, pick(total[0], side, 0).astype(F32)
        self.trip = Trip(pick(total[0], 1 - side, 0).astype(BF16), "t")

    def by_model(self):
        place = lax.broadcasted_iota(jnp.int32, (2, 1, 1), 0)
        return jnp.where(place == self.side, self.own[None], self.trip.got.astype(F32)[None])


def mixed_kernel(core_ref, left_ref, ctx_ref, dqkv_ref, da_ref, small_ref, send_ref, own_ref):
    at, core = pl.program_id(0), core_ref[0]

    @pl.when(at < 3)
    def _():
        halves_kernel(core, left_ref, dqkv_ref, send_ref, own_ref)

    @pl.when(at == 3)
    def _():
        halves_kernel(core, ctx_ref, da_ref, send_ref, own_ref)

    @pl.when(at == 4)
    def _():
        send_ref[:, :, :LANES] = small_ref[:, 1 - core]
        own_ref[:, :, :LANES] = small_ref[:, core]


def mixed_grad(rows_t, ctx_t, dqkv, da, small, core1, parts):
    size, tokens = rows_t.shape
    run = size // (2 * parts)
    width = da.shape[1]
    small = small.reshape(parts, 2, run, LANES)
    lanes = 4 * width + LANES
    if run % 16:
        full = [dot(rows_t, dqkv), dot(ctx_t, da)]
        full = [f.astype(BF16).reshape(parts, 2, run, -1) for f in full] + [small]
        full = jnp.concatenate(full, axis=-1)
        return pick(full, 1 - core1[0], 1), pick(full, core1[0], 1)
    left = whole_spec((parts, 2, run, tokens))
    half = pl.BlockSpec((parts, run, width), lambda j, _: (0, 0, j))
    return pl.pallas_call(
        mixed_kernel,
        out_shape=[jax.ShapeDtypeStruct((parts, run, lanes), BF16)] * 2,
        grid_spec=pltpu.PrefetchScalarGridSpec(
            num_scalar_prefetch=1,
            grid=(5,),
            in_specs=[
                left,
                left,
                pl.BlockSpec((tokens, width), lambda j, _: (0, jnp.minimum(j, 2))),
                whole_spec(da.shape),
                whole_spec(small.shape),
            ],
            out_specs=[half, half],
        ),
        compiler_params=params(16 * 2**20),
        cost_estimate=taking(8),
        name="attention_gradients",
    )(
        core1,
        rows_t.reshape(parts, 2, run, tokens),
        ctx_t.reshape(parts, 2, run, tokens),
        dqkv,
        da,
        small,
    )


def wide_kernel(core_ref, left_ref, right_ref, send_ref, own_ref):
    out = dot(left_ref[...], right_ref[...], TN).astype(BF16)

    @pl.when(pl.program_id(0) == 0)
    def _():
        send_ref[...] = out.reshape(send_ref.shape)

    @pl.when(pl.program_id(0) == 1)
    def _():
        own_ref[...] = out.reshape(own_ref.shape)


def wide_grad(left, right, core1, parts):
    tokens, size = left.shape
    run = size // (2 * parts)
    n = right.shape[1]
    if run % LANES:
        full = dot(left, right, TN).astype(BF16).reshape(parts, 2, run, n)
        return pick(full, 1 - core1[0], 1), pick(full, core1[0], 1)

    def columns(h, i, core_ref):
        return (0, 2 * i + jnp.where(h == 0, 1 - core_ref[0], core_ref[0]))

    return pl.pallas_call(
        wide_kernel,
        out_shape=[jax.ShapeDtypeStruct((parts, run, n), BF16)] * 2,
        grid_spec=pltpu.PrefetchScalarGridSpec(
            num_scalar_prefetch=1,
            grid=(2, parts),
            in_specs=[pl.BlockSpec((tokens, run), columns), whole_spec((tokens, n))],
            out_specs=[
                pl.BlockSpec((1, run, n), lambda h, i, _: (jnp.where(h == 0, i, parts - 1), 0, 0)),
                pl.BlockSpec((1, run, n), lambda h, i, _: (jnp.where(h == 0, 0, i), 0, 0)),
            ],
        ),
        compiler_params=params(14 * 2**20),
        cost_estimate=taking(5),
        name="down_gradient",
    )(core1, left, right)


def places(tags, model):
    member = tags[:, 0] == model
    count = member.shape[0]
    before = lax.broadcasted_iota(jnp.int32, (count, count), 0) < lax.broadcasted_iota(
        jnp.int32, (count, count), 1
    )
    ranking = jnp.sum(jnp.where(before & member[:, None], 1, 0), axis=0)
    slots = lax.broadcasted_iota(jnp.int32, (CAP, count), 0)
    return (slots == ranking[None, :]) & member[None, :]


def route(chosen, chains):
    marked = jnp.where(chosen[:, :, None, None], chains[None], jnp.zeros((), chains.dtype))
    return jnp.sum(marked.astype(F32), axis=1).astype(chains.dtype)


def body(ring, groups, *args):
    (
        inputs,
        cotangent,
        lengths,
        tags,
        query_weight,
        query_bias,
        key_weight,
        value_weight,
        value_bias,
        output_projection_weight,
        out_bias,
        first_gain,
        first_shift,
        up_weight,
        up_bias,
        down_weight,
        down_bias,
        second_gain,
        second_shift,
    ) = args
    side, core = lax.axis_index("t"), lax.axis_index("core")
    core1 = core.astype(jnp.int32)[None]
    chains = lengths.shape[0]
    width = inputs.shape[1]
    ff = up_weight.shape[2]
    slots = inputs.shape[0] // chains
    tokens = 2 * CAP * slots
    parts = 2 * groups

    own_a, send_a = pack(
        (query_weight, key_weight, value_weight, output_projection_weight),
        (
            query_bias,
            value_bias,
            out_bias,
            first_gain,
            first_shift,
            down_bias,
            second_gain,
            second_shift,
        ),
        up_bias,
        side,
    )
    block_a = two_sides(own_a, swap(send_a, "t"), side, groups)

    own_places, other_places = places(tags, side), places(tags, 1 - side)
    own_len = jnp.sum(jnp.where(own_places, lengths[None, :], 0), axis=1)
    other_len = jnp.sum(jnp.where(other_places, lengths[None, :], 0), axis=1)
    chain_rows = inputs.reshape(chains, slots, width)
    sent_lens = jnp.broadcast_to(other_len[:, None, None], (CAP, 16, width)).astype(BF16)
    sent = jnp.concatenate([route(other_places, chain_rows), sent_lens], axis=1)

    def other_side(weight):
        return Trip(pick(weight, 1 - side, 0), "t")

    def joined(weight, trip):
        return two_sides(pick(weight, side, 0), trip.got, side, groups)

    ring_a, trip = Gather(ring, block_a), other_side(up_weight)
    message = slot([ring_a, trip], lambda now: tie(now, sent)[1])
    ring_u = Gather(ring, joined(up_weight, trip))
    down_weight = slot([ring_a], lambda now: tie(now, down_weight)[1])
    trip_rows, trip = Trip(message, "t"), other_side(down_weight)
    slot([ring_a, ring_u, trip_rows])

    def make_rows(now):
        _, got, cots = tie(now, trip_rows.got, cotangent.reshape(chains, slots, width))
        rows = jnp.concatenate([route(own_places, chain_rows), got[:, :slots]], axis=0)
        lens = jnp.concatenate([own_len, got[:, slots, 0].astype(jnp.int32)])
        return rows.reshape(tokens, width), lens, route(other_places, cots), cots

    rows_in, lens, other_cot, cot_rows = slot([ring_a, ring_u, trip], make_rows)
    ring_d, trip_cot = Gather(ring, joined(down_weight, trip)), Trip(other_cot, "t")
    for _ in range(ring.long - 4):
        slot([ring_a, ring_u, ring_d])

    def join_attention(now):
        _, blocks, rows = tie(now, ring_a.blocks(), rows_in)
        whole, small, out_part = assemble(ring, *blocks, core, True)
        return Kept((small, turned(rows)), whole, out_part)

    (vectors, rows_t), whole_a, out_weight = slot([ring_u, ring_d, trip_cot], join_attention)

    def do_attention(now):
        _, counts = tie(now, lens)
        out = attention(rows_in, counts, whole_a, vectors)
        return Kept(out[2], *out[:2], *out[3:])

    root1, qkv, unit1, low1, ctx_t, low_t = slot([ring_u, ring_d], do_attention)

    def join_up(now):
        _, blocks, own, other = tie(now, ring_u.blocks(), cot_rows, trip_cot.got)
        cot = jnp.concatenate([route(own_places, own), other], axis=0)
        return assemble(ring, *blocks, core)[0], cot.reshape(tokens, width)

    whole_u, cot = slot([ring_d], join_up)

    def do_up(now):
        _, rows = tie(now, low1)
        return up_and_gelu(rows, whole_u, whole_a)

    active, slope = slot([ring_d], do_up)
    whole_d, _ = assemble(ring, *ring_d.blocks(), core)
    gain1 = vectors[3:4]

    result, df, down_sums = down_and_norm(active, whole_d, unit1, cot, vectors)

    origins = ring.origins(core, lax.axis_index("f"))

    def blocks_of(half):
        return half.reshape(groups, 2, ring.count, -1, half.shape[-1])

    def scatter(own, arrived):
        return Scatter(ring, blocks_of(own), blocks_of(arrived), origins)

    send_d, own_d = wide_grad(active, df, core1, parts)
    trip = Trip(send_d, "core")

    def do_feed_back(now):
        _, rows = tie(now, vectors)
        out = feed_back(df, whole_d, slope, whole_u, low_t, unit1, root1, rows, core1, parts)
        return Kept(out[3:], *out[:3])

    (bias_sums, back_sums), send_u, own_u, da = slot([trip], do_feed_back)
    ring_d = scatter(own_d, trip.got)

    def do_attention_back(now):
        _, counts = tie(now, lens)
        out = attention_back(qkv, da, out_weight, counts)
        return Kept(out[1], out[0])

    def second_half(values):
        return values.reshape(2, CAP, slots, width)[1]

    trip, trip_result = Trip(send_u, "core"), Trip(second_half(tie(result, back_sums)[0]), "t")
    qkv_sums, dqkv = slot([ring_d, trip, trip_result], do_attention_back)
    ring_u = scatter(own_u, trip.got)

    def attention_grads(now):
        _, sums, place = tie(now, qkv_sums, core1)
        small = small_grads(down_sums, back_sums, bias_sums, sums)
        return mixed_grad(rows_t, ctx_t, dqkv, da, small, place, parts)

    send_a, own_a = slot([ring_d, ring_u], attention_grads)
    def do_rows(now):
        _, base = tie(now, da)
        rows = (base.astype(F32) + dot(dqkv, whole_a[:, : 3 * width], NT)).astype(BF16)
        return rows, second_half(rows)

    trip = Trip(send_a, "core")
    rows_grad, rows = slot([ring_d, ring_u, trip], do_rows)
    trip_rows = Trip(rows, "t")
    to_home = jnp.concatenate([own_places, other_places], axis=0).T

    def home(values, back):
        both = jnp.concatenate([values.reshape(2, CAP, slots, width)[0], back], axis=0)
        return route(to_home, both).reshape(-1, width)

    def outputs(now):
        _, values, back = tie(now, result, trip_result.got)
        return home(values, back)

    output = slot([ring_d, ring_u, trip_rows], outputs)
    for _ in range(ring.long - 4):
        slot([ring_d, ring_u])
    ring_a = scatter(own_a, trip.got)
    owners_d = Owners(ring_d.total, side, groups)

    def input_grads(now):
        _, values, back = tie(now, rows_grad, trip_rows.got)
        return home(values, back)

    input_grad = slot([ring_u, ring_a, owners_d.trip], input_grads)
    owners_u = Owners(ring_u.total, side, groups)
    grads_d = slot([ring_a, owners_u.trip], lambda now: owners_d.by_model())
    grads_u = slot([ring_a], lambda now: owners_u.by_model())
    for _ in range(ring.long - 3):
        slot([ring_a])

    owners_a = Owners(ring_a.total, side, groups)
    slot([owners_a.trip])
    grads_a = owners_a.by_model()
    columns = jnp.swapaxes(grads_a[:, :, 4 * width : 4 * width + 16], 1, 2)
    return (
        output,
        input_grad,
        grads_a[:, :, :width],
        columns[:, 0],
        grads_a[:, :, width : 2 * width],
        grads_a[:, :, 2 * width : 3 * width],
        columns[:, 1],
        grads_a[:, :, 3 * width : 4 * width],
        columns[:, 2],
        columns[:, 3],
        columns[:, 4],
        grads_u,
        jnp.swapaxes(columns[:, 8:12], 1, 2).reshape(2, -1),
        grads_d,
        columns[:, 5],
        columns[:, 6],
        columns[:, 7],
    )


def solution(mesh):
    dp, fsdp = mesh.shape["dp"], mesh.shape["fsdp"]
    groups = dp // 4
    inner = Mesh(mesh.devices.reshape(groups, 2, 2, fsdp), ("r", "t", "core", "f"))
    every = ("r", "t", "core", "f")
    rows, vector, matrix = P(every, None), P(None, every), P(None, every, None)
    weights = (
        matrix,
        vector,
        matrix,
        matrix,
        vector,
        matrix,
        vector,
        vector,
        vector,
        matrix,
        vector,
        matrix,
        vector,
        vector,
        vector,
    )
    return jax.shard_map(
        functools.partial(body, Ring(fsdp), groups),
        mesh=inner,
        in_specs=(rows, rows, P(every), rows) + weights,
        out_specs=(rows, rows) + weights,
        check_vma=False,
    )
```

```python
import functools

import jax
import jax.numpy as jnp
import numpy as np
from jax import lax
from jax.experimental import pallas as pl
from jax.experimental.pallas import tpu as pltpu
from jax.sharding import Mesh
from jax.sharding import PartitionSpec as P

HEADS = 12
HEAD_DIM = 64
CAP = 3
MIN_LEN = 96
LANES = 128
PAIRS = 3
BF16 = jnp.bfloat16
F32 = jnp.float32
NN = (((1,), (0,)), ((), ()))
NT = (((1,), (1,)), ((), ()))
TN = (((0,), (0,)), ((), ()))
SWAP = [(0, 1), (1, 0)]
VMEM_LIMIT = 56 * 2**20
VMEM_MOST = 56 * 2**20
SMALL = 12


def dot(a, b, dims=NN):
    return lax.dot_general(a, b, dims, preferred_element_type=F32)


def tie(*values):
    return lax.optimization_barrier(values)


def params(limit=VMEM_LIMIT):
    return pltpu.CompilerParams(vmem_limit_bytes=limit)


def taking(micros):
    return pl.CostEstimate(flops=int(micros * 1.1e9), bytes_accessed=1, transcendentals=0)


def whole_spec(shape):
    return pl.BlockSpec(shape, lambda *_: (0,) * len(shape), pipeline_mode=pl.Buffered(1))


def fixed(shape):
    return pl.BlockSpec(shape, lambda *_: (0,) * len(shape))


def head_masks(value=1.0):
    lane = lax.broadcasted_iota(jnp.int32, (1, LANES), 1)
    first = jnp.where(lane < HEAD_DIM, value, 0.0).astype(BF16)
    second = jnp.where(lane >= HEAD_DIM, value, 0.0).astype(BF16)
    return first, second


def stacked(two_heads, masks):
    return jnp.concatenate([two_heads * masks[0], two_heads * masks[1]], axis=0)


def side_by_side(rows):
    half = rows.shape[0] // 2
    return jnp.concatenate([rows[:half], rows[half:]], axis=1)


def probs_of(scores, length):
    keys = scores.shape[0] // 2
    scores = scores.reshape(2, keys, scores.shape[1])
    rest = scores[:, MIN_LEN:]
    slot = lax.broadcasted_iota(jnp.int32, rest.shape, 1) + MIN_LEN
    rest = jnp.where(slot < length, rest, -1000000000.0)
    scores = jnp.concatenate([scores[:, :MIN_LEN], rest], axis=1)
    exponent = jnp.exp(scores - jnp.max(scores, axis=1, keepdims=True))
    return exponent * (1.0 / jnp.sum(exponent, axis=1, keepdims=True))


def as_rows(probs):
    return probs.astype(BF16).reshape(-1, probs.shape[-1])


def in_groups(width, pairs):
    starts = list(range(0, width, LANES))
    return [starts[i : i + pairs] for i in range(0, len(starts), pairs)]


def attention_rows(length, qkv_ref, ctx_ref, base, rows, width):
    masks, scaled = head_masks(), head_masks(HEAD_DIM**-0.5)
    at = slice(base, base + rows)

    def part(index, start):
        return qkv_ref[at, index * width + start : index * width + start + LANES]

    for starts in in_groups(width, 1):
        scores = [dot(stacked(part(1, s), scaled), part(0, s), NT) for s in starts]
        probs = [as_rows(probs_of(s, length)) for s in scores]
        for start, low in zip(starts, probs):
            context = dot(low, stacked(part(2, start), masks), TN)
            ctx_ref[at, start : start + LANES] = context.astype(BF16)


def attention_kernel(
    lens_ref,
    rows_ref,
    weight_ref,
    vec_ref,
    qkv_ref,
    unit_ref,
    root_ref,
    low_ref,
    ctx_t_ref,
    low_t_ref,
    ctx_ref,
):
    width = ctx_ref.shape[1]
    rows = qkv_ref.shape[0] // 2
    for part in range(3):
        columns = slice(part * width, (part + 1) * width)
        product = dot(rows_ref[...], weight_ref[:, columns])
        if part != 1:
            product = product + vec_ref[part // 2 : part // 2 + 1, :]
        qkv_ref[:, columns] = product.astype(BF16)
    for chain in range(2):
        length = lens_ref[2 * pl.program_id(0) + chain]
        attention_rows(length, qkv_ref, ctx_ref, chain * rows, rows, width)
    branch = dot(ctx_ref[...], weight_ref[:, 3 * width : 4 * width]) + vec_ref[2:3, :]
    unit, root = normed(rows_ref[...].astype(F32) + branch)
    unit_ref[...] = unit.astype(BF16)
    root_ref[...] = root
    low = (unit * vec_ref[3:4, :] + vec_ref[4:5, :]).astype(BF16)
    low_ref[...] = low
    low_t_ref[...] = low.T
    ctx_t_ref[...] = ctx_ref[...].T


def turn_kernel(rows_ref, out_ref):
    out_ref[...] = rows_ref[...].T


def turned(rows):
    return pl.pallas_call(
        turn_kernel,
        out_shape=jax.ShapeDtypeStruct(rows.shape[::-1], rows.dtype),
        compiler_params=params(12 * 2**20),
        cost_estimate=taking(2),
        name="turn_rows",
    )(rows)


def attention(rows_in, lens, whole_a, vectors):
    total, width = rows_in.shape
    rows = 2 * total // lens.shape[0]

    def tokens(lanes):
        return pl.BlockSpec((rows, lanes), lambda i, _: (i, 0))

    return pl.pallas_call(
        attention_kernel,
        out_shape=[
            jax.ShapeDtypeStruct((total, 3 * width), BF16),
            jax.ShapeDtypeStruct((total, width), BF16),
            jax.ShapeDtypeStruct((total, 1), F32),
            jax.ShapeDtypeStruct((total, width), BF16),
        ]
        + [jax.ShapeDtypeStruct((width, total), BF16)] * 2,
        grid_spec=pltpu.PrefetchScalarGridSpec(
            num_scalar_prefetch=1,
            grid=(total // rows,),
            in_specs=[tokens(width), whole_spec(whole_a.shape), whole_spec(vectors.shape)],
            out_specs=[tokens(3 * width), tokens(width), tokens(1), tokens(width)]
            + [pl.BlockSpec((width, rows), lambda i, _: (0, i))] * 2,
            scratch_shapes=[pltpu.VMEM((rows, width), BF16)],
        ),
        compiler_params=params(20 * 2**20),
        cost_estimate=taking(14),
        name="attention_forward",
    )(lens, rows_in, whole_a, vectors)


def attention_back_kernel(lens_ref, qkv_ref, da_ref, out_weight_ref, dqkv_ref, sum_ref):
    width = da_ref.shape[1]
    length = lens_ref[pl.program_id(0)]
    masks, scaled = head_masks(), head_masks(HEAD_DIM**-0.5)
    dctx = dot(da_ref[...], out_weight_ref[...], NT).astype(BF16)

    @pl.when(pl.program_id(0) == 0)
    def _():
        sum_ref[...] = jnp.zeros_like(sum_ref)

    def store(column, value):
        low = value.astype(BF16)
        dqkv_ref[:, column : column + LANES] = low
        sum_ref[:, column : column + LANES] += jnp.sum(low.astype(F32), axis=0, keepdims=True)

    def part(index, start):
        return qkv_ref[:, index * width + start : index * width + start + LANES]

    for starts in in_groups(width, PAIRS):
        queries = [part(0, s) for s in starts]
        keys = [stacked(part(1, s), scaled) for s in starts]
        grads = [dctx[:, s : s + LANES] for s in starts]
        scores = [dot(k, q, NT) for k, q in zip(keys, queries)]
        dprobs = [dot(stacked(part(2, s), masks), d, NT) for s, d in zip(starts, grads)]
        probs = [probs_of(s, length) for s in scores]
        dprobs = [d.reshape(p.shape) for d, p in zip(dprobs, probs)]
        dscores = [
            as_rows(p * (d - jnp.sum(d * p, axis=1, keepdims=True)))
            for p, d in zip(probs, dprobs)
        ]
        for start, p, d in zip(starts, probs, grads):
            store(2 * width + start, dot(side_by_side(as_rows(p)), stacked(d, masks)))
        for start, d, q in zip(starts, dscores, queries):
            store(width + start, dot(side_by_side(d), stacked(q, scaled)))
        for start, d, k in zip(starts, dscores, keys):
            store(start, dot(d, k, TN))


def attention_back(qkv, da, out_weight, lens):
    total, width = da.shape
    rows = total // lens.shape[0]

    def tokens(lanes):
        return pl.BlockSpec((rows, lanes), lambda i, _: (i, 0))

    return pl.pallas_call(
        attention_back_kernel,
        out_shape=[
            jax.ShapeDtypeStruct((total, 3 * width), BF16),
            jax.ShapeDtypeStruct((1, 3 * width), F32),
        ],
        grid_spec=pltpu.PrefetchScalarGridSpec(
            num_scalar_prefetch=1,
            grid=(lens.shape[0],),
            in_specs=[tokens(3 * width), tokens(width), whole_spec((width, width))],
            out_specs=[tokens(3 * width), fixed((1, 3 * width))],
        ),
        compiler_params=params(12 * 2**20),
        cost_estimate=taking(11),
        name="attention_backward",
    )(lens, qkv, da, out_weight)


def up_kernel(low_ref, up_ref, small_ref, active_ref, slope_ref):
    weight = up_ref[...]
    block = weight.shape[1]
    rows = small_ref.shape[0]
    fold = block // rows
    column = lax.broadcasted_iota(jnp.int32, (LANES, block), 0)
    lane = lax.broadcasted_iota(jnp.int32, (LANES, block), 1)
    spread = (column == SMALL - 4 + lane % fold).astype(F32).astype(BF16)
    row = lax.broadcasted_iota(jnp.int32, (rows, block), 0)
    at = lax.broadcasted_iota(jnp.int32, (rows, block), 1)
    bias = jnp.sum(
        jnp.where(at // fold == row, dot(small_ref[...], spread), 0.0), axis=0, keepdims=True
    )
    step = LANES
    for start in range(0, low_ref.shape[0], step):
        hidden = dot(low_ref[start : start + step, :], weight) + bias
        cdf = 0.5 * (1.0 + lax.erf(hidden * (2.0**-0.5)))
        active_ref[start : start + step, :] = (hidden * cdf).astype(BF16)
        density = jnp.exp(-0.5 * hidden * hidden) * ((2.0 * np.pi) ** -0.5)
        slope_ref[start : start + step, :] = (cdf + hidden * density).astype(BF16)


def up_and_gelu(low, up, whole_a):
    rows, width = low.shape
    ff = up.shape[1]
    block = 512
    return pl.pallas_call(
        up_kernel,
        out_shape=[jax.ShapeDtypeStruct((rows, ff), BF16)] * 2,
        grid=(ff // block,),
        in_specs=[
            whole_spec((rows, width)),
            pl.BlockSpec((width, block), lambda i: (0, i)),
            pl.BlockSpec(
                (width * block // ff, LANES), lambda i: (i, whole_a.shape[1] // LANES - 1)
            ),
        ],
        out_specs=[pl.BlockSpec((rows, block), lambda i: (0, i))] * 2,
        cost_estimate=taking(10),
        compiler_params=params(12 * 2**20),
        name="up_gelu",
    )(low, up, whole_a)


def down_kernel(
    active_ref, down_ref, unit_ref, cot_ref, vec_ref, out_ref, df_ref, sum_ref
):
    @pl.when(pl.program_id(0) == 0)
    def _():
        sum_ref[...] = jnp.zeros_like(sum_ref)

    bias, gain, shift = vec_ref[5:6, :], vec_ref[6:7, :], vec_ref[7:8, :]
    hidden = unit_ref[...].astype(F32) * vec_ref[3:4, :] + vec_ref[4:5, :]
    total = hidden + dot(active_ref[...], down_ref[...]) + bias
    unit, root = normed(total)
    out_ref[...] = (unit * gain + shift).astype(BF16)
    grad = cot_ref[...].astype(F32)
    df = norm_back(grad, unit, root, gain).astype(BF16)
    df_ref[...] = df
    sum_ref[0:1, :] += jnp.sum(df.astype(F32), axis=0, keepdims=True)
    sum_ref[1:2, :] += jnp.sum(grad * unit, axis=0, keepdims=True)
    sum_ref[2:3, :] += jnp.sum(grad, axis=0, keepdims=True)


def down_and_norm(active, down, unit, cot, vectors):
    rows, ff = active.shape
    width = down.shape[1]
    block = 256
    tokens = pl.BlockSpec((block, width), lambda i: (i, 0))
    return pl.pallas_call(
        down_kernel,
        out_shape=[
            jax.ShapeDtypeStruct((rows, width), BF16),
            jax.ShapeDtypeStruct((rows, width), BF16),
            jax.ShapeDtypeStruct((8, width), F32),
        ],
        grid=(rows // block,),
        in_specs=[
            pl.BlockSpec((block, ff), lambda i: (i, 0)),
            whole_spec((ff, width)),
            tokens,
            tokens,
            whole_spec(vectors.shape),
        ],
        out_specs=[tokens, tokens, fixed((8, width))],
        compiler_params=params(18 * 2**20),
        cost_estimate=taking(10),
        name="down_norm",
    )(active, down, unit, cot, vectors)


def back_kernel(
    core_ref,
    df_ref,
    down_ref,
    slope_ref,
    up_ref,
    low_t_ref,
    unit_ref,
    root_ref,
    vec_ref,
    send_ref,
    own_ref,
    da_ref,
    bias_ref,
    sum_ref,
    total,
    grad,
):
    at = pl.program_id(0)
    step = 384

    @pl.when(at == 0)
    def _():
        total[...] = df_ref[...].astype(F32)
        sum_ref[...] = jnp.zeros_like(sum_ref)

    bias = jnp.zeros(bias_ref.shape, F32)
    for start in range(0, df_ref.shape[0], step):
        rows = slice(start, start + step)
        du = dot(df_ref[rows, :], down_ref[...], NT) * slope_ref[rows, :].astype(F32)
        du = du.astype(BF16)
        grad[rows, :] = du
        bias += jnp.sum(du.astype(F32), axis=0, keepdims=True)
        total[rows, :] += dot(du, up_ref[...], NT)
    bias_ref[...] = bias
    halves_kernel(core_ref[0], low_t_ref, grad, send_ref, own_ref)

    @pl.when(at == pl.num_programs(0) - 1)
    def _():
        for start in range(0, df_ref.shape[0], step):
            rows = slice(start, start + step)
            dh1, unit = total[rows, :], unit_ref[rows, :].astype(F32)
            da = norm_back(dh1, unit, root_ref[rows, :], vec_ref[3:4, :]).astype(BF16)
            da_ref[rows, :] = da
            sum_ref[0:1, :] += jnp.sum(da.astype(F32), axis=0, keepdims=True)
            sum_ref[1:2, :] += jnp.sum(dh1 * unit, axis=0, keepdims=True)
            sum_ref[2:3, :] += jnp.sum(dh1, axis=0, keepdims=True)


def halves_kernel(core, left_ref, right_ref, send_ref, own_ref):
    parts, _, run, tokens = left_ref.shape
    for half, out_ref in ((1 - core, send_ref), (core, own_ref)):
        left = left_ref[:, half].reshape(parts * run, tokens)
        out_ref[...] = dot(left, right_ref[...]).astype(BF16).reshape(out_ref.shape)


def feed_back(df, down, slope, up, low_t, unit, root, vectors, core1, parts):
    rows, width = df.shape
    ff = up.shape[1]
    block = 768
    run = width // (2 * parts)
    tokens = whole_spec((rows, width))
    half = pl.BlockSpec((parts, run, block), lambda i, _: (0, 0, i))
    return pl.pallas_call(
        back_kernel,
        out_shape=[
            jax.ShapeDtypeStruct((parts, run, ff), BF16),
            jax.ShapeDtypeStruct((parts, run, ff), BF16),
            jax.ShapeDtypeStruct((rows, width), BF16),
            jax.ShapeDtypeStruct((1, ff), F32),
            jax.ShapeDtypeStruct((8, width), F32),
        ],
        grid_spec=pltpu.PrefetchScalarGridSpec(
            num_scalar_prefetch=1,
            grid=(ff // block,),
            in_specs=[
                tokens,
                pl.BlockSpec((block, width), lambda i, _: (i, 0)),
                pl.BlockSpec((rows, block), lambda i, _: (0, i)),
                pl.BlockSpec((width, block), lambda i, _: (0, i)),
                whole_spec((parts, 2, run, rows)),
                tokens,
                whole_spec(root.shape),
                whole_spec(vectors.shape),
            ],
            out_specs=[
                half,
                half,
                fixed((rows, width)),
                pl.BlockSpec((1, block), lambda i, _: (0, i)),
                fixed((8, width)),
            ],
            scratch_shapes=[pltpu.VMEM((rows, width), F32), pltpu.VMEM((rows, block), BF16)],
        ),
        compiler_params=params(30 * 2**20),
        cost_estimate=taking(21),
        name="feed_forward_back",
    )(core1, df, down, slope, up, low_t.reshape(parts, 2, run, rows), unit, root, vectors)


def normed(values):
    centre = values - jnp.mean(values, axis=-1, keepdims=True)
    root = lax.rsqrt(jnp.mean(centre * centre, axis=-1, keepdims=True) + 1e-05)
    return centre * root, root


def norm_back(grad, unit, root, gain):
    scaled = grad * gain
    inner = jnp.mean(scaled * unit, axis=-1, keepdims=True)
    return root * (scaled - jnp.mean(scaled, axis=-1, keepdims=True) - unit * inner)


def transposed_rows(vectors):
    count, size = vectors.shape
    padded = jnp.concatenate([vectors, jnp.zeros((LANES - count, size), vectors.dtype)], axis=0)
    row = lax.broadcasted_iota(jnp.int32, (size, size), 0)
    column = lax.broadcasted_iota(jnp.int32, (size, size), 1)
    unit = (row == column).astype(F32).astype(BF16)
    return dot(unit, padded.astype(BF16), NT)


def folded(values, rows):
    size = values.shape[1]
    fold = size // rows
    row = lax.broadcasted_iota(jnp.int32, (rows, size), 0)
    at = lax.broadcasted_iota(jnp.int32, (rows, size), 1)
    spread = jnp.where(at // fold == row, values.astype(F32), 0.0).astype(BF16)
    column = lax.broadcasted_iota(jnp.int32, (LANES, size), 0)
    lane = lax.broadcasted_iota(jnp.int32, (LANES, size), 1)
    place = (column == SMALL - 4 + lane % fold).astype(F32).astype(BF16)
    return dot(spread, place, NT)


def pack_kernel(side_ref, *refs):
    matrices, vectors, up_bias_ref = refs[:4], refs[4:12], refs[12]
    rows = refs[13].shape[0]
    for model, out_ref in ((side_ref[0], refs[13]), (1 - side_ref[0], refs[14])):

        def row(vector):
            both = vector[...].astype(F32)
            return jnp.where(model == 0, both[0:1, :], both[1:2, :])

        start = 0
        for matrix in matrices:
            out_ref[:, start : start + matrix.shape[2]] = matrix[model]
            start += matrix.shape[2]
        eight = jnp.concatenate([row(v) for v in vectors], axis=0)
        small = transposed_rows(eight) + folded(row(up_bias_ref), rows)
        out_ref[:, start:] = small.astype(BF16)


def pack(matrices, vectors, up_bias, side):
    models, rows, _ = matrices[0].shape
    lanes = sum(m.shape[2] for m in matrices) + LANES
    if rows % 8:
        parts = [v[..., None] for v in vectors] + [up_bias.reshape(models, rows, -1)]
        small = jnp.concatenate(parts, axis=-1)
        small = jnp.pad(small, [(0, 0), (0, 0), (0, LANES - small.shape[-1])])
        both = jnp.concatenate(list(matrices) + [small], axis=-1)
        return pick(both, side, 0), pick(both, 1 - side, 0)
    return pl.pallas_call(
        pack_kernel,
        out_shape=[jax.ShapeDtypeStruct((rows, lanes), BF16)] * 2,
        in_specs=[pl.BlockSpec(memory_space=pltpu.SMEM)]
        + [pl.BlockSpec(memory_space=pltpu.VMEM)] * 13,
        compiler_params=params(VMEM_MOST),
        name="pack_shard",
    )(side.astype(jnp.int32)[None], *matrices, *vectors, up_bias)


def small_grads_kernel(down_ref, back_ref, bias_ref, qkv_ref, out_ref):
    rows = out_ref.shape[0]
    width = down_ref.shape[1]
    eight = jnp.concatenate(
        [
            qkv_ref[:, :width],
            qkv_ref[:, 2 * width :],
            back_ref[0:3, :],
            down_ref[0:3, :],
        ],
        axis=0,
    )
    out_ref[...] = transposed_rows(eight).astype(BF16)
    step = LANES
    fold = bias_ref.shape[1] // rows
    for start in range(0, rows, step):
        values = bias_ref[:, start * fold : (start + step) * fold]
        here = slice(start, start + step)
        out_ref[here, :] = (out_ref[here, :].astype(F32) + folded(values, step)).astype(BF16)


def small_grads(down_sums, back_sums, bias_sums, qkv_sums):
    width = down_sums.shape[1]
    return pl.pallas_call(
        small_grads_kernel,
        out_shape=jax.ShapeDtypeStruct((width, LANES), BF16),
        compiler_params=params(8 * 2**20),
        name="small_gradients",
    )(down_sums, back_sums, bias_sums, qkv_sums)


class Ring:
    def __init__(self, count):
        depth = 4 if count % 4 == 0 else 2
        wide = count // depth
        order = []
        if wide > 1:
            for z in range(depth):
                ys = range(1, wide) if z % 2 == 0 else reversed(range(1, wide))
                order += [z * wide + y for y in ys]
            order += [z * wide for z in reversed(range(depth))]
        else:
            order = list(range(count))
        self.count, self.depth, self.wide = count, depth, wide
        self.long = count // 2
        self.short = count - 1 - self.long
        self.ahead, self.behind = [], []
        for core in range(2):
            sign = 1 if core == 0 else -1
            here = core * count
            for place, chip in enumerate(order):
                self.ahead.append((here + chip, here + order[(place + sign) % count]))
                self.behind.append((here + chip, here + order[(place - sign) % count]))

    def origins(self, core, chip):
        depth, turn = self.depth, self.wide - 1
        if turn == 0:
            place = chip
        else:
            z, y = lax.div(chip, self.wide), lax.rem(chip, self.wide)
            along = jnp.where(lax.rem(z, 2) == 0, y - 1, turn - y)
            place = jnp.where(y == 0, depth * turn + depth - 1 - z, z * turn + along)
        sign = 1 - 2 * core
        chips = []
        for k in range(self.count):
            off = -k if k <= self.long else k - self.long
            at = lax.rem(place + sign * off + self.count, self.count)
            if turn > 0:
                z, j = lax.div(at, turn), lax.rem(at, turn)
                y = jnp.where(lax.rem(z, 2) == 0, 1 + j, turn - j)
                at = jnp.where(
                    at < depth * turn, z * self.wide + y, (depth * (turn + 1) - 1 - at) * self.wide
                )
            chips.append(at)
        return chips

    def forth(self, block):
        return lax.ppermute(block, ("core", "f"), self.ahead)

    def back(self, block):
        return lax.ppermute(block, ("core", "f"), self.behind)


def swap(value, axis):
    return lax.ppermute(value, axis, SWAP)


def pick(value, index, axis):
    return lax.dynamic_index_in_dim(value, index, axis, keepdims=False)


def two_sides(own, other, side, groups):
    place = lax.broadcasted_iota(jnp.int32, (2, 1, 1), 0)
    block = jnp.where(place == side, own[None], other[None])
    if groups > 1:
        return lax.all_gather(block, "r", axis=0, tiled=False)
    return block[None]


class Gather:
    def __init__(self, ring, block):
        self.ring, self.step = ring, 0
        self.forth, self.back = [block], [block]
        self.theirs_forth, self.theirs_back = [swap(block, "core")], []

    def launch(self):
        self.step += 1
        sent = [self.ring.forth(self.forth[-1])]
        if self.step <= self.ring.short:
            sent.append(self.ring.back(self.back[-1]))
        return sent

    def now(self):
        return self.forth[-1]

    def land(self, sent):
        self.forth.append(sent[0])
        self.theirs_forth.append(swap(sent[0], "core"))
        if len(sent) > 1:
            self.back.append(sent[1])
            self.theirs_back.append(swap(sent[1], "core"))

    def settle(self, values):
        for kept, value in zip((self.theirs_forth, self.theirs_back), values):
            kept[:] = value

    def blocks(self):
        return self.forth + self.back[1:], self.theirs_forth + self.theirs_back


class Scatter:
    def __init__(self, ring, own, other, origins):
        self.ring, self.step = ring, 0
        self.own, self.other, self.origins = own, other, origins
        self.far = self.term(ring.long).astype(BF16)
        self.near = self.term(ring.long + ring.short).astype(BF16)
        self.total = None

    def term(self, k):
        a, b = pick(self.own, self.origins[k], 2), pick(self.other, self.origins[k], 2)
        return a.astype(F32) + b.astype(F32)

    def launch(self):
        self.step += 1
        sent = [self.ring.back(self.far)]
        if self.step > self.ring.long - self.ring.short:
            sent.append(self.ring.forth(self.near))
        return sent

    def now(self):
        return self.far

    def land(self, sent):
        left = self.ring.long - self.step
        if left:
            self.far = (sent[0].astype(F32) + self.term(left)).astype(BF16)
            if len(sent) > 1:
                near = sent[1].astype(F32) + self.term(self.ring.long + left)
                self.near = near.astype(BF16)
        else:
            self.total = sent[0].astype(F32) + sent[1].astype(F32) + self.term(0)


class Trip:
    def __init__(self, value, axis):
        self.value, self.axis, self.got = value, axis, None

    def launch(self):
        return [swap(self.value, self.axis)]

    def now(self):
        return self.value

    def land(self, sent):
        self.got = sent[0]


class Kept:
    def __init__(self, small, *rest):
        self.small, self.rest = small, rest


def slot(movers, work=None):
    now = [m.now() for m in movers]
    sent = [m.launch() for m in movers]
    gathers = [m for m in movers if isinstance(m, Gather)]
    before = [(m.theirs_forth, m.theirs_back) for m in gathers]
    done = None if work is None else work((now, before))
    if isinstance(done, Kept):
        kept, done = done.rest, done.small
    else:
        kept = None
    sent, done, before = tie(sent, done, before)
    for mover, settled in zip(gathers, before):
        mover.settle(settled)
    for mover, arrived in zip(movers, sent):
        mover.land(arrived)
    return done if kept is None else (done,) + tuple(kept)


def assemble_kernel(ring, with_vectors, at_ref, *refs):
    count = ring.count
    blocks, out_ref = refs[: 2 * count], refs[2 * count]
    held, sems_in, sems_out = refs[-3:]
    core, chip = at_ref[0], at_ref[1]
    here, there = ring.origins(core, chip), ring.origins(1 - core, chip)
    incoming, outgoing = [], []
    for i, (block, at) in enumerate(zip(blocks, here + there)):
        half = core if i < count else 1 - core
        for r in range(block.shape[0]):
            inside, outside = held.at[r, :, half, at], out_ref.at[r, :, half, at]
            n = len(incoming)
            incoming.append(pltpu.make_async_copy(block.at[r], inside, sems_in.at[n]))
            outgoing.append(pltpu.make_async_copy(inside, outside, sems_out.at[n]))
    for copy in incoming:
        copy.start()
    for copy, after in zip(incoming, outgoing):
        copy.wait()
        after.start()
    if with_vectors:
        rows = held[:, :, :, :, :, held.shape[-1] - LANES :]
        small = rows.astype(F32).reshape(-1, LANES)
        refs[2 * count + 1][...] = small.T[:16]
        width = refs[2 * count + 2].shape[0]
        output = held[:, :, :, :, :, 3 * width : 4 * width]
        refs[2 * count + 2][...] = output.astype(F32).reshape(-1, width).astype(BF16)
    for copy in outgoing:
        copy.wait()


def assemble(ring, mine, theirs, core, with_vectors=False):
    groups, _, rows, lanes = mine[0].shape
    count = ring.count
    chip = lax.axis_index("f")
    shape = (groups, 2, 2, count, rows, lanes)
    width = shape[1] * shape[2] * groups * count * rows
    if rows % 8:
        whole = jnp.zeros(shape, BF16)
        at = ring.origins(core, chip) + ring.origins(1 - core, chip)
        for i, block in enumerate(mine + theirs):
            half = core if i < count else 1 - core
            where = (0, 0, half, at[i], 0, 0)
            whole = lax.dynamic_update_slice(whole, block[:, :, None, None], where)
        whole = whole.reshape(-1, lanes)
        if not with_vectors:
            return whole, None
        vectors = whole[:, lanes - LANES :].astype(F32).T[:16]
        return whole, vectors, whole[:, 3 * width : 4 * width]
    out_shape = [jax.ShapeDtypeStruct(shape, BF16)]
    if with_vectors:
        out_shape.append(jax.ShapeDtypeStruct((16, width), F32))
        out_shape.append(jax.ShapeDtypeStruct((width, width), BF16))
    out = pl.pallas_call(
        functools.partial(assemble_kernel, ring, with_vectors),
        out_shape=out_shape,
        in_specs=[pl.BlockSpec(memory_space=pltpu.SMEM)]
        + [pl.BlockSpec(memory_space=pl.ANY)] * (2 * count),
        out_specs=[pl.BlockSpec(memory_space=pl.ANY)]
        + [pl.BlockSpec(memory_space=pltpu.VMEM)] * (2 * with_vectors),
        scratch_shapes=[
            pltpu.VMEM(shape, BF16),
            pltpu.SemaphoreType.DMA((2 * count * groups,)),
            pltpu.SemaphoreType.DMA((2 * count * groups,)),
        ],
        cost_estimate=taking(4),
        compiler_params=params((56 if with_vectors else 8) * 2**20),
        name="assemble",
    )(jnp.stack([core, chip]).astype(jnp.int32), *mine, *theirs)
    whole = out[0].reshape(-1, lanes)
    return (whole,) + (tuple(out[1:]) if with_vectors else (None,))


class Owners:
    def __init__(self, total, side, groups):
        if groups > 1:
            total = lax.psum_scatter(total.astype(BF16), "r", scatter_dimension=0, tiled=True)
        self.side, self.own = side, pick(total[0], side, 0).astype(F32)
        self.trip = Trip(pick(total[0], 1 - side, 0).astype(BF16), "t")

    def by_model(self):
        place = lax.broadcasted_iota(jnp.int32, (2, 1, 1), 0)
        return jnp.where(place == self.side, self.own[None], self.trip.got.astype(F32)[None])


def mixed_kernel(core_ref, left_ref, ctx_ref, dqkv_ref, da_ref, small_ref, send_ref, own_ref):
    at, core = pl.program_id(0), core_ref[0]

    @pl.when(at < 3)
    def _():
        halves_kernel(core, left_ref, dqkv_ref, send_ref, own_ref)

    @pl.when(at == 3)
    def _():
        halves_kernel(core, ctx_ref, da_ref, send_ref, own_ref)

    @pl.when(at == 4)
    def _():
        send_ref[:, :, :LANES] = small_ref[:, 1 - core]
        own_ref[:, :, :LANES] = small_ref[:, core]


def mixed_grad(rows_t, ctx_t, dqkv, da, small, core1, parts):
    size, tokens = rows_t.shape
    run = size // (2 * parts)
    width = da.shape[1]
    small = small.reshape(parts, 2, run, LANES)
    lanes = 4 * width + LANES
    if run % 16:
        full = [dot(rows_t, dqkv), dot(ctx_t, da)]
        full = [f.astype(BF16).reshape(parts, 2, run, -1) for f in full] + [small]
        full = jnp.concatenate(full, axis=-1)
        return pick(full, 1 - core1[0], 1), pick(full, core1[0], 1)
    left = whole_spec((parts, 2, run, tokens))
    half = pl.BlockSpec((parts, run, width), lambda j, _: (0, 0, j))
    return pl.pallas_call(
        mixed_kernel,
        out_shape=[jax.ShapeDtypeStruct((parts, run, lanes), BF16)] * 2,
        grid_spec=pltpu.PrefetchScalarGridSpec(
            num_scalar_prefetch=1,
            grid=(5,),
            in_specs=[
                left,
                left,
                pl.BlockSpec((tokens, width), lambda j, _: (0, jnp.minimum(j, 2))),
                whole_spec(da.shape),
                whole_spec(small.shape),
            ],
            out_specs=[half, half],
        ),
        compiler_params=params(16 * 2**20),
        cost_estimate=taking(8),
        name="attention_gradients",
    )(
        core1,
        rows_t.reshape(parts, 2, run, tokens),
        ctx_t.reshape(parts, 2, run, tokens),
        dqkv,
        da,
        small,
    )


def wide_kernel(core_ref, left_ref, right_ref, send_ref, own_ref):
    out = dot(left_ref[...], right_ref[...], TN).astype(BF16)

    @pl.when(pl.program_id(0) == 0)
    def _():
        send_ref[...] = out.reshape(send_ref.shape)

    @pl.when(pl.program_id(0) == 1)
    def _():
        own_ref[...] = out.reshape(own_ref.shape)


def wide_grad(left, right, core1, parts):
    tokens, size = left.shape
    run = size // (2 * parts)
    n = right.shape[1]
    if run % LANES:
        full = dot(left, right, TN).astype(BF16).reshape(parts, 2, run, n)
        return pick(full, 1 - core1[0], 1), pick(full, core1[0], 1)

    def columns(h, i, core_ref):
        return (0, 2 * i + jnp.where(h == 0, 1 - core_ref[0], core_ref[0]))

    return pl.pallas_call(
        wide_kernel,
        out_shape=[jax.ShapeDtypeStruct((parts, run, n), BF16)] * 2,
        grid_spec=pltpu.PrefetchScalarGridSpec(
            num_scalar_prefetch=1,
            grid=(2, parts),
            in_specs=[pl.BlockSpec((tokens, run), columns), whole_spec((tokens, n))],
            out_specs=[
                pl.BlockSpec((1, run, n), lambda h, i, _: (jnp.where(h == 0, i, parts - 1), 0, 0)),
                pl.BlockSpec((1, run, n), lambda h, i, _: (jnp.where(h == 0, 0, i), 0, 0)),
            ],
        ),
        compiler_params=params(14 * 2**20),
        cost_estimate=taking(5),
        name="down_gradient",
    )(core1, left, right)


def places(tags, model):
    member = tags[:, 0] == model
    count = member.shape[0]
    before = lax.broadcasted_iota(jnp.int32, (count, count), 0) < lax.broadcasted_iota(
        jnp.int32, (count, count), 1
    )
    ranking = jnp.sum(jnp.where(before & member[:, None], 1, 0), axis=0)
    slots = lax.broadcasted_iota(jnp.int32, (CAP, count), 0)
    return (slots == ranking[None, :]) & member[None, :]


def route(chosen, chains):
    marked = jnp.where(chosen[:, :, None, None], chains[None], jnp.zeros((), chains.dtype))
    return jnp.sum(marked.astype(F32), axis=1).astype(chains.dtype)


def body(ring, groups, *args):
    (
        inputs,
        cotangent,
        lengths,
        tags,
        query_weight,
        query_bias,
        key_weight,
        value_weight,
        value_bias,
        output_projection_weight,
        out_bias,
        first_gain,
        first_shift,
        up_weight,
        up_bias,
        down_weight,
        down_bias,
        second_gain,
        second_shift,
    ) = args
    side, core = lax.axis_index("t"), lax.axis_index("core")
    core1 = core.astype(jnp.int32)[None]
    chains = lengths.shape[0]
    width = inputs.shape[1]
    ff = up_weight.shape[2]
    slots = inputs.shape[0] // chains
    tokens = 2 * CAP * slots
    parts = 2 * groups

    own_a, send_a = pack(
        (query_weight, key_weight, value_weight, output_projection_weight),
        (
            query_bias,
            value_bias,
            out_bias,
            first_gain,
            first_shift,
            down_bias,
            second_gain,
            second_shift,
        ),
        up_bias,
        side,
    )
    block_a = two_sides(own_a, swap(send_a, "t"), side, groups)

    own_places, other_places = places(tags, side), places(tags, 1 - side)
    own_len = jnp.sum(jnp.where(own_places, lengths[None, :], 0), axis=1)
    other_len = jnp.sum(jnp.where(other_places, lengths[None, :], 0), axis=1)
    chain_rows = inputs.reshape(chains, slots, width)
    sent_lens = jnp.broadcast_to(other_len[:, None, None], (CAP, 16, width)).astype(BF16)
    sent = jnp.concatenate([route(other_places, chain_rows), sent_lens], axis=1)

    def other_side(weight):
        return Trip(pick(weight, 1 - side, 0), "t")

    def joined(weight, trip):
        return two_sides(pick(weight, side, 0), trip.got, side, groups)

    ring_a, trip = Gather(ring, block_a), other_side(up_weight)
    message = slot([ring_a, trip], lambda now: tie(now, sent)[1])
    ring_u = Gather(ring, joined(up_weight, trip))
    down_weight = slot([ring_a], lambda now: tie(now, down_weight)[1])
    trip_rows, trip = Trip(message, "t"), other_side(down_weight)
    slot([ring_a, ring_u, trip_rows])

    def make_rows(now):
        _, got, cots = tie(now, trip_rows.got, cotangent.reshape(chains, slots, width))
        rows = jnp.concatenate([route(own_places, chain_rows), got[:, :slots]], axis=0)
        lens = jnp.concatenate([own_len, got[:, slots, 0].astype(jnp.int32)])
        return rows.reshape(tokens, width), lens, route(other_places, cots), cots

    rows_in, lens, other_cot, cot_rows = slot([ring_a, ring_u, trip], make_rows)
    ring_d, trip_cot = Gather(ring, joined(down_weight, trip)), Trip(other_cot, "t")
    for _ in range(ring.long - 4):
        slot([ring_a, ring_u, ring_d])

    def join_attention(now):
        _, blocks, rows = tie(now, ring_a.blocks(), rows_in)
        whole, small, out_part = assemble(ring, *blocks, core, True)
        return Kept((small, turned(rows)), whole, out_part)

    (vectors, rows_t), whole_a, out_weight = slot([ring_u, ring_d, trip_cot], join_attention)

    def do_attention(now):
        _, counts = tie(now, lens)
        out = attention(rows_in, counts, whole_a, vectors)
        return Kept(out[2], *out[:2], *out[3:])

    root1, qkv, unit1, low1, ctx_t, low_t = slot([ring_u, ring_d], do_attention)

    def join_up(now):
        _, blocks, own, other = tie(now, ring_u.blocks(), cot_rows, trip_cot.got)
        cot = jnp.concatenate([route(own_places, own), other], axis=0)
        return assemble(ring, *blocks, core)[0], cot.reshape(tokens, width)

    whole_u, cot = slot([ring_d], join_up)

    def do_up(now):
        _, rows = tie(now, low1)
        return up_and_gelu(rows, whole_u, whole_a)

    active, slope = slot([ring_d], do_up)
    whole_d, _ = assemble(ring, *ring_d.blocks(), core)
    gain1 = vectors[3:4]

    result, df, down_sums = down_and_norm(active, whole_d, unit1, cot, vectors)

    origins = ring.origins(core, lax.axis_index("f"))

    def blocks_of(half):
        return half.reshape(groups, 2, ring.count, -1, half.shape[-1])

    def scatter(own, arrived):
        return Scatter(ring, blocks_of(own), blocks_of(arrived), origins)

    send_d, own_d = wide_grad(active, df, core1, parts)
    trip = Trip(send_d, "core")

    def do_feed_back(now):
        _, rows = tie(now, vectors)
        out = feed_back(df, whole_d, slope, whole_u, low_t, unit1, root1, rows, core1, parts)
        return Kept(out[3:], *out[:3])

    (bias_sums, back_sums), send_u, own_u, da = slot([trip], do_feed_back)
    ring_d = scatter(own_d, trip.got)

    def do_attention_back(now):
        _, counts = tie(now, lens)
        out = attention_back(qkv, da, out_weight, counts)
        return Kept(out[1], out[0])

    def second_half(values):
        return values.reshape(2, CAP, slots, width)[1]

    trip, trip_result = Trip(send_u, "core"), Trip(second_half(tie(result, back_sums)[0]), "t")
    qkv_sums, dqkv = slot([ring_d, trip, trip_result], do_attention_back)
    ring_u = scatter(own_u, trip.got)

    def attention_grads(now):
        _, sums, place = tie(now, qkv_sums, core1)
        small = small_grads(down_sums, back_sums, bias_sums, sums)
        return mixed_grad(rows_t, ctx_t, dqkv, da, small, place, parts)

    send_a, own_a = slot([ring_d, ring_u], attention_grads)
    def do_rows(now):
        _, base = tie(now, da)
        rows = (base.astype(F32) + dot(dqkv, whole_a[:, : 3 * width], NT)).astype(BF16)
        return rows, second_half(rows)

    trip = Trip(send_a, "core")
    rows_grad, rows = slot([ring_d, ring_u, trip], do_rows)
    trip_rows = Trip(rows, "t")
    to_home = jnp.concatenate([own_places, other_places], axis=0).T

    def home(values, back):
        both = jnp.concatenate([values.reshape(2, CAP, slots, width)[0], back], axis=0)
        return route(to_home, both).reshape(-1, width)

    def outputs(now):
        _, values, back = tie(now, result, trip_result.got)
        return home(values, back)

    ring_a = scatter(own_a, trip.got)
    output = slot([ring_d, ring_u, ring_a, trip_rows], outputs)
    for _ in range(ring.long - 4):
        slot([ring_d, ring_u, ring_a])
    owners_d = Owners(ring_d.total, side, groups)

    def input_grads(now):
        _, values, back = tie(now, rows_grad, trip_rows.got)
        return home(values, back)

    input_grad = slot([ring_u, ring_a, owners_d.trip], input_grads)
    owners_u = Owners(ring_u.total, side, groups)
    grads_d = slot([ring_a, owners_u.trip], lambda now: owners_d.by_model())
    grads_u = slot([ring_a], lambda now: owners_u.by_model())

    owners_a = Owners(ring_a.total, side, groups)
    slot([owners_a.trip])
    grads_a = owners_a.by_model()
    columns = jnp.swapaxes(grads_a[:, :, 4 * width : 4 * width + 16], 1, 2)
    return (
        output,
        input_grad,
        grads_a[:, :, :width],
        columns[:, 0],
        grads_a[:, :, width : 2 * width],
        grads_a[:, :, 2 * width : 3 * width],
        columns[:, 1],
        grads_a[:, :, 3 * width : 4 * width],
        columns[:, 2],
        columns[:, 3],
        columns[:, 4],
        grads_u,
        jnp.swapaxes(columns[:, 8:12], 1, 2).reshape(2, -1),
        grads_d,
        columns[:, 5],
        columns[:, 6],
        columns[:, 7],
    )


def solution(mesh):
    dp, fsdp = mesh.shape["dp"], mesh.shape["fsdp"]
    groups = dp // 4
    inner = Mesh(mesh.devices.reshape(groups, 2, 2, fsdp), ("r", "t", "core", "f"))
    every = ("r", "t", "core", "f")
    rows, vector, matrix = P(every, None), P(None, every), P(None, every, None)
    weights = (
        matrix,
        vector,
        matrix,
        matrix,
        vector,
        matrix,
        vector,
        vector,
        vector,
        matrix,
        vector,
        matrix,
        vector,
        vector,
        vector,
    )
    return jax.shard_map(
        functools.partial(body, Ring(fsdp), groups),
        mesh=inner,
        in_specs=(rows, rows, P(every), rows) + weights,
        out_specs=(rows, rows) + weights,
        check_vma=False,
    )
```
